512 devices in a mesh: field: 16 (over z_lo, core), spatial: 32 (over x, y, z_hi).
Axes of the slice: x: 4, y: 4, z: 16 (z_hi: 2, z_lo: 8; z = z_hi * 8 + z_lo), core: 2. Of those that a mesh axis runs over, the one named last changes fastest.
Arguments:
- field_in: bfloat16 [512, 384, 1024], P('field', 'spatial'), may hold values from -6 to 6
- spectral_weight: float32 [2, 512, 384], P(None, 'field'), may hold values from -5 to 5
- proj_in: bfloat16 [2048, 512], P(('field', 'spatial')), may hold values from -0.25 to 0.25
- bias_in: float32 [2048], replicated, may hold values from -4 to 4
- proj_out: bfloat16 [2048, 512], P(('field', 'spatial')), may hold values from -0.125 to 0.125
Outputs:
- field_out: bfloat16 [512, 384, 1024], P('field', 'spatial')
The draws below stay inside these ranges and needn't reach their ends.
All inputs are finite; a program needn't handle non-finite values.
Results may differ from the reference program's by a relative error of at most 0.0095.
Values may be sent and summed in bfloat16 or wider, within the bound.
No kernel may reach another device: no remote copies, remote signals or barrier semaphores. Data moves between devices by JAX's collectives and lax.ppermute only.
A program may use at most 128 MiB of HBM per device.

```python
import math
import jax
import jax.numpy as jnp
from jax import lax

C = 512
HID = 2048
NLAT = 384
NLON = 1024
LMAX = 384
MMAX = 384


def level_of(rng, extent, shards, low, high):
    def one(position, shards_of):
        draws = jax.random.uniform(jax.random.fold_in(jax.random.fold_in(rng, 6), position), (shards_of,), jnp.float32, low / len(shards), high / len(shards))
        return jnp.repeat(jnp.exp(draws), extent[position] // shards_of).reshape((-1,) + (1,) * (len(extent) - position - 1))

    level = one(*shards[0])
    for cut in shards[1:]:
        level = level * one(*cut)
    return level


def gaussian(key, dims, width, bound, pieces=(), held_as=jnp.bfloat16):
    result = jax.random.normal(key, dims, jnp.float32) * width
    if len(pieces) > 0:
        result = level_of(key, dims, pieces, -0.22, 0.18) * result
    return jnp.clip(result, min=-bound, max=bound).astype(held_as)


def setup_inputs(seed: int = 0) -> dict:
    seeds = jax.random.split(jax.random.key(seed), 6)
    field_in = gaussian(seeds[0], (C, NLAT, NLON), 1.0, 6.0, ((0, 16), (1, 32)))
    spectral_weight = gaussian(seeds[1], (2, C, LMAX), 1.0, 5.0, ((1, 16),), jnp.float32)
    proj_in = gaussian(seeds[2], (HID, C), C ** -0.5, 0.25, ((0, 512),))
    bias_in = gaussian(seeds[3], (HID,), 1.0, 4.0, (), jnp.float32)
    proj_out = gaussian(seeds[4], (HID, C), HID ** -0.5, 0.125, ((0, 512),))
    return {"field_in": field_in, "spectral_weight": spectral_weight, "proj_in": proj_in, "bias_in": bias_in, "proj_out": proj_out}


def legendre_table(orders, cosines, sines):
    order = orders[:, None]
    log_start = 0.5 * (jnp.log((2.0 * order + 1.0) / 2.0) + lax.lgamma(order + 0.5) - lax.lgamma(jnp.ones_like(order) * 0.5) - lax.lgamma(order + 1.0)) + order * jnp.log(sines)[None, :]
    unity = jnp.ones_like(log_start)
    nought = jnp.zeros_like(log_start)

    def advance(carry, degree):
        current, previous, scale = carry
        level = degree.astype(jnp.float32)
        below = level < order
        start = level == order
        fresh = jnp.logical_or(below, start)
        denom = jnp.maximum(level * level - order * order, 1.0)
        alpha = jnp.sqrt(jnp.maximum(4.0 * level * level - 1.0, 0.0) / denom)
        beta = jnp.sqrt(jnp.maximum((2.0 * level + 1.0) * ((level - 1.0) ** 2 - order * order), 0.0) / (jnp.maximum(2.0 * level - 3.0, 1.0) * denom))
        stepped = alpha * cosines[None, :] * current - beta * previous
        total = jnp.abs(stepped) + jnp.abs(current)
        new_current = jnp.where(fresh, unity, stepped / total)
        new_previous = jnp.where(fresh, nought, current / total)
        new_scale = jnp.where(fresh, log_start, scale + jnp.log(total))
        value = jnp.where(below, nought, new_current * jnp.exp(new_scale))
        return ((new_current, new_previous, new_scale), value)
    carry_end, values = lax.scan(advance, (unity, nought, log_start), jnp.arange(LMAX, dtype=jnp.int32))
    return jnp.transpose(values, (1, 0, 2))

def rounded(values):
    narrow = lax.optimization_barrier(values.astype(jnp.bfloat16))
    return narrow.astype(jnp.float32)

def reference(field_in, spectral_weight, proj_in, bias_in, proj_out):
    theta = math.pi * (jnp.arange(NLAT, dtype=jnp.float32) + 0.5) / NLAT
    quad = math.pi / NLAT * jnp.sin(theta)
    table = legendre_table(jnp.arange(MMAX, dtype=jnp.float32), jnp.cos(theta), jnp.sin(theta))
    block = math.gcd(C, 64)
    count = C // block

    def filter_block(pair):
        values, weights = pair
        spectrum = jnp.fft.rfft(values.astype(jnp.float32), axis=-1)[..., :MMAX] / NLON
        spec_re = rounded(jnp.real(spectrum)) * quad[None, :, None]
        spec_im = rounded(jnp.imag(spectrum)) * quad[None, :, None]
        coef_re = jnp.einsum('mlj,cjm->cml', table, spec_re, precision=lax.Precision.HIGHEST)
        coef_im = jnp.einsum('mlj,cjm->cml', table, spec_im, precision=lax.Precision.HIGHEST)
        real_w = weights[0][:, None, :]
        imag_w = weights[1][:, None, :]
        filt_re = real_w * coef_re - imag_w * coef_im
        filt_im = real_w * coef_im + imag_w * coef_re
        synth_re = rounded(jnp.einsum('mlj,cml->cjm', table, filt_re, precision=lax.Precision.HIGHEST))
        synth_im = rounded(jnp.einsum('mlj,cml->cjm', table, filt_im, precision=lax.Precision.HIGHEST))
        spectra = synth_re + 1j * synth_im
        padded = jnp.pad(spectra, ((0, 0), (0, 0), (0, NLON // 2 + 1 - MMAX)))
        smooth = jnp.fft.irfft(padded, n=NLON, axis=-1) * NLON
        return (values.astype(jnp.float32) + smooth).astype(jnp.bfloat16)
    blocks = field_in.reshape(count, block, NLAT, NLON)
    weight_blocks = jnp.transpose(spectral_weight.reshape(2, count, block, LMAX), (1, 0, 2, 3))
    mixed = lax.map(filter_block, (blocks, weight_blocks)).reshape(C, NLAT, NLON)

    def mlp_row(row):
        hidden_pre = jnp.dot(proj_in, row, preferred_element_type=jnp.float32) + bias_in[:, None]
        act = jax.nn.gelu(hidden_pre, approximate=True).astype(jnp.bfloat16)
        branch = lax.dot_general(proj_out, act, (((0,), (0,)), ((), ())), preferred_element_type=jnp.float32)
        return (row.astype(jnp.float32) + branch).astype(jnp.bfloat16)
    rows_out = lax.map(mlp_row, jnp.transpose(mixed, (1, 0, 2)))
    return jnp.transpose(rows_out, (1, 0, 2))
```

```python
import functools
import math

import jax
import jax.numpy as jnp
from jax import lax
from jax.experimental import pallas as pl
from jax.experimental.pallas import tpu as pltpu
from jax.sharding import PartitionSpec as P

F32 = jnp.float32
BF16 = jnp.bfloat16

CHANS = 32
BAND = 12
BANDS = 32
ORDERS = 12
NLAT = 384
NLON = 1024
LMAX = 384
HID = 2048
FULL = 512
MEMBERS = 16
ROWS = CHANS * BAND
PARTS = 2 * BANDS * ORDERS
POINTS = 768
LONS = 256
LATS = 3
BLOCK = LATS * CHANS
LANES = 128
PAD = 16
VMEM = 56 * 1024 * 1024


def params():
    return pltpu.CompilerParams(vmem_limit_bytes=VMEM)


def lanes(tile):
    return slice(tile * LANES, (tile + 1) * LANES)


def whole():
    return pl.BlockSpec(memory_space=pltpu.VMEM)


def forward_kernel(x_ref, y_ref, t_ref, xr_ref, rows_ref):
    unit = 2.0 * math.pi / NLON
    place = lax.broadcasted_iota(jnp.int32, (PAD, NLON), 1)
    row = lax.broadcasted_iota(jnp.int32, (PAD, NLON), 0)
    angle = unit * (((row >> 1) * place + (row & 1) * (NLON // 4)) & (NLON - 1)).astype(F32)
    turn = unit * ((place[:8] * 8) & (NLON - 1)).astype(F32)
    turn_cos = jnp.concatenate([jnp.cos(turn)] * 2, axis=0)
    turn_sin = jnp.concatenate([jnp.sin(turn)] * 2, axis=0)

    def turned(step, carry):
        cos, sin = carry
        t_ref[pl.ds(pl.multiple_of(step * PAD, PAD), PAD), :] = cos.astype(BF16)
        return (cos * turn_cos - sin * turn_sin, sin * turn_cos + cos * turn_sin)

    lax.fori_loop(0, PARTS // PAD, turned, (jnp.cos(angle), jnp.sin(angle)))

    for chan in range(CHANS):
        lats = x_ref[chan].astype(F32)
        for tile in range(NLON // LANES):
            rows_ref[tile, pl.ds(chan, BAND, stride=CHANS), :] = lats[:, lanes(tile)]
    for tile in range(NLON // LANES):
        xr_ref[:, lanes(tile)] = rows_ref[tile].astype(BF16)

    def transform(step, carry):
        at = pl.ds(pl.multiple_of(step * 128, 128), 128)
        y = lax.dot_general(
            t_ref[at, :], xr_ref[...], (((1,), (1,)), ((), ())), preferred_element_type=F32
        )
        y_ref[at, :] = (y * (1.0 / NLON)).astype(BF16)
        return carry

    lax.fori_loop(0, PARTS // 128, transform, 0)


def forward(x):
    return pl.pallas_call(
        forward_kernel,
        out_shape=(
            jax.ShapeDtypeStruct((PARTS, ROWS), BF16),
            jax.ShapeDtypeStruct((PARTS, NLON), BF16),
            jax.ShapeDtypeStruct((ROWS, NLON), BF16),
        ),
        in_specs=[whole()],
        out_specs=(whole(), whole(), whole()),
        scratch_shapes=[pltpu.VMEM((NLON // LANES, ROWS, LANES), F32)],
        compiler_params=params(),
        name="forward_fourier",
    )(x)


def theta_of(lane):
    lat = (lane & (BANDS - 1)) * BAND + (lane >> 5)
    return (lat.astype(F32) + 0.5) * (math.pi / NLAT)


def legendre_kernel(first_ref, table_ref, work_ref):
    first = first_ref[0]
    lane = lax.broadcasted_iota(jnp.int32, (PAD, NLAT), 1)
    theta = theta_of(lane)
    cosine = jnp.cos(theta)
    sine = jnp.sin(theta)
    order = first + lax.broadcasted_iota(jnp.int32, (PAD, NLAT), 0)
    order = jnp.minimum(order, LMAX - 1)
    level0 = order.astype(F32)
    step0 = (lane + 1).astype(F32)
    factor = jnp.where(lane < order, jnp.log2((2.0 * step0 - 1.0) / (2.0 * step0)), 0.0)
    log_start = 0.5 * (jnp.log2(level0 + 0.5) + jnp.sum(factor, axis=1, keepdims=True))
    log_start = log_start + level0 * jnp.log2(sine)
    whole_part = jnp.floor(log_start)
    start = jnp.exp2(log_start - whole_part)
    narrow = level0[:, :128]
    square = narrow * narrow

    def eight(group, carry):
        current, previous, power = carry
        half = jnp.exp2(0.5 * power)
        for inner in range(8):
            degree = group * 8 + inner
            level = degree.astype(F32)
            inverse = lax.rsqrt(jnp.maximum(level * level - square, 1.0))
            alpha = inverse * jnp.sqrt(
                jnp.maximum(jnp.full_like(square, 4.0) * (level * level) - 1.0, 0.0)
            )
            ratio = jnp.full_like(square, 1.0) * (2.0 * level + 1.0)
            ratio = ratio / jnp.maximum(jnp.full_like(square, 1.0) * (2.0 * level - 3.0), 1.0)
            below = level - 1.0
            beta = inverse * jnp.sqrt(jnp.maximum(ratio * (below * below - square), 0.0))
            alpha = jnp.concatenate([alpha] * 3, axis=1)
            beta = jnp.concatenate([beta] * 3, axis=1)
            stepped = (alpha * cosine) * current - beta * previous
            fresh = order == degree
            previous = jnp.where(fresh, 0.0, current)
            current = jnp.where(fresh, start, stepped)
            at = pl.ds(pl.multiple_of(degree * PAD, PAD), PAD)
            value = (current * half) * half
            for tile in range(3):
                work_ref[tile, at, :] = value[:, lanes(tile)]
        size = jnp.abs(current) + jnp.abs(previous)
        live = size > 0.0
        shift = jnp.where(live, jnp.floor(jnp.log2(jnp.where(live, size, 1.0))), 0.0)
        scale = jnp.exp2(-shift)
        return (current * scale, previous * scale, power + shift)

    nought = jnp.zeros((PAD, NLAT), F32)
    lax.fori_loop(0, LMAX // 8, eight, (nought, nought, whole_part))

    def store(item, carry):
        for tile in range(3):
            table_ref[item, :, lanes(tile)] = work_ref[
                tile, pl.ds(item, LMAX, stride=PAD), :
            ].astype(BF16)
        return carry

    lax.fori_loop(0, ORDERS, store, 0)


def legendre(first):
    return pl.pallas_call(
        legendre_kernel,
        out_shape=jax.ShapeDtypeStruct((ORDERS, LMAX, NLAT), BF16),
        in_specs=[pl.BlockSpec(memory_space=pltpu.SMEM)],
        out_specs=whole(),
        scratch_shapes=[pltpu.VMEM((3, LMAX * PAD, LANES), F32)],
        compiler_params=params(),
        cost_estimate=pl.CostEstimate(
            flops=100_000_000, bytes_accessed=20_000_000, transcendentals=1_000_000
        ),
        name="legendre_table",
    )(first)


def filter_kernel(r_ref, p_ref, w_ref, s_ref, rin, sout, data, gain0, gain1, quad):
    pair = pl.program_id(0)
    group = 4 * CHANS

    @pl.when(pair == 0)
    def _():
        for tile in range(3):
            rin[tile] = r_ref[:, lanes(tile)].astype(F32)
        lane = lax.broadcasted_iota(jnp.int32, (LMAX, group), 1)
        row = lax.broadcasted_iota(jnp.int32, (NLAT, group), 0)
        quad[...] = jnp.sin(theta_of(row)) * (math.pi / NLAT)
        gain0[...] = jnp.concatenate([w_ref[0]] * 4, axis=0).T
        turned = jnp.concatenate([w_ref[1]] * 4, axis=0).T
        gain1[...] = jnp.where((lane & CHANS) == 0, -turned, turned)

    lane32 = lax.broadcasted_iota(jnp.int32, (BANDS, group), 1)
    for tile in range(3):
        parts = [
            rin[tile, pl.ds(4 * pair + part, BANDS, stride=2 * ORDERS), :] for part in range(4)
        ]
        for lat in range(4):
            block = jnp.zeros((BANDS, group), F32)
            for part in range(4):
                shift = (part - lat) % 4 * CHANS
                moved = pltpu.roll(parts[part], shift, 1) if shift else parts[part]
                block = jnp.where((lane32 >> 5) == part, moved, block)
            rows = slice(group * tile + BANDS * lat, group * tile + BANDS * (lat + 1))
            data[rows, :] = (block * quad[rows, :]).astype(BF16)

    lane = lax.broadcasted_iota(jnp.int32, (LMAX, group), 1)
    upper = lane >= 2 * CHANS
    both = [
        jnp.dot(p_ref[item], data[...], preferred_element_type=F32) for item in range(2)
    ]
    coef = jnp.where(upper, both[1], both[0])
    other = jnp.where(
        (lane & CHANS) == 0, pltpu.roll(coef, group - CHANS, 1), pltpu.roll(coef, CHANS, 1)
    )
    filtered = (gain0[...] * coef + gain1[...] * other).astype(BF16)
    both = [
        lax.dot_general(
            p_ref[item], filtered, (((0,), (0,)), ((), ())), preferred_element_type=F32
        )
        for item in range(2)
    ]
    synth = jnp.where(upper, both[1], both[0])
    for tile in range(3):
        lats = [
            synth[group * tile + BANDS * lat : group * tile + BANDS * (lat + 1), :]
            for lat in range(4)
        ]
        for part in range(4):
            block = jnp.zeros((BANDS, group), F32)
            for lat in range(4):
                shift = (lat - part) % 4 * CHANS
                moved = pltpu.roll(lats[lat], shift, 1) if shift else lats[lat]
                block = jnp.where((lane32 >> 5) == lat, moved, block)
            sout[tile, pl.ds(4 * pair + part, BANDS, stride=2 * ORDERS), :] = block

    @pl.when(pair == ORDERS // 2 - 1)
    def _():
        for tile in range(3):
            s_ref[:, lanes(tile)] = sout[tile].astype(BF16)


def spectral_filter(received, table, weights):
    same2 = lambda pair: (0, 0)
    return pl.pallas_call(
        filter_kernel,
        grid=(ORDERS // 2,),
        out_shape=jax.ShapeDtypeStruct((PARTS, ROWS), BF16),
        in_specs=[
            pl.BlockSpec((PARTS, ROWS), same2),
            pl.BlockSpec((2, LMAX, NLAT), lambda pair: (pair, 0, 0)),
            pl.BlockSpec((2, CHANS, LMAX), lambda pair: (0, 0, 0)),
        ],
        out_specs=pl.BlockSpec((PARTS, ROWS), same2),
        scratch_shapes=[
            pltpu.VMEM((3, PARTS, LANES), F32),
            pltpu.VMEM((3, PARTS, LANES), F32),
            pltpu.VMEM((NLAT, 4 * CHANS), BF16),
            pltpu.VMEM((LMAX, 4 * CHANS), F32),
            pltpu.VMEM((LMAX, 4 * CHANS), F32),
            pltpu.VMEM((NLAT, 4 * CHANS), F32),
        ],
        compiler_params=params(),
        name="spectral_filter",
    )(received, table, weights)


def inverse_kernel(r_ref, t_ref, xr_ref, m_ref, spectra):
    row = lax.broadcasted_iota(jnp.int32, (PARTS, ROWS), 0)
    gained = jnp.where(row < 2, 1.0, 2.0) * r_ref[...].astype(F32)
    spectra[...] = gained.T.astype(BF16)

    def rows_of(step, carry):
        at = pl.ds(pl.multiple_of(step * BLOCK, BLOCK), BLOCK)
        smooth = jnp.dot(spectra[at, :], t_ref[...], preferred_element_type=F32)
        mixed = (xr_ref[at, :].astype(F32) + smooth).astype(BF16)
        for part in range(NLON // LONS):
            to = pl.ds(pl.multiple_of((step * 4 + part) * BLOCK, BLOCK), BLOCK)
            m_ref[to, :] = mixed[:, part * LONS : (part + 1) * LONS]
        return carry

    lax.fori_loop(0, BAND // LATS, rows_of, 0)


def inverse(returned, table, rows):
    return pl.pallas_call(
        inverse_kernel,
        out_shape=jax.ShapeDtypeStruct((MEMBERS * BLOCK, LONS), BF16),
        in_specs=[whole()] * 3,
        out_specs=whole(),
        scratch_shapes=[pltpu.VMEM((ROWS, PARTS), BF16)],
        compiler_params=params(),
        name="inverse_fourier",
    )(returned, table, rows)


def mlp_kernel(r_ref, win_ref, wout_ref, bias_ref, o_ref, points, total):
    step = pl.program_id(0)

    @pl.when(step == 0)
    def _():
        blocks = r_ref[...].reshape(MEMBERS, BLOCK, LONS)
        for lat in range(LATS):
            points[:, lat * LONS : (lat + 1) * LONS] = blocks[
                :, lat * CHANS : (lat + 1) * CHANS, :
            ].reshape(FULL, LONS)
        total[...] = points[...].astype(F32)

    rows = win_ref.shape[0] * win_ref.shape[2]
    w_in = win_ref[...].reshape(rows, FULL)
    w_out = wout_ref[...].reshape(rows, FULL)
    pre = jnp.dot(w_in, points[...], preferred_element_type=F32) + bias_ref[...]
    act = jax.nn.gelu(pre, approximate=True).astype(BF16)
    total[...] += lax.dot_general(
        w_out, act, (((0,), (0,)), ((), ())), preferred_element_type=F32
    )

    @pl.when(step == pl.num_programs(0) - 1)
    def _():
        out = total[...].astype(BF16)
        for member in range(MEMBERS):
            for lat in range(LATS):
                at = member * BLOCK + lat * CHANS
                o_ref[at : at + CHANS, :] = out[
                    member * CHANS : (member + 1) * CHANS, lat * LONS : (lat + 1) * LONS
                ]


def mlp(received, weights, bias):
    blocks, _, units, _ = weights.shape
    take = 256 // units
    same2 = lambda step: (0, 0)
    return pl.pallas_call(
        mlp_kernel,
        grid=(blocks // take,),
        out_shape=jax.ShapeDtypeStruct((MEMBERS * BLOCK, LONS), BF16),
        in_specs=[
            pl.BlockSpec((MEMBERS * BLOCK, LONS), same2),
            pl.BlockSpec((take, 1, units, FULL), lambda step: (step, 0, 0, 0)),
            pl.BlockSpec((take, 1, units, FULL), lambda step: (step, 1, 0, 0)),
            pl.BlockSpec((256, 1), lambda step: (step, 0)),
        ],
        out_specs=pl.BlockSpec((MEMBERS * BLOCK, LONS), same2),
        scratch_shapes=[pltpu.VMEM((FULL, POINTS), BF16), pltpu.VMEM((FULL, POINTS), F32)],
        compiler_params=params(),
        name="pointwise_mlp",
    )(received, weights, weights, bias)


def home_kernel(r_ref, o_ref, rows_ref):
    for member in range(MEMBERS):
        lat, part = member // 4, member % 4
        block = r_ref[member * BLOCK : (member + 1) * BLOCK, :].astype(F32)
        for tile in range(LONS // LANES):
            rows_ref[part * 2 + tile, lat * BLOCK : (lat + 1) * BLOCK, :] = block[:, lanes(tile)]
    for chan in range(CHANS):
        for tile in range(NLON // LANES):
            o_ref[chan, :, lanes(tile)] = rows_ref[
                tile, pl.ds(chan, BAND, stride=CHANS), :
            ].astype(BF16)


def home(received):
    return pl.pallas_call(
        home_kernel,
        out_shape=jax.ShapeDtypeStruct((CHANS, BAND, NLON), BF16),
        in_specs=[whole()],
        out_specs=whole(),
        scratch_shapes=[pltpu.VMEM((NLON // LANES, ROWS, LANES), F32)],
        compiler_params=params(),
        name="home_layout",
    )(received)


def gather_weights(proj_in, proj_out):
    units = proj_in.shape[0]
    both = jnp.concatenate([proj_in, proj_out], axis=0)
    column = [[xy * 32 + low * 2 + high * 16 + core for low in range(8) for core in range(2) for high in range(2)] for xy in range(16)]
    first = lax.all_gather(both, ("spatial", "field"), axis=0, axis_index_groups=column, tiled=True)
    split = first.reshape(32, 2, units, FULL).transpose(1, 0, 2, 3).reshape(64 * units, FULL)
    planes = [[xy * 2 + high for xy in range(16)] for high in range(2)]
    second = lax.all_gather(split, "spatial", axis=0, axis_index_groups=planes, tiled=True)
    return second.reshape(16, 2, 32 * units, FULL)


def shards(field_in, spectral_weight, proj_in, bias_in, proj_out):
    weights = gather_weights(proj_in, proj_out)
    bias = bias_in.reshape(16, 16, 8).transpose(1, 0, 2).reshape(HID, 1)
    spectrum, table, rows = forward(field_in)
    pencil = lax.all_to_all(
        spectrum.reshape(BANDS, 2 * ORDERS, ROWS), "spatial", split_axis=0, concat_axis=0, tiled=True
    )
    first = (lax.axis_index("spatial") * ORDERS).astype(jnp.int32).reshape(1)
    synth = spectral_filter(pencil.reshape(PARTS, ROWS), legendre(first), spectral_weight)
    returned = lax.all_to_all(
        synth.reshape(BANDS, 2 * ORDERS, ROWS), "spatial", split_axis=0, concat_axis=0, tiled=True
    )
    mixed = inverse(returned.reshape(PARTS, ROWS), table, rows)
    points = lax.all_to_all(
        mixed.reshape(MEMBERS, BLOCK, LONS), "field", split_axis=0, concat_axis=0, tiled=True
    )
    result = mlp(points.reshape(MEMBERS * BLOCK, LONS), weights, bias)
    homed = lax.all_to_all(
        result.reshape(MEMBERS, BLOCK, LONS), "field", split_axis=0, concat_axis=0, tiled=True
    )
    return home(homed.reshape(MEMBERS * BLOCK, LONS))


def solution(mesh):
    in_specs = (
        P("field", "spatial", None),
        P(None, "field", None),
        P(("field", "spatial"), None),
        P(),
        P(("field", "spatial"), None),
    )
    out_specs = P("field", "spatial", None)
    return jax.shard_map(shards, mesh=mesh, in_specs=in_specs, out_specs=out_specs, check_vma=False)
```

```python
import functools
import math

import jax
import jax.numpy as jnp
from jax import lax
from jax.experimental import pallas as pl
from jax.experimental.pallas import tpu as pltpu
from jax.sharding import PartitionSpec as P

F32 = jnp.float32
BF16 = jnp.bfloat16

CHANS = 32
BAND = 12
BANDS = 32
ORDERS = 12
NLAT = 384
NLON = 1024
LMAX = 384
HID = 2048
FULL = 512
MEMBERS = 16
ROWS = CHANS * BAND
PARTS = 2 * BANDS * ORDERS
POINTS = 768
LONS = 256
LATS = 3
BLOCK = LATS * CHANS
LANES = 128
PAD = 16
VMEM = 56 * 1024 * 1024


def params():
    return pltpu.CompilerParams(vmem_limit_bytes=VMEM)


def lanes(tile):
    return slice(tile * LANES, (tile + 1) * LANES)


def whole():
    return pl.BlockSpec(memory_space=pltpu.VMEM)


def forward_kernel(x_ref, y_ref, t_ref):
    unit = 2.0 * math.pi / NLON
    place = lax.broadcasted_iota(jnp.int32, (PAD, NLON), 1)
    row = lax.broadcasted_iota(jnp.int32, (PAD, NLON), 0)
    angle = unit * (((row >> 1) * place + (row & 1) * (NLON // 4)) & (NLON - 1)).astype(F32)
    turn = unit * ((place[:8] * 8) & (NLON - 1)).astype(F32)
    turn_cos = jnp.concatenate([jnp.cos(turn)] * 2, axis=0)
    turn_sin = jnp.concatenate([jnp.sin(turn)] * 2, axis=0)

    def turned(step, carry):
        cos, sin = carry
        t_ref[pl.ds(pl.multiple_of(step * PAD, PAD), PAD), :] = cos.astype(BF16)
        return (cos * turn_cos - sin * turn_sin, sin * turn_cos + cos * turn_sin)

    lax.fori_loop(0, PARTS // PAD, turned, (jnp.cos(angle), jnp.sin(angle)))

    def transform(step, carry):
        at = pl.ds(pl.multiple_of(step * 128, 128), 128)
        y = lax.dot_general(
            t_ref[at, :], x_ref[...], (((1,), (1,)), ((), ())), preferred_element_type=F32
        )
        y_ref[at, :] = (y * (1.0 / NLON)).astype(BF16)
        return carry

    lax.fori_loop(0, PARTS // 128, transform, 0)


def forward(x):
    return pl.pallas_call(
        forward_kernel,
        out_shape=(
            jax.ShapeDtypeStruct((PARTS, ROWS), BF16),
            jax.ShapeDtypeStruct((PARTS, NLON), BF16),
        ),
        in_specs=[whole()],
        out_specs=(whole(), whole()),
        compiler_params=params(),
        name="forward_fourier",
    )(x)


def theta_of(lane):
    lat = (lane & (BANDS - 1)) * BAND + (lane >> 5)
    return (lat.astype(F32) + 0.5) * (math.pi / NLAT)


def legendre_kernel(first_ref, table_ref, work_ref):
    first = first_ref[0]
    lane = lax.broadcasted_iota(jnp.int32, (PAD, NLAT), 1)
    theta = theta_of(lane)
    cosine = jnp.cos(theta)
    sine = jnp.sin(theta)
    order = first + lax.broadcasted_iota(jnp.int32, (PAD, NLAT), 0)
    order = jnp.minimum(order, LMAX - 1)
    level0 = order.astype(F32)
    step0 = (lane + 1).astype(F32)
    factor = jnp.where(lane < order, jnp.log2((2.0 * step0 - 1.0) / (2.0 * step0)), 0.0)
    log_start = 0.5 * (jnp.log2(level0 + 0.5) + jnp.sum(factor, axis=1, keepdims=True))
    log_start = log_start + level0 * jnp.log2(sine)
    whole_part = jnp.floor(log_start)
    start = jnp.exp2(log_start - whole_part)
    narrow = level0[:, :128]
    square = narrow * narrow

    def eight(group, carry):
        current, previous, power = carry
        half = jnp.exp2(0.5 * power)
        for inner in range(8):
            degree = group * 8 + inner
            level = degree.astype(F32)
            inverse = lax.rsqrt(jnp.maximum(level * level - square, 1.0))
            alpha = inverse * jnp.sqrt(
                jnp.maximum(jnp.full_like(square, 4.0) * (level * level) - 1.0, 0.0)
            )
            ratio = jnp.full_like(square, 1.0) * (2.0 * level + 1.0)
            ratio = ratio / jnp.maximum(jnp.full_like(square, 1.0) * (2.0 * level - 3.0), 1.0)
            below = level - 1.0
            beta = inverse * jnp.sqrt(jnp.maximum(ratio * (below * below - square), 0.0))
            alpha = jnp.concatenate([alpha] * 3, axis=1)
            beta = jnp.concatenate([beta] * 3, axis=1)
            stepped = (alpha * cosine) * current - beta * previous
            fresh = order == degree
            previous = jnp.where(fresh, 0.0, current)
            current = jnp.where(fresh, start, stepped)
            at = pl.ds(pl.multiple_of(degree * PAD, PAD), PAD)
            value = (current * half) * half
            for tile in range(3):
                work_ref[tile, at, :] = value[:, lanes(tile)]
        size = jnp.abs(current) + jnp.abs(previous)
        live = size > 0.0
        shift = jnp.where(live, jnp.floor(jnp.log2(jnp.where(live, size, 1.0))), 0.0)
        scale = jnp.exp2(-shift)
        return (current * scale, previous * scale, power + shift)

    nought = jnp.zeros((PAD, NLAT), F32)
    lax.fori_loop(0, LMAX // 8, eight, (nought, nought, whole_part))

    def store(item, carry):
        for tile in range(3):
            table_ref[item, :, lanes(tile)] = work_ref[
                tile, pl.ds(item, LMAX, stride=PAD), :
            ].astype(BF16)
        return carry

    lax.fori_loop(0, ORDERS, store, 0)


def legendre(first):
    return pl.pallas_call(
        legendre_kernel,
        out_shape=jax.ShapeDtypeStruct((ORDERS, LMAX, NLAT), BF16),
        in_specs=[pl.BlockSpec(memory_space=pltpu.SMEM)],
        out_specs=whole(),
        scratch_shapes=[pltpu.VMEM((3, LMAX * PAD, LANES), F32)],
        compiler_params=params(),
        cost_estimate=pl.CostEstimate(
            flops=100_000_000, bytes_accessed=20_000_000, transcendentals=1_000_000
        ),
        name="legendre_table",
    )(first)


def filter_kernel(r_ref, p_ref, w_ref, s_ref, rin, sout, quad):
    pair = pl.program_id(0)
    group = 4 * CHANS

    @pl.when(pair == 0)
    def _():
        for tile in range(3):
            rin[tile] = r_ref[:, lanes(tile)].astype(F32)
        lane = lax.broadcasted_iota(jnp.int32, (8, NLAT), 1)
        quad[...] = jnp.sin(theta_of(lane)) * (math.pi / NLAT)

    lane32 = lax.broadcasted_iota(jnp.int32, (BANDS, group), 1) >> 5
    tiles = []
    for tile in range(3):
        parts = [
            rin[tile, pl.ds(4 * pair + part, BANDS, stride=2 * ORDERS), :] for part in range(4)
        ]
        blocks = []
        for lat in range(4):
            block = jnp.zeros((BANDS, group), F32)
            for part in range(4):
                shift = (part - lat) % 4 * CHANS
                moved = pltpu.roll(parts[part], shift, 1) if shift else parts[part]
                block = jnp.where(lane32 == part, moved, block)
            blocks.append(block)
        tiles.append(jnp.concatenate(blocks, axis=0).T)
    data = jnp.concatenate(tiles, axis=1)
    data = (data * quad[:1, :]).astype(BF16)

    out = []
    for item in range(2):
        coef = lax.dot_general(
            data[2 * CHANS * item : 2 * CHANS * (item + 1), :],
            p_ref[item],
            (((1,), (1,)), ((), ())),
            preferred_element_type=F32,
        )
        real, imag = coef[:CHANS], coef[CHANS:]
        filtered = jnp.concatenate(
            [w_ref[0] * real - w_ref[1] * imag, w_ref[0] * imag + w_ref[1] * real], axis=0
        ).astype(BF16)
        out.append(jnp.dot(filtered, p_ref[item], preferred_element_type=F32))
    synth = jnp.concatenate(out, axis=0)
    for tile in range(3):
        turned = synth[:, lanes(tile)].T
        lats = [turned[BANDS * lat : BANDS * (lat + 1), :] for lat in range(4)]
        for part in range(4):
            block = jnp.zeros((BANDS, group), F32)
            for lat in range(4):
                shift = (lat - part) % 4 * CHANS
                moved = pltpu.roll(lats[lat], shift, 1) if shift else lats[lat]
                block = jnp.where(lane32 == lat, moved, block)
            sout[tile, pl.ds(4 * pair + part, BANDS, stride=2 * ORDERS), :] = block

    @pl.when(pair == ORDERS // 2 - 1)
    def _():
        for tile in range(3):
            s_ref[:, lanes(tile)] = sout[tile].astype(BF16)


def spectral_filter(received, table, weights):
    same2 = lambda pair: (0, 0)
    return pl.pallas_call(
        filter_kernel,
        grid=(ORDERS // 2,),
        out_shape=jax.ShapeDtypeStruct((PARTS, ROWS), BF16),
        in_specs=[
            pl.BlockSpec((PARTS, ROWS), same2),
            pl.BlockSpec((2, LMAX, NLAT), lambda pair: (pair, 0, 0)),
            pl.BlockSpec((2, CHANS, LMAX), lambda pair: (0, 0, 0)),
        ],
        out_specs=pl.BlockSpec((PARTS, ROWS), same2),
        scratch_shapes=[
            pltpu.VMEM((3, PARTS, LANES), F32),
            pltpu.VMEM((3, PARTS, LANES), F32),
            pltpu.VMEM((8, NLAT), F32),
        ],
        compiler_params=params(),
        name="spectral_filter",
    )(received, table, weights)


def inverse_kernel(r_ref, t_ref, xr_ref, m_ref, spectra):
    row = lax.broadcasted_iota(jnp.int32, (PARTS, ROWS), 0)
    gained = jnp.where(row < 2, 1.0, 2.0) * r_ref[...].astype(F32)
    spectra[...] = gained.T.astype(BF16)

    def rows_of(step, carry):
        at = pl.ds(pl.multiple_of(step * BLOCK, BLOCK), BLOCK)
        smooth = jnp.dot(spectra[at, :], t_ref[...], preferred_element_type=F32)
        mixed = (xr_ref[at, :].astype(F32) + smooth).astype(BF16)
        for part in range(NLON // LONS):
            to = pl.ds(pl.multiple_of((step * 4 + part) * BLOCK, BLOCK), BLOCK)
            m_ref[to, :] = mixed[:, part * LONS : (part + 1) * LONS]
        return carry

    lax.fori_loop(0, BAND // LATS, rows_of, 0)


def inverse(returned, table, rows):
    return pl.pallas_call(
        inverse_kernel,
        out_shape=jax.ShapeDtypeStruct((MEMBERS * BLOCK, LONS), BF16),
        in_specs=[whole()] * 3,
        out_specs=whole(),
        scratch_shapes=[pltpu.VMEM((ROWS, PARTS), BF16)],
        compiler_params=params(),
        name="inverse_fourier",
    )(returned, table, rows)


def mlp_kernel(r_ref, w_ref, bias_ref, o_ref, points, act, w_out):
    step = pl.program_id(0)
    rows = w_ref.shape[0] * LANES

    @pl.when(step == 0)
    def _():
        blocks = r_ref[...].reshape(MEMBERS, BLOCK, LONS)
        for lat in range(LATS):
            points[:, lat * LONS : (lat + 1) * LONS] = blocks[
                :, lat * CHANS : (lat + 1) * CHANS, :
            ].reshape(FULL, LONS)

    w_in = []
    for part in range(w_ref.shape[0]):
        block = w_ref[part]
        w_in.append(
            jnp.concatenate([block[LANES * tile : LANES * (tile + 1)] for tile in range(4)], axis=1)
        )
        at = pl.ds(pl.multiple_of((step * w_ref.shape[0] + part) * LANES, LANES), LANES)
        w_out[:, at] = block[FULL:]
    w_in = jnp.concatenate(w_in, axis=0)
    at = pl.ds(pl.multiple_of(step * rows, rows), rows)
    for lat in range(LATS):
        cols = slice(lat * LONS, (lat + 1) * LONS)
        pre = jnp.dot(w_in, points[:, cols], preferred_element_type=F32) + bias_ref[...]
        act[at, cols] = jax.nn.gelu(pre, approximate=True).astype(BF16)

    @pl.when(step == pl.num_programs(0) - 1)
    def _():
        for lat in range(LATS):
            cols = slice(lat * LONS, (lat + 1) * LONS)
            branch = jnp.dot(w_out[...], act[:, cols], preferred_element_type=F32)
            out = (points[:, cols].astype(F32) + branch).astype(BF16)
            for member in range(MEMBERS):
                to = member * BLOCK + lat * CHANS
                o_ref[to : to + CHANS, :] = out[member * CHANS : (member + 1) * CHANS, :]


def mlp(received, weights, bias):
    blocks = weights.shape[0]
    take = 2
    same2 = lambda step: (0, 0)
    return pl.pallas_call(
        mlp_kernel,
        grid=(blocks // take,),
        out_shape=jax.ShapeDtypeStruct((MEMBERS * BLOCK, LONS), BF16),
        in_specs=[
            pl.BlockSpec((MEMBERS * BLOCK, LONS), same2),
            pl.BlockSpec((take, 2 * FULL, LANES), lambda step: (step, 0, 0)),
            pl.BlockSpec((take * LANES, 1), lambda step: (step, 0)),
        ],
        out_specs=pl.BlockSpec((MEMBERS * BLOCK, LONS), same2),
        scratch_shapes=[
            pltpu.VMEM((FULL, POINTS), BF16),
            pltpu.VMEM((HID, POINTS), BF16),
            pltpu.VMEM((FULL, HID), BF16),
        ],
        compiler_params=params(),
        name="pointwise_mlp",
    )(received, weights, bias)


def home_kernel(r_ref, o_ref):
    for member in range(MEMBERS):
        lat, part = member // 4, member % 4
        o_ref[lat * BLOCK : (lat + 1) * BLOCK, part * LONS : (part + 1) * LONS] = r_ref[
            member * BLOCK : (member + 1) * BLOCK, :
        ]


def home(received):
    return pl.pallas_call(
        home_kernel,
        out_shape=jax.ShapeDtypeStruct((ROWS, NLON), BF16),
        in_specs=[whole()],
        out_specs=whole(),
        compiler_params=params(),
        name="home_layout",
    )(received)


def gather_first(proj_in, proj_out):
    column = [[xy * 32 + place for place in range(32)] for xy in range(16)]
    both = jnp.concatenate([proj_in, proj_out], axis=0)
    return lax.all_gather(both, ("spatial", "field"), axis=0, axis_index_groups=column, tiled=True)


def gather_second(column):
    split = column.reshape(32, 2, HID // FULL, FULL)
    w_in = split[:, 0].reshape(LANES, 4, LANES).transpose(1, 0, 2).reshape(FULL, LANES)
    w_out = split[:, 1].reshape(LANES, FULL).T
    block = jnp.concatenate([w_in, w_out], axis=0)
    planes = [[xy * 2 + high for xy in range(16)] for high in range(2)]
    whole_weights = lax.all_gather(block, "spatial", axis=0, axis_index_groups=planes, tiled=True)
    return whole_weights.reshape(16, 2 * FULL, LANES)


def shards(field_in, spectral_weight, proj_in, bias_in, proj_out):
    column = gather_first(proj_in, proj_out)
    bias = bias_in.reshape(16, 16, 2, 4).transpose(1, 2, 0, 3).reshape(HID, 1)
    rows = field_in.transpose(1, 0, 2).reshape(ROWS, NLON)
    spectrum, table = forward(rows)
    pencil = lax.all_to_all(
        spectrum.reshape(BANDS, 2 * ORDERS, ROWS), "spatial", split_axis=0, concat_axis=0, tiled=True
    )
    first = (lax.axis_index("spatial") * ORDERS).astype(jnp.int32).reshape(1)
    polar = legendre(first)
    polar, column = lax.optimization_barrier((polar, column))
    weights = gather_second(column)
    synth = spectral_filter(pencil.reshape(PARTS, ROWS), polar, spectral_weight)
    returned = lax.all_to_all(
        synth.reshape(BANDS, 2 * ORDERS, ROWS), "spatial", split_axis=0, concat_axis=0, tiled=True
    )
    mixed = inverse(returned.reshape(PARTS, ROWS), table, rows)
    points = lax.all_to_all(
        mixed.reshape(MEMBERS, BLOCK, LONS), "field", split_axis=0, concat_axis=0, tiled=True
    )
    result = mlp(points.reshape(MEMBERS * BLOCK, LONS), weights, bias)
    homed = lax.all_to_all(
        result.reshape(MEMBERS, BLOCK, LONS), "field", split_axis=0, concat_axis=0, tiled=True
    )
    return home(homed.reshape(MEMBERS * BLOCK, LONS)).reshape(BAND, CHANS, NLON).transpose(1, 0, 2)


def solution(mesh):
    in_specs = (
        P("field", "spatial", None),
        P(None, "field", None),
        P(("field", "spatial"), None),
        P(),
        P(("field", "spatial"), None),
    )
    out_specs = P("field", "spatial", None)
    return jax.shard_map(shards, mesh=mesh, in_specs=in_specs, out_specs=out_specs, check_vma=False)
```

```python
import functools
import math

import jax
import jax.numpy as jnp
from jax import lax
from jax.experimental import pallas as pl
from jax.experimental.pallas import tpu as pltpu
from jax.sharding import PartitionSpec as P

F32 = jnp.float32
BF16 = jnp.bfloat16

CHANS = 32
BAND = 12
BANDS = 32
ORDERS = 12
NLAT = 384
NLON = 1024
LMAX = 384
HID = 2048
FULL = 512
MEMBERS = 16
ROWS = CHANS * BAND
PARTS = 2 * BANDS * ORDERS
POINTS = 768
LONS = 256
LATS = 3
BLOCK = LATS * CHANS
LANES = 128
PAD = 16
VMEM = 56 * 1024 * 1024


def params():
    return pltpu.CompilerParams(vmem_limit_bytes=VMEM)


def lanes(tile):
    return slice(tile * LANES, (tile + 1) * LANES)


def whole():
    return pl.BlockSpec(memory_space=pltpu.VMEM)


def forward_kernel(x_ref, y_ref, t_ref):
    unit = 2.0 * math.pi / NLON
    place = lax.broadcasted_iota(jnp.int32, (PAD, NLON), 1)
    row = lax.broadcasted_iota(jnp.int32, (PAD, NLON), 0)
    angle = unit * (((row >> 1) * place + (row & 1) * (NLON // 4)) & (NLON - 1)).astype(F32)
    turn = unit * ((place[:8] * 8) & (NLON - 1)).astype(F32)
    turn_cos = jnp.concatenate([jnp.cos(turn)] * 2, axis=0)
    turn_sin = jnp.concatenate([jnp.sin(turn)] * 2, axis=0)

    def turned(step, carry):
        cos, sin = carry
        t_ref[pl.ds(pl.multiple_of(step * PAD, PAD), PAD), :] = cos.astype(BF16)
        return (cos * turn_cos - sin * turn_sin, sin * turn_cos + cos * turn_sin)

    lax.fori_loop(0, PARTS // PAD, turned, (jnp.cos(angle), jnp.sin(angle)))

    def transform(step, carry):
        at = pl.ds(pl.multiple_of(step * 128, 128), 128)
        y = lax.dot_general(
            t_ref[at, :], x_ref[...], (((1,), (1,)), ((), ())), preferred_element_type=F32
        )
        y_ref[at, :] = (y * (1.0 / NLON)).astype(BF16)
        return carry

    lax.fori_loop(0, PARTS // 128, transform, 0)


def forward(x):
    return pl.pallas_call(
        forward_kernel,
        out_shape=(
            jax.ShapeDtypeStruct((PARTS, ROWS), BF16),
            jax.ShapeDtypeStruct((PARTS, NLON), BF16),
        ),
        in_specs=[whole()],
        out_specs=(whole(), whole()),
        compiler_params=params(),
        name="forward_fourier",
    )(x)


def theta_of(lane):
    lat = (lane & (BANDS - 1)) * BAND + (lane >> 5)
    return (lat.astype(F32) + 0.5) * (math.pi / NLAT)


def legendre_kernel(first_ref, bias_ref, table_ref, laid_ref, work_ref):
    laid_ref[...] = bias_ref[...]
    first = first_ref[0]
    lane = lax.broadcasted_iota(jnp.int32, (PAD, NLAT), 1)
    theta = theta_of(lane)
    cosine = jnp.cos(theta)
    sine = jnp.sin(theta)
    order = first + lax.broadcasted_iota(jnp.int32, (PAD, NLAT), 0)
    order = jnp.minimum(order, LMAX - 1)
    level0 = order.astype(F32)
    step0 = (lane + 1).astype(F32)
    factor = jnp.where(lane < order, jnp.log2((2.0 * step0 - 1.0) / (2.0 * step0)), 0.0)
    log_start = 0.5 * (jnp.log2(level0 + 0.5) + jnp.sum(factor, axis=1, keepdims=True))
    log_start = log_start + level0 * jnp.log2(sine)
    whole_part = jnp.floor(log_start)
    start = jnp.exp2(log_start - whole_part)
    narrow = level0[:, :128]
    square = narrow * narrow

    def eight(group, carry):
        current, previous, power = carry
        half = jnp.exp2(0.5 * power)
        for inner in range(8):
            degree = group * 8 + inner
            level = degree.astype(F32)
            inverse = lax.rsqrt(jnp.maximum(level * level - square, 1.0))
            alpha = inverse * jnp.sqrt(
                jnp.maximum(jnp.full_like(square, 4.0) * (level * level) - 1.0, 0.0)
            )
            ratio = jnp.full_like(square, 1.0) * (2.0 * level + 1.0)
            ratio = ratio / jnp.maximum(jnp.full_like(square, 1.0) * (2.0 * level - 3.0), 1.0)
            below = level - 1.0
            beta = inverse * jnp.sqrt(jnp.maximum(ratio * (below * below - square), 0.0))
            alpha = jnp.concatenate([alpha] * 3, axis=1)
            beta = jnp.concatenate([beta] * 3, axis=1)
            stepped = (alpha * cosine) * current - beta * previous
            fresh = order == degree
            previous = jnp.where(fresh, 0.0, current)
            current = jnp.where(fresh, start, stepped)
            at = pl.ds(pl.multiple_of(degree * PAD, PAD), PAD)
            value = (current * half) * half
            for tile in range(3):
                work_ref[tile, at, :] = value[:, lanes(tile)]
        size = jnp.abs(current) + jnp.abs(previous)
        live = size > 0.0
        shift = jnp.where(live, jnp.floor(jnp.log2(jnp.where(live, size, 1.0))), 0.0)
        scale = jnp.exp2(-shift)
        return (current * scale, previous * scale, power + shift)

    nought = jnp.zeros((PAD, NLAT), F32)
    lax.fori_loop(0, LMAX // 8, eight, (nought, nought, whole_part))

    def store(item, carry):
        for tile in range(3):
            table_ref[item, :, lanes(tile)] = work_ref[
                tile, pl.ds(item, LMAX, stride=PAD), :
            ].astype(BF16)
        return carry

    lax.fori_loop(0, ORDERS, store, 0)


def legendre(first, bias):
    return pl.pallas_call(
        legendre_kernel,
        out_shape=(
            jax.ShapeDtypeStruct((ORDERS, LMAX, NLAT), BF16),
            jax.ShapeDtypeStruct(bias.shape, F32),
        ),
        in_specs=[pl.BlockSpec(memory_space=pltpu.SMEM), whole()],
        out_specs=(whole(), whole()),
        scratch_shapes=[pltpu.VMEM((3, LMAX * PAD, LANES), F32)],
        compiler_params=params(),
        cost_estimate=pl.CostEstimate(
            flops=100_000_000, bytes_accessed=20_000_000, transcendentals=1_000_000
        ),
        name="legendre_table",
    )(first, bias)


def filter_kernel(r_ref, p_ref, w_ref, s_ref, rin, sout, quad):
    pair = pl.program_id(0)
    group = 4 * CHANS

    @pl.when(pair == 0)
    def _():
        for tile in range(3):
            rin[tile] = r_ref[:, lanes(tile)].astype(F32)
        lane = lax.broadcasted_iota(jnp.int32, (8, NLAT), 1)
        quad[...] = jnp.sin(theta_of(lane)) * (math.pi / NLAT)

    lane32 = lax.broadcasted_iota(jnp.int32, (BANDS, group), 1) >> 5
    tiles = []
    for tile in range(3):
        parts = [
            rin[tile, pl.ds(4 * pair + part, BANDS, stride=2 * ORDERS), :] for part in range(4)
        ]
        blocks = []
        for lat in range(4):
            block = jnp.zeros((BANDS, group), F32)
            for part in range(4):
                shift = (part - lat) % 4 * CHANS
                moved = pltpu.roll(parts[part], shift, 1) if shift else parts[part]
                block = jnp.where(lane32 == part, moved, block)
            blocks.append(block)
        tiles.append(jnp.concatenate(blocks, axis=0).T)
    data = jnp.concatenate(tiles, axis=1)
    data = (data * quad[:1, :]).astype(BF16)

    out = []
    for item in range(2):
        coef = lax.dot_general(
            data[2 * CHANS * item : 2 * CHANS * (item + 1), :],
            p_ref[item],
            (((1,), (1,)), ((), ())),
            preferred_element_type=F32,
        )
        real, imag = coef[:CHANS], coef[CHANS:]
        filtered = jnp.concatenate(
            [w_ref[0] * real - w_ref[1] * imag, w_ref[0] * imag + w_ref[1] * real], axis=0
        ).astype(BF16)
        out.append(jnp.dot(filtered, p_ref[item], preferred_element_type=F32))
    synth = jnp.concatenate(out, axis=0)
    for tile in range(3):
        turned = synth[:, lanes(tile)].T
        lats = [turned[BANDS * lat : BANDS * (lat + 1), :] for lat in range(4)]
        for part in range(4):
            block = jnp.zeros((BANDS, group), F32)
            for lat in range(4):
                shift = (lat - part) % 4 * CHANS
                moved = pltpu.roll(lats[lat], shift, 1) if shift else lats[lat]
                block = jnp.where(lane32 == lat, moved, block)
            sout[tile, pl.ds(4 * pair + part, BANDS, stride=2 * ORDERS), :] = block

    @pl.when(pair == ORDERS // 2 - 1)
    def _():
        for tile in range(3):
            s_ref[:, lanes(tile)] = sout[tile].astype(BF16)


def spectral_filter(received, table, weights):
    same2 = lambda pair: (0, 0)
    return pl.pallas_call(
        filter_kernel,
        grid=(ORDERS // 2,),
        out_shape=jax.ShapeDtypeStruct((PARTS, ROWS), BF16),
        in_specs=[
            pl.BlockSpec((PARTS, ROWS), same2),
            pl.BlockSpec((2, LMAX, NLAT), lambda pair: (pair, 0, 0)),
            pl.BlockSpec((2, CHANS, LMAX), lambda pair: (0, 0, 0)),
        ],
        out_specs=pl.BlockSpec((PARTS, ROWS), same2),
        scratch_shapes=[
            pltpu.VMEM((3, PARTS, LANES), F32),
            pltpu.VMEM((3, PARTS, LANES), F32),
            pltpu.VMEM((8, NLAT), F32),
        ],
        compiler_params=params(),
        name="spectral_filter",
    )(received, table, weights)


def inverse_kernel(r_ref, t_ref, xr_ref, m_ref, spectra):
    row = lax.broadcasted_iota(jnp.int32, (PARTS, ROWS), 0)
    gained = jnp.where(row < 2, 1.0, 2.0) * r_ref[...].astype(F32)
    spectra[...] = gained.T.astype(BF16)

    def rows_of(step, carry):
        at = pl.ds(pl.multiple_of(step * BLOCK, BLOCK), BLOCK)
        smooth = jnp.dot(spectra[at, :], t_ref[...], preferred_element_type=F32)
        mixed = (xr_ref[at, :].astype(F32) + smooth).astype(BF16)
        for part in range(NLON // LONS):
            to = pl.ds(pl.multiple_of((step * 4 + part) * BLOCK, BLOCK), BLOCK)
            m_ref[to, :] = mixed[:, part * LONS : (part + 1) * LONS]
        return carry

    lax.fori_loop(0, BAND // LATS, rows_of, 0)


def inverse(returned, table, rows):
    return pl.pallas_call(
        inverse_kernel,
        out_shape=jax.ShapeDtypeStruct((MEMBERS * BLOCK, LONS), BF16),
        in_specs=[whole()] * 3,
        out_specs=whole(),
        scratch_shapes=[pltpu.VMEM((ROWS, PARTS), BF16)],
        compiler_params=params(),
        name="inverse_fourier",
    )(returned, table, rows)


def mlp_kernel(r_ref, w_ref, bias_ref, o_ref, points, act, w_out):
    step = pl.program_id(0)
    rows = w_ref.shape[0] * LANES

    @pl.when(step == 0)
    def _():
        blocks = r_ref[...].reshape(MEMBERS, BLOCK, LONS)
        for lat in range(LATS):
            points[:, lat * LONS : (lat + 1) * LONS] = blocks[
                :, lat * CHANS : (lat + 1) * CHANS, :
            ].reshape(FULL, LONS)

    w_in, bias = [], []
    for part in range(w_ref.shape[0]):
        block = w_ref[part]
        column = bias_ref[pl.ds(step * w_ref.shape[0] + part, 1), :]
        bias.append(jnp.broadcast_to(column, (LANES, LANES)).T)
        w_in.append(
            jnp.concatenate([block[LANES * tile : LANES * (tile + 1)] for tile in range(4)], axis=1)
        )
        at = pl.ds(pl.multiple_of((step * w_ref.shape[0] + part) * LANES, LANES), LANES)
        w_out[:, at] = block[FULL:]
    w_in = jnp.concatenate(w_in, axis=0)
    bias = jnp.concatenate([jnp.concatenate(bias, axis=0)] * (LONS // LANES), axis=1)
    at = pl.ds(pl.multiple_of(step * rows, rows), rows)
    for lat in range(LATS):
        cols = slice(lat * LONS, (lat + 1) * LONS)
        pre = jnp.dot(w_in, points[:, cols], preferred_element_type=F32) + bias
        act[at, cols] = jax.nn.gelu(pre, approximate=True).astype(BF16)

    @pl.when(step == pl.num_programs(0) - 1)
    def _():
        for lat in range(LATS):
            cols = slice(lat * LONS, (lat + 1) * LONS)
            branch = jnp.dot(w_out[...], act[:, cols], preferred_element_type=F32)
            out = (points[:, cols].astype(F32) + branch).astype(BF16)
            for member in range(MEMBERS):
                to = member * BLOCK + lat * CHANS
                o_ref[to : to + CHANS, :] = out[member * CHANS : (member + 1) * CHANS, :]


def mlp(received, weights, bias):
    blocks = weights.shape[0]
    take = 2
    same2 = lambda step: (0, 0)
    return pl.pallas_call(
        mlp_kernel,
        grid=(blocks // take,),
        out_shape=jax.ShapeDtypeStruct((MEMBERS * BLOCK, LONS), BF16),
        in_specs=[
            pl.BlockSpec((MEMBERS * BLOCK, LONS), same2),
            pl.BlockSpec((take, 2 * FULL, LANES), lambda step: (step, 0, 0)),
            pl.BlockSpec((blocks, LANES), same2),
        ],
        out_specs=pl.BlockSpec((MEMBERS * BLOCK, LONS), same2),
        scratch_shapes=[
            pltpu.VMEM((FULL, POINTS), BF16),
            pltpu.VMEM((HID, POINTS), BF16),
            pltpu.VMEM((FULL, HID), BF16),
        ],
        compiler_params=params(),
        name="pointwise_mlp",
    )(received, weights, bias)


def home_kernel(r_ref, o_ref):
    for member in range(MEMBERS):
        lat, part = member // 4, member % 4
        o_ref[lat * BLOCK : (lat + 1) * BLOCK, part * LONS : (part + 1) * LONS] = r_ref[
            member * BLOCK : (member + 1) * BLOCK, :
        ]


def home(received):
    return pl.pallas_call(
        home_kernel,
        out_shape=jax.ShapeDtypeStruct((ROWS, NLON), BF16),
        in_specs=[whole()],
        out_specs=whole(),
        compiler_params=params(),
        name="home_layout",
    )(received)


SENT = 32


def gather_first(proj_in, proj_out):
    column = [[xy * 32 + place for place in range(32)] for xy in range(16)]
    both = jnp.concatenate([proj_in, proj_out], axis=0)
    both = jnp.pad(both, ((0, SENT - both.shape[0]), (0, 0)))
    return lax.all_gather(both, ("spatial", "field"), axis=0, axis_index_groups=column, tiled=True)


def gather_second(column):
    split = column.reshape(32, SENT // 4, HID // FULL, FULL)
    w_in = split[:, 0].reshape(LANES, 4, LANES).transpose(1, 0, 2).reshape(FULL, LANES)
    w_out = split[:, 1].reshape(LANES, FULL).T
    block = jnp.concatenate([w_in, w_out], axis=0)
    planes = [[xy * 2 + high for xy in range(16)] for high in range(2)]
    whole_weights = lax.all_gather(block, "spatial", axis=0, axis_index_groups=planes, tiled=True)
    return whole_weights.reshape(16, 2 * FULL, LANES)


def shards(field_in, spectral_weight, proj_in, bias_in, proj_out):
    column = gather_first(proj_in, proj_out)
    bias = bias_in.reshape(16, 16, 2, 4).transpose(1, 2, 0, 3).reshape(16, LANES)
    rows = field_in.transpose(1, 0, 2).reshape(ROWS, NLON)
    spectrum, table = forward(rows)
    pencil = lax.all_to_all(
        spectrum.reshape(BANDS, 2 * ORDERS, ROWS), "spatial", split_axis=0, concat_axis=0, tiled=True
    )
    first = (lax.axis_index("spatial") * ORDERS).astype(jnp.int32).reshape(1)
    polar, bias = legendre(first, bias)
    synth = spectral_filter(pencil.reshape(PARTS, ROWS), polar, spectral_weight)
    synth, column = lax.optimization_barrier((synth, column))
    weights = gather_second(column)
    returned = lax.all_to_all(
        synth.reshape(BANDS, 2 * ORDERS, ROWS), "spatial", split_axis=0, concat_axis=0, tiled=True
    )
    mixed = inverse(returned.reshape(PARTS, ROWS), table, rows)
    points = lax.all_to_all(
        mixed.reshape(MEMBERS, BLOCK, LONS), "field", split_axis=0, concat_axis=0, tiled=True
    )
    result = mlp(points.reshape(MEMBERS * BLOCK, LONS), weights, bias)
    homed = lax.all_to_all(
        result.reshape(MEMBERS, BLOCK, LONS), "field", split_axis=0, concat_axis=0, tiled=True
    )
    return home(homed.reshape(MEMBERS * BLOCK, LONS)).reshape(BAND, CHANS, NLON).transpose(1, 0, 2)


def solution(mesh):
    in_specs = (
        P("field", "spatial", None),
        P(None, "field", None),
        P(("field", "spatial"), None),
        P(),
        P(("field", "spatial"), None),
    )
    out_specs = P("field", "spatial", None)
    return jax.shard_map(shards, mesh=mesh, in_specs=in_specs, out_specs=out_specs, check_vma=False)
```

```python
import functools
import math

import jax
import jax.numpy as jnp
from jax import lax
from jax.experimental import pallas as pl
from jax.experimental.pallas import tpu as pltpu
from jax.sharding import PartitionSpec as P

F32 = jnp.float32
BF16 = jnp.bfloat16

CHANS = 32
BAND = 12
BANDS = 32
ORDERS = 12
NLAT = 384
NLON = 1024
LMAX = 384
HID = 2048
FULL = 512
MEMBERS = 16
ROWS = CHANS * BAND
PARTS = 2 * BANDS * ORDERS
POINTS = 768
LONS = 256
LATS = 3
BLOCK = LATS * CHANS
LANES = 128
PAD = 16
VMEM = 56 * 1024 * 1024


def params():
    return pltpu.CompilerParams(vmem_limit_bytes=VMEM)


def lanes(tile):
    return slice(tile * LANES, (tile + 1) * LANES)


def whole():
    return pl.BlockSpec(memory_space=pltpu.VMEM)


def forward_kernel(x_ref, y_ref, t_ref):
    unit = 2.0 * math.pi / NLON
    place = lax.broadcasted_iota(jnp.int32, (PAD, NLON), 1)
    row = lax.broadcasted_iota(jnp.int32, (PAD, NLON), 0)
    angle = unit * (((row >> 1) * place + (row & 1) * (NLON // 4)) & (NLON - 1)).astype(F32)
    turn = unit * ((place[:8] * 8) & (NLON - 1)).astype(F32)
    turn_cos = jnp.concatenate([jnp.cos(turn)] * 2, axis=0)
    turn_sin = jnp.concatenate([jnp.sin(turn)] * 2, axis=0)

    def turned(step, carry):
        cos, sin = carry
        t_ref[pl.ds(pl.multiple_of(step * PAD, PAD), PAD), :] = cos.astype(BF16)
        return (cos * turn_cos - sin * turn_sin, sin * turn_cos + cos * turn_sin)

    lax.fori_loop(0, PARTS // PAD, turned, (jnp.cos(angle), jnp.sin(angle)))

    def transform(step, carry):
        at = pl.ds(pl.multiple_of(step * 128, 128), 128)
        y = lax.dot_general(
            t_ref[at, :], x_ref[...], (((1,), (1,)), ((), ())), preferred_element_type=F32
        )
        y_ref[at, :] = (y * (1.0 / NLON)).astype(BF16)
        return carry

    lax.fori_loop(0, PARTS // 128, transform, 0)


def forward(x):
    return pl.pallas_call(
        forward_kernel,
        out_shape=(
            jax.ShapeDtypeStruct((PARTS, ROWS), BF16),
            jax.ShapeDtypeStruct((PARTS, NLON), BF16),
        ),
        in_specs=[whole()],
        out_specs=(whole(), whole()),
        compiler_params=params(),
        name="forward_fourier",
    )(x)


def theta_of(lane):
    lat = (lane & (BANDS - 1)) * BAND + (lane >> 5)
    return (lat.astype(F32) + 0.5) * (math.pi / NLAT)


def legendre_kernel(first_ref, bias_ref, table_ref, laid_ref, work_ref):
    laid_ref[...] = bias_ref[...]
    first = first_ref[0]
    lane = lax.broadcasted_iota(jnp.int32, (PAD, NLAT), 1)
    theta = theta_of(lane)
    cosine = jnp.cos(theta)
    sine = jnp.sin(theta)
    order = first + lax.broadcasted_iota(jnp.int32, (PAD, NLAT), 0)
    order = jnp.minimum(order, LMAX - 1)
    level0 = order.astype(F32)
    step0 = (lane + 1).astype(F32)
    factor = jnp.where(lane < order, jnp.log2((2.0 * step0 - 1.0) / (2.0 * step0)), 0.0)
    log_start = 0.5 * (jnp.log2(level0 + 0.5) + jnp.sum(factor, axis=1, keepdims=True))
    log_start = log_start + level0 * jnp.log2(sine)
    whole_part = jnp.floor(log_start)
    start = jnp.exp2(log_start - whole_part)
    narrow = level0[:, :128]
    square = narrow * narrow

    def eight(group, carry):
        current, previous, power = carry
        half = jnp.exp2(0.5 * power)
        for inner in range(8):
            degree = group * 8 + inner
            level = degree.astype(F32)
            inverse = lax.rsqrt(jnp.maximum(level * level - square, 1.0))
            alpha = inverse * jnp.sqrt(
                jnp.maximum(jnp.full_like(square, 4.0) * (level * level) - 1.0, 0.0)
            )
            ratio = jnp.full_like(square, 1.0) * (2.0 * level + 1.0)
            ratio = ratio / jnp.maximum(jnp.full_like(square, 1.0) * (2.0 * level - 3.0), 1.0)
            below = level - 1.0
            beta = inverse * jnp.sqrt(jnp.maximum(ratio * (below * below - square), 0.0))
            alpha = jnp.concatenate([alpha] * 3, axis=1)
            beta = jnp.concatenate([beta] * 3, axis=1)
            stepped = (alpha * cosine) * current - beta * previous
            fresh = order == degree
            previous = jnp.where(fresh, 0.0, current)
            current = jnp.where(fresh, start, stepped)
            at = pl.ds(pl.multiple_of(degree * PAD, PAD), PAD)
            value = (current * half) * half
            for tile in range(3):
                work_ref[tile, at, :] = value[:, lanes(tile)]
        size = jnp.abs(current) + jnp.abs(previous)
        live = size > 0.0
        shift = jnp.where(live, jnp.floor(jnp.log2(jnp.where(live, size, 1.0))), 0.0)
        scale = jnp.exp2(-shift)
        return (current * scale, previous * scale, power + shift)

    nought = jnp.zeros((PAD, NLAT), F32)
    lax.fori_loop(0, LMAX // 8, eight, (nought, nought, whole_part))

    def store(item, carry):
        for tile in range(3):
            table_ref[item, :, lanes(tile)] = work_ref[
                tile, pl.ds(item, LMAX, stride=PAD), :
            ].astype(BF16)
        return carry

    lax.fori_loop(0, ORDERS, store, 0)


def legendre(first, bias):
    return pl.pallas_call(
        legendre_kernel,
        out_shape=(
            jax.ShapeDtypeStruct((ORDERS, LMAX, NLAT), BF16),
            jax.ShapeDtypeStruct(bias.shape, F32),
        ),
        in_specs=[pl.BlockSpec(memory_space=pltpu.SMEM), whole()],
        out_specs=(whole(), whole()),
        scratch_shapes=[pltpu.VMEM((3, LMAX * PAD, LANES), F32)],
        compiler_params=params(),
        cost_estimate=pl.CostEstimate(
            flops=100_000_000, bytes_accessed=20_000_000, transcendentals=1_000_000
        ),
        name="legendre_table",
    )(first, bias)


def filter_kernel(r_ref, p_ref, w_ref, s_ref, rin, sout, quad):
    pair = pl.program_id(0)
    group = 4 * CHANS

    @pl.when(pair == 0)
    def _():
        for tile in range(3):
            rin[tile] = r_ref[:, lanes(tile)].astype(F32)
        lane = lax.broadcasted_iota(jnp.int32, (8, NLAT), 1)
        quad[...] = jnp.sin(theta_of(lane)) * (math.pi / NLAT)

    lane32 = lax.broadcasted_iota(jnp.int32, (BANDS, group), 1) >> 5
    tiles = []
    for tile in range(3):
        parts = [
            rin[tile, pl.ds(4 * pair + part, BANDS, stride=2 * ORDERS), :] for part in range(4)
        ]
        blocks = []
        for lat in range(4):
            block = jnp.zeros((BANDS, group), F32)
            for part in range(4):
                shift = (part - lat) % 4 * CHANS
                moved = pltpu.roll(parts[part], shift, 1) if shift else parts[part]
                block = jnp.where(lane32 == part, moved, block)
            blocks.append(block)
        tiles.append(jnp.concatenate(blocks, axis=0).T)
    data = jnp.concatenate(tiles, axis=1)
    data = (data * quad[:1, :]).astype(BF16)

    out = []
    for item in range(2):
        coef = lax.dot_general(
            data[2 * CHANS * item : 2 * CHANS * (item + 1), :],
            p_ref[item],
            (((1,), (1,)), ((), ())),
            preferred_element_type=F32,
        )
        real, imag = coef[:CHANS], coef[CHANS:]
        filtered = jnp.concatenate(
            [w_ref[0] * real - w_ref[1] * imag, w_ref[0] * imag + w_ref[1] * real], axis=0
        ).astype(BF16)
        out.append(jnp.dot(filtered, p_ref[item], preferred_element_type=F32))
    synth = jnp.concatenate(out, axis=0)
    for tile in range(3):
        turned = synth[:, lanes(tile)].T
        lats = [turned[BANDS * lat : BANDS * (lat + 1), :] for lat in range(4)]
        for part in range(4):
            block = jnp.zeros((BANDS, group), F32)
            for lat in range(4):
                shift = (lat - part) % 4 * CHANS
                moved = pltpu.roll(lats[lat], shift, 1) if shift else lats[lat]
                block = jnp.where(lane32 == lat, moved, block)
            sout[tile, pl.ds(4 * pair + part, BANDS, stride=2 * ORDERS), :] = block

    @pl.when(pair == ORDERS // 2 - 1)
    def _():
        for tile in range(3):
            s_ref[:, lanes(tile)] = sout[tile].astype(BF16)


def spectral_filter(received, table, weights):
    same2 = lambda pair: (0, 0)
    return pl.pallas_call(
        filter_kernel,
        grid=(ORDERS // 2,),
        out_shape=jax.ShapeDtypeStruct((PARTS, ROWS), BF16),
        in_specs=[
            pl.BlockSpec((PARTS, ROWS), same2),
            pl.BlockSpec((2, LMAX, NLAT), lambda pair: (pair, 0, 0)),
            pl.BlockSpec((2, CHANS, LMAX), lambda pair: (0, 0, 0)),
        ],
        out_specs=pl.BlockSpec((PARTS, ROWS), same2),
        scratch_shapes=[
            pltpu.VMEM((3, PARTS, LANES), F32),
            pltpu.VMEM((3, PARTS, LANES), F32),
            pltpu.VMEM((8, NLAT), F32),
        ],
        compiler_params=params(),
        name="spectral_filter",
    )(received, table, weights)


def inverse_kernel(r_ref, t_ref, xr_ref, m_ref, spectra):
    row = lax.broadcasted_iota(jnp.int32, (PARTS, ROWS), 0)
    gained = jnp.where(row < 2, 1.0, 2.0) * r_ref[...].astype(F32)
    spectra[...] = gained.T.astype(BF16)

    def rows_of(step, carry):
        at = pl.ds(pl.multiple_of(step * BLOCK, BLOCK), BLOCK)
        smooth = jnp.dot(spectra[at, :], t_ref[...], preferred_element_type=F32)
        mixed = (xr_ref[at, :].astype(F32) + smooth).astype(BF16)
        for part in range(NLON // LONS):
            to = pl.ds(pl.multiple_of((step * 4 + part) * BLOCK, BLOCK), BLOCK)
            m_ref[to, :] = mixed[:, part * LONS : (part + 1) * LONS]
        return carry

    lax.fori_loop(0, BAND // LATS, rows_of, 0)


def inverse(returned, table, rows):
    return pl.pallas_call(
        inverse_kernel,
        out_shape=jax.ShapeDtypeStruct((MEMBERS * BLOCK, LONS), BF16),
        in_specs=[whole()] * 3,
        out_specs=whole(),
        scratch_shapes=[pltpu.VMEM((ROWS, PARTS), BF16)],
        compiler_params=params(),
        name="inverse_fourier",
    )(returned, table, rows)


def mlp_kernel(r_ref, w_ref, bias_ref, o_ref, points, act, w_out):
    step = pl.program_id(0)
    rows = w_ref.shape[0] * LANES

    @pl.when(step == 0)
    def _():
        blocks = r_ref[...].reshape(MEMBERS, BLOCK, LONS)
        for lat in range(LATS):
            points[:, lat * LONS : (lat + 1) * LONS] = blocks[
                :, lat * CHANS : (lat + 1) * CHANS, :
            ].reshape(FULL, LONS)

    w_in, bias = [], []
    for part in range(w_ref.shape[0]):
        block = w_ref[part]
        column = bias_ref[pl.ds(step * w_ref.shape[0] + part, 1), :]
        bias.append(jnp.broadcast_to(column, (LANES, LANES)).T)
        w_in.append(
            jnp.concatenate([block[LANES * tile : LANES * (tile + 1)] for tile in range(4)], axis=1)
        )
        at = pl.ds(pl.multiple_of((step * w_ref.shape[0] + part) * LANES, LANES), LANES)
        w_out[:, at] = block[FULL:]
    w_in = jnp.concatenate(w_in, axis=0)
    bias = jnp.concatenate([jnp.concatenate(bias, axis=0)] * (LONS // LANES), axis=1)
    at = pl.ds(pl.multiple_of(step * rows, rows), rows)
    for lat in range(LATS):
        cols = slice(lat * LONS, (lat + 1) * LONS)
        pre = jnp.dot(w_in, points[:, cols], preferred_element_type=F32) + bias
        act[at, cols] = jax.nn.gelu(pre, approximate=True).astype(BF16)

    @pl.when(step == pl.num_programs(0) - 1)
    def _():
        for lat in range(LATS):
            cols = slice(lat * LONS, (lat + 1) * LONS)
            branch = jnp.dot(w_out[...], act[:, cols], preferred_element_type=F32)
            out = (points[:, cols].astype(F32) + branch).astype(BF16)
            for member in range(MEMBERS):
                to = member * BLOCK + lat * CHANS
                o_ref[to : to + CHANS, :] = out[member * CHANS : (member + 1) * CHANS, :]


def mlp(received, weights, bias):
    blocks = weights.shape[0]
    take = 2
    same2 = lambda step: (0, 0)
    return pl.pallas_call(
        mlp_kernel,
        grid=(blocks // take,),
        out_shape=jax.ShapeDtypeStruct((MEMBERS * BLOCK, LONS), BF16),
        in_specs=[
            pl.BlockSpec((MEMBERS * BLOCK, LONS), same2),
            pl.BlockSpec((take, 2 * FULL, LANES), lambda step: (step, 0, 0)),
            pl.BlockSpec((blocks, LANES), same2),
        ],
        out_specs=pl.BlockSpec((MEMBERS * BLOCK, LONS), same2),
        scratch_shapes=[
            pltpu.VMEM((FULL, POINTS), BF16),
            pltpu.VMEM((HID, POINTS), BF16),
            pltpu.VMEM((FULL, HID), BF16),
        ],
        compiler_params=params(),
        name="pointwise_mlp",
    )(received, weights, bias)


def home_kernel(r_ref, o_ref):
    for member in range(MEMBERS):
        lat, part = member // 4, member % 4
        o_ref[lat * BLOCK : (lat + 1) * BLOCK, part * LONS : (part + 1) * LONS] = r_ref[
            member * BLOCK : (member + 1) * BLOCK, :
        ]


def home(received):
    return pl.pallas_call(
        home_kernel,
        out_shape=jax.ShapeDtypeStruct((ROWS, NLON), BF16),
        in_specs=[whole()],
        out_specs=whole(),
        compiler_params=params(),
        name="home_layout",
    )(received)


def place_in_column():
    return (lax.axis_index("spatial") & 1) * 8 + (lax.axis_index("field") >> 1)


def partner(bit):
    pairs = []
    for field in range(16):
        for spatial in range(32):
            other = ((spatial & 1) * 8 + (field >> 1)) ^ bit
            pairs.append(
                (
                    field * 32 + spatial,
                    ((other & 7) * 2 + (field & 1)) * 32 + (spatial & 30) + (other >> 3),
                )
            )
    return pairs


def gather_first(proj_in, proj_out):
    held = jnp.concatenate([proj_in, proj_out], axis=0)
    place = place_in_column()
    for bit in (1, 2, 4, 8):
        other = lax.ppermute(held, ("field", "spatial"), partner(bit))
        upper = (place & bit) != 0
        held = jnp.concatenate(
            [jnp.where(upper, other, held), jnp.where(upper, held, other)], axis=0
        )
    cores = [[2 * chip, 2 * chip + 1] for chip in range(8)]
    return lax.all_gather(held, "field", axis=0, axis_index_groups=cores, tiled=True)


def gather_second(column):
    split = column.reshape(32, 2, HID // FULL, FULL)
    w_in = split[:, 0].reshape(LANES, 4, LANES).transpose(1, 0, 2).reshape(FULL, LANES)
    w_out = split[:, 1].reshape(LANES, FULL).T
    block = jnp.concatenate([w_in, w_out], axis=0)
    planes = [[xy * 2 + high for xy in range(16)] for high in range(2)]
    whole_weights = lax.all_gather(block, "spatial", axis=0, axis_index_groups=planes, tiled=True)
    return whole_weights.reshape(16, 2 * FULL, LANES)


def shards(field_in, spectral_weight, proj_in, bias_in, proj_out):
    column = gather_first(proj_in, proj_out)
    bias = bias_in.reshape(8, 2, 16, 2, 4).transpose(2, 1, 3, 0, 4).reshape(16, LANES)
    rows = field_in.transpose(1, 0, 2).reshape(ROWS, NLON)
    spectrum, table = forward(rows)
    pencil = lax.all_to_all(
        spectrum.reshape(BANDS, 2 * ORDERS, ROWS), "spatial", split_axis=0, concat_axis=0, tiled=True
    )
    first = (lax.axis_index("spatial") * ORDERS).astype(jnp.int32).reshape(1)
    polar, bias = legendre(first, bias)
    synth = spectral_filter(pencil.reshape(PARTS, ROWS), polar, spectral_weight)
    synth, column = lax.optimization_barrier((synth, column))
    weights = gather_second(column)
    returned = lax.all_to_all(
        synth.reshape(BANDS, 2 * ORDERS, ROWS), "spatial", split_axis=0, concat_axis=0, tiled=True
    )
    mixed = inverse(returned.reshape(PARTS, ROWS), table, rows)
    points = lax.all_to_all(
        mixed.reshape(MEMBERS, BLOCK, LONS), "field", split_axis=0, concat_axis=0, tiled=True
    )
    result = mlp(points.reshape(MEMBERS * BLOCK, LONS), weights, bias)
    homed = lax.all_to_all(
        result.reshape(MEMBERS, BLOCK, LONS), "field", split_axis=0, concat_axis=0, tiled=True
    )
    return home(homed.reshape(MEMBERS * BLOCK, LONS)).reshape(BAND, CHANS, NLON).transpose(1, 0, 2)


def solution(mesh):
    in_specs = (
        P("field", "spatial", None),
        P(None, "field", None),
        P(("field", "spatial"), None),
        P(),
        P(("field", "spatial"), None),
    )
    out_specs = P("field", "spatial", None)
    return jax.shard_map(shards, mesh=mesh, in_specs=in_specs, out_specs=out_specs, check_vma=False)
```

```python
import functools
import math

import jax
import jax.numpy as jnp
from jax import lax
from jax.experimental import pallas as pl
from jax.experimental.pallas import tpu as pltpu
from jax.sharding import PartitionSpec as P

F32 = jnp.float32
BF16 = jnp.bfloat16

CHANS = 32
BAND = 12
BANDS = 32
ORDERS = 12
NLAT = 384
NLON = 1024
LMAX = 384
HID = 2048
FULL = 512
MEMBERS = 16
ROWS = CHANS * BAND
PARTS = 2 * BANDS * ORDERS
POINTS = 768
LONS = 256
LATS = 3
BLOCK = LATS * CHANS
LANES = 128
PAD = 16
VMEM = 56 * 1024 * 1024


def params():
    return pltpu.CompilerParams(vmem_limit_bytes=VMEM)


def lanes(tile):
    return slice(tile * LANES, (tile + 1) * LANES)


def whole():
    return pl.BlockSpec(memory_space=pltpu.VMEM)


def forward_kernel(x_ref, y_ref, t_ref):
    unit = 2.0 * math.pi / NLON
    place = lax.broadcasted_iota(jnp.int32, (PAD, NLON), 1)
    row = lax.broadcasted_iota(jnp.int32, (PAD, NLON), 0)
    angle = unit * (((row >> 1) * place + (row & 1) * (NLON // 4)) & (NLON - 1)).astype(F32)
    turn = unit * ((place[:8] * 8) & (NLON - 1)).astype(F32)
    turn_cos = jnp.concatenate([jnp.cos(turn)] * 2, axis=0)
    turn_sin = jnp.concatenate([jnp.sin(turn)] * 2, axis=0)

    def turned(step, carry):
        cos, sin = carry
        t_ref[pl.ds(pl.multiple_of(step * PAD, PAD), PAD), :] = cos.astype(BF16)
        return (cos * turn_cos - sin * turn_sin, sin * turn_cos + cos * turn_sin)

    lax.fori_loop(0, PARTS // PAD, turned, (jnp.cos(angle), jnp.sin(angle)))

    def transform(step, carry):
        at = pl.ds(pl.multiple_of(step * 128, 128), 128)
        y = lax.dot_general(
            t_ref[at, :], x_ref[...], (((1,), (1,)), ((), ())), preferred_element_type=F32
        )
        y_ref[at, :] = (y * (1.0 / NLON)).astype(BF16)
        return carry

    lax.fori_loop(0, PARTS // 128, transform, 0)


def forward(x):
    return pl.pallas_call(
        forward_kernel,
        out_shape=(
            jax.ShapeDtypeStruct((PARTS, ROWS), BF16),
            jax.ShapeDtypeStruct((PARTS, NLON), BF16),
        ),
        in_specs=[whole()],
        out_specs=(whole(), whole()),
        compiler_params=params(),
        name="forward_fourier",
    )(x)


def theta_of(lane):
    lat = (lane & (BANDS - 1)) * BAND + (lane >> 5)
    return (lat.astype(F32) + 0.5) * (math.pi / NLAT)


def legendre_kernel(first_ref, bias_ref, table_ref, laid_ref, work_ref):
    laid_ref[...] = bias_ref[...]
    first = first_ref[0]
    lane = lax.broadcasted_iota(jnp.int32, (PAD, NLAT), 1)
    theta = theta_of(lane)
    cosine = jnp.cos(theta)
    sine = jnp.sin(theta)
    order = first + lax.broadcasted_iota(jnp.int32, (PAD, NLAT), 0)
    order = jnp.minimum(order, LMAX - 1)
    level0 = order.astype(F32)
    step0 = (lane + 1).astype(F32)
    factor = jnp.where(lane < order, jnp.log2((2.0 * step0 - 1.0) / (2.0 * step0)), 0.0)
    log_start = 0.5 * (jnp.log2(level0 + 0.5) + jnp.sum(factor, axis=1, keepdims=True))
    log_start = log_start + level0 * jnp.log2(sine)
    whole_part = jnp.floor(log_start)
    start = jnp.exp2(log_start - whole_part)
    narrow = level0[:, :128]
    square = narrow * narrow

    def eight(group, carry):
        current, previous, power = carry
        half = jnp.exp2(0.5 * power)
        for inner in range(8):
            degree = group * 8 + inner
            level = degree.astype(F32)
            inverse = lax.rsqrt(jnp.maximum(level * level - square, 1.0))
            alpha = inverse * jnp.sqrt(
                jnp.maximum(jnp.full_like(square, 4.0) * (level * level) - 1.0, 0.0)
            )
            ratio = jnp.full_like(square, 1.0) * (2.0 * level + 1.0)
            ratio = ratio / jnp.maximum(jnp.full_like(square, 1.0) * (2.0 * level - 3.0), 1.0)
            below = level - 1.0
            beta = inverse * jnp.sqrt(jnp.maximum(ratio * (below * below - square), 0.0))
            alpha = jnp.concatenate([alpha] * 3, axis=1)
            beta = jnp.concatenate([beta] * 3, axis=1)
            stepped = (alpha * cosine) * current - beta * previous
            fresh = order == degree
            previous = jnp.where(fresh, 0.0, current)
            current = jnp.where(fresh, start, stepped)
            at = pl.ds(pl.multiple_of(degree * PAD, PAD), PAD)
            value = (current * half) * half
            for tile in range(3):
                work_ref[tile, at, :] = value[:, lanes(tile)]
        size = jnp.abs(current) + jnp.abs(previous)
        live = size > 0.0
        shift = jnp.where(live, jnp.floor(jnp.log2(jnp.where(live, size, 1.0))), 0.0)
        scale = jnp.exp2(-shift)
        return (current * scale, previous * scale, power + shift)

    nought = jnp.zeros((PAD, NLAT), F32)
    lax.fori_loop(0, LMAX // 8, eight, (nought, nought, whole_part))

    def store(item, carry):
        for tile in range(3):
            table_ref[item, :, lanes(tile)] = work_ref[
                tile, pl.ds(item, LMAX, stride=PAD), :
            ].astype(BF16)
        return carry

    lax.fori_loop(0, ORDERS, store, 0)


def legendre(first, bias):
    return pl.pallas_call(
        legendre_kernel,
        out_shape=(
            jax.ShapeDtypeStruct((ORDERS, LMAX, NLAT), BF16),
            jax.ShapeDtypeStruct(bias.shape, F32),
        ),
        in_specs=[pl.BlockSpec(memory_space=pltpu.SMEM), whole()],
        out_specs=(whole(), whole()),
        scratch_shapes=[pltpu.VMEM((3, LMAX * PAD, LANES), F32)],
        compiler_params=params(),
        cost_estimate=pl.CostEstimate(
            flops=100_000_000, bytes_accessed=20_000_000, transcendentals=1_000_000
        ),
        name="legendre_table",
    )(first, bias)


def filter_kernel(r_ref, p_ref, w_ref, s_ref, rin, sout, quad):
    pair = pl.program_id(0)
    group = 4 * CHANS

    @pl.when(pair == 0)
    def _():
        for tile in range(3):
            rin[tile] = r_ref[:, lanes(tile)].astype(F32)
        lane = lax.broadcasted_iota(jnp.int32, (8, NLAT), 1)
        quad[...] = jnp.sin(theta_of(lane)) * (math.pi / NLAT)

    lane32 = lax.broadcasted_iota(jnp.int32, (BANDS, group), 1) >> 5
    tiles = []
    for tile in range(3):
        parts = [
            rin[tile, pl.ds(4 * pair + part, BANDS, stride=2 * ORDERS), :] for part in range(4)
        ]
        blocks = []
        for lat in range(4):
            block = jnp.zeros((BANDS, group), F32)
            for part in range(4):
                shift = (part - lat) % 4 * CHANS
                moved = pltpu.roll(parts[part], shift, 1) if shift else parts[part]
                block = jnp.where(lane32 == part, moved, block)
            blocks.append(block)
        tiles.append(jnp.concatenate(blocks, axis=0).T)
    data = jnp.concatenate(tiles, axis=1)
    data = (data * quad[:1, :]).astype(BF16)

    out = []
    for item in range(2):
        coef = lax.dot_general(
            data[2 * CHANS * item : 2 * CHANS * (item + 1), :],
            p_ref[item],
            (((1,), (1,)), ((), ())),
            preferred_element_type=F32,
        )
        real, imag = coef[:CHANS], coef[CHANS:]
        filtered = jnp.concatenate(
            [w_ref[0] * real - w_ref[1] * imag, w_ref[0] * imag + w_ref[1] * real], axis=0
        ).astype(BF16)
        out.append(jnp.dot(filtered, p_ref[item], preferred_element_type=F32))
    synth = jnp.concatenate(out, axis=0)
    for tile in range(3):
        turned = synth[:, lanes(tile)].T
        lats = [turned[BANDS * lat : BANDS * (lat + 1), :] for lat in range(4)]
        for part in range(4):
            block = jnp.zeros((BANDS, group), F32)
            for lat in range(4):
                shift = (lat - part) % 4 * CHANS
                moved = pltpu.roll(lats[lat], shift, 1) if shift else lats[lat]
                block = jnp.where(lane32 == lat, moved, block)
            sout[tile, pl.ds(4 * pair + part, BANDS, stride=2 * ORDERS), :] = block

    @pl.when(pair == ORDERS // 2 - 1)
    def _():
        for tile in range(3):
            s_ref[:, lanes(tile)] = sout[tile].astype(BF16)


def spectral_filter(received, table, weights):
    same2 = lambda pair: (0, 0)
    return pl.pallas_call(
        filter_kernel,
        grid=(ORDERS // 2,),
        out_shape=jax.ShapeDtypeStruct((PARTS, ROWS), BF16),
        in_specs=[
            pl.BlockSpec((PARTS, ROWS), same2),
            pl.BlockSpec((2, LMAX, NLAT), lambda pair: (pair, 0, 0)),
            pl.BlockSpec((2, CHANS, LMAX), lambda pair: (0, 0, 0)),
        ],
        out_specs=pl.BlockSpec((PARTS, ROWS), same2),
        scratch_shapes=[
            pltpu.VMEM((3, PARTS, LANES), F32),
            pltpu.VMEM((3, PARTS, LANES), F32),
            pltpu.VMEM((8, NLAT), F32),
        ],
        compiler_params=params(),
        name="spectral_filter",
    )(received, table, weights)


def inverse_kernel(r_ref, t_ref, xr_ref, m_ref, spectra):
    row = lax.broadcasted_iota(jnp.int32, (PARTS, ROWS), 0)
    gained = jnp.where(row < 2, 1.0, 2.0) * r_ref[...].astype(F32)
    spectra[...] = gained.T.astype(BF16)

    def rows_of(step, carry):
        at = pl.ds(pl.multiple_of(step * BLOCK, BLOCK), BLOCK)
        smooth = jnp.dot(spectra[at, :], t_ref[...], preferred_element_type=F32)
        mixed = (xr_ref[at, :].astype(F32) + smooth).astype(BF16)
        for part in range(NLON // LONS):
            to = pl.ds(pl.multiple_of((step * 4 + part) * BLOCK, BLOCK), BLOCK)
            m_ref[to, :] = mixed[:, part * LONS : (part + 1) * LONS]
        return carry

    lax.fori_loop(0, BAND // LATS, rows_of, 0)


def inverse(returned, table, rows):
    return pl.pallas_call(
        inverse_kernel,
        out_shape=jax.ShapeDtypeStruct((MEMBERS * BLOCK, LONS), BF16),
        in_specs=[whole()] * 3,
        out_specs=whole(),
        scratch_shapes=[pltpu.VMEM((ROWS, PARTS), BF16)],
        compiler_params=params(),
        name="inverse_fourier",
    )(returned, table, rows)


def mlp_kernel(r_ref, w_ref, bias_ref, o_ref, points, act, w_out):
    step = pl.program_id(0)
    rows = w_ref.shape[0] * LANES

    @pl.when(step == 0)
    def _():
        blocks = r_ref[...].reshape(MEMBERS, BLOCK, LONS)
        for lat in range(LATS):
            points[:, lat * LONS : (lat + 1) * LONS] = blocks[
                :, lat * CHANS : (lat + 1) * CHANS, :
            ].reshape(FULL, LONS)

    w_in, bias = [], []
    for part in range(w_ref.shape[0]):
        block = w_ref[part]
        column = bias_ref[pl.ds(step * w_ref.shape[0] + part, 1), :]
        bias.append(jnp.broadcast_to(column, (LANES, LANES)).T)
        w_in.append(
            jnp.concatenate([block[LANES * tile : LANES * (tile + 1)] for tile in range(4)], axis=1)
        )
        at = pl.ds(pl.multiple_of((step * w_ref.shape[0] + part) * LANES, LANES), LANES)
        w_out[:, at] = block[FULL:]
    w_in = jnp.concatenate(w_in, axis=0)
    bias = jnp.concatenate([jnp.concatenate(bias, axis=0)] * (LONS // LANES), axis=1)
    at = pl.ds(pl.multiple_of(step * rows, rows), rows)
    for lat in range(LATS):
        cols = slice(lat * LONS, (lat + 1) * LONS)
        pre = jnp.dot(w_in, points[:, cols], preferred_element_type=F32) + bias
        act[at, cols] = jax.nn.gelu(pre, approximate=True).astype(BF16)

    @pl.when(step == pl.num_programs(0) - 1)
    def _():
        for lat in range(LATS):
            cols = slice(lat * LONS, (lat + 1) * LONS)
            branch = jnp.dot(w_out[...], act[:, cols], preferred_element_type=F32)
            out = (points[:, cols].astype(F32) + branch).astype(BF16)
            for member in range(MEMBERS):
                to = member * BLOCK + lat * CHANS
                o_ref[to : to + CHANS, :] = out[member * CHANS : (member + 1) * CHANS, :]


def mlp(received, weights, bias):
    blocks = weights.shape[0]
    take = 2
    same2 = lambda step: (0, 0)
    return pl.pallas_call(
        mlp_kernel,
        grid=(blocks // take,),
        out_shape=jax.ShapeDtypeStruct((MEMBERS * BLOCK, LONS), BF16),
        in_specs=[
            pl.BlockSpec((MEMBERS * BLOCK, LONS), same2),
            pl.BlockSpec((take, 2 * FULL, LANES), lambda step: (step, 0, 0)),
            pl.BlockSpec((blocks, LANES), same2),
        ],
        out_specs=pl.BlockSpec((MEMBERS * BLOCK, LONS), same2),
        scratch_shapes=[
            pltpu.VMEM((FULL, POINTS), BF16),
            pltpu.VMEM((HID, POINTS), BF16),
            pltpu.VMEM((FULL, HID), BF16),
        ],
        compiler_params=params(),
        name="pointwise_mlp",
    )(received, weights, bias)


def home_kernel(r_ref, o_ref):
    for member in range(MEMBERS):
        lat, part = member // 4, member % 4
        o_ref[lat * BLOCK : (lat + 1) * BLOCK, part * LONS : (part + 1) * LONS] = r_ref[
            member * BLOCK : (member + 1) * BLOCK, :
        ]


def home(received):
    return pl.pallas_call(
        home_kernel,
        out_shape=jax.ShapeDtypeStruct((ROWS, NLON), BF16),
        in_specs=[whole()],
        out_specs=whole(),
        compiler_params=params(),
        name="home_layout",
    )(received)


SENT = 32


def gather_first(proj_in, proj_out):
    column = [[xy * 32 + place for place in range(32)] for xy in range(16)]
    both = jnp.concatenate([proj_in, proj_out], axis=0)
    both = jnp.pad(both, ((0, SENT - both.shape[0]), (0, 0)))
    return lax.all_gather(both, ("spatial", "field"), axis=0, axis_index_groups=column, tiled=True)


def gather_second(column):
    split = column.reshape(32, SENT // 4, HID // FULL, FULL)
    w_in = split[:, 0].reshape(LANES, 4, LANES).transpose(1, 0, 2).reshape(FULL, LANES)
    w_out = split[:, 1].reshape(LANES, FULL).T
    block = jnp.concatenate([w_in, w_out], axis=0)
    planes = [[xy * 2 + high for xy in range(16)] for high in range(2)]
    whole_weights = lax.all_gather(block, "spatial", axis=0, axis_index_groups=planes, tiled=True)
    return whole_weights.reshape(16, 2 * FULL, LANES)


def shards(field_in, spectral_weight, proj_in, bias_in, proj_out):
    column = gather_first(proj_in, proj_out)
    bias = bias_in.reshape(16, 16, 2, 4).transpose(1, 2, 0, 3).reshape(16, LANES)
    rows = field_in.transpose(1, 0, 2).reshape(ROWS, NLON)
    first = (lax.axis_index("spatial") * ORDERS).astype(jnp.int32).reshape(1)

    def analyse(step, carry):
        spectrum, table = forward(rows)
        pencil = lax.all_to_all(
            spectrum.reshape(BANDS, 2 * ORDERS, ROWS),
            "spatial",
            split_axis=0,
            concat_axis=0,
            tiled=True,
        )
        polar, laid = legendre(first, bias)
        return spectral_filter(pencil.reshape(PARTS, ROWS), polar, spectral_weight), table, laid

    steps = 1 + (lax.axis_index("field") >> 8)
    synth, table, bias = lax.fori_loop(
        0,
        steps,
        analyse,
        (jnp.zeros((PARTS, ROWS), BF16), jnp.zeros((PARTS, NLON), BF16), bias),
    )
    synth, column = lax.optimization_barrier((synth, column))
    weights = gather_second(column)
    returned = lax.all_to_all(
        synth.reshape(BANDS, 2 * ORDERS, ROWS), "spatial", split_axis=0, concat_axis=0, tiled=True
    )
    mixed = inverse(returned.reshape(PARTS, ROWS), table, rows)
    points = lax.all_to_all(
        mixed.reshape(MEMBERS, BLOCK, LONS), "field", split_axis=0, concat_axis=0, tiled=True
    )
    result = mlp(points.reshape(MEMBERS * BLOCK, LONS), weights, bias)
    homed = lax.all_to_all(
        result.reshape(MEMBERS, BLOCK, LONS), "field", split_axis=0, concat_axis=0, tiled=True
    )
    return home(homed.reshape(MEMBERS * BLOCK, LONS)).reshape(BAND, CHANS, NLON).transpose(1, 0, 2)


def solution(mesh):
    in_specs = (
        P("field", "spatial", None),
        P(None, "field", None),
        P(("field", "spatial"), None),
        P(),
        P(("field", "spatial"), None),
    )
    out_specs = P("field", "spatial", None)
    return jax.shard_map(shards, mesh=mesh, in_specs=in_specs, out_specs=out_specs, check_vma=False)
```

```python
import functools
import math

import jax
import jax.numpy as jnp
from jax import lax
from jax.experimental import pallas as pl
from jax.experimental.pallas import tpu as pltpu
from jax.sharding import PartitionSpec as P

F32 = jnp.float32
BF16 = jnp.bfloat16

CHANS = 32
BAND = 12
BANDS = 32
ORDERS = 12
NLAT = 384
NLON = 1024
LMAX = 384
HID = 2048
FULL = 512
MEMBERS = 16
ROWS = CHANS * BAND
PARTS = 2 * BANDS * ORDERS
POINTS = 768
LONS = 256
LATS = 3
BLOCK = LATS * CHANS
LANES = 128
PAIRS = 3
PAD = 16
VMEM = 56 * 1024 * 1024


def params():
    return pltpu.CompilerParams(vmem_limit_bytes=VMEM)


def lanes(tile):
    return slice(tile * LANES, (tile + 1) * LANES)


def whole():
    return pl.BlockSpec(memory_space=pltpu.VMEM)


def forward_kernel(x_ref, y_ref, t_ref):
    unit = 2.0 * math.pi / NLON
    place = lax.broadcasted_iota(jnp.int32, (PAD, NLON), 1)
    row = lax.broadcasted_iota(jnp.int32, (PAD, NLON), 0)
    angle = unit * (((row >> 1) * place + (row & 1) * (NLON // 4)) & (NLON - 1)).astype(F32)
    turn = unit * ((place[:8] * 8) & (NLON - 1)).astype(F32)
    turn_cos = jnp.concatenate([jnp.cos(turn)] * 2, axis=0)
    turn_sin = jnp.concatenate([jnp.sin(turn)] * 2, axis=0)

    def turned(step, carry):
        cos, sin = carry
        t_ref[pl.ds(pl.multiple_of(step * PAD, PAD), PAD), :] = cos.astype(BF16)
        return (cos * turn_cos - sin * turn_sin, sin * turn_cos + cos * turn_sin)

    lax.fori_loop(0, PARTS // PAD, turned, (jnp.cos(angle), jnp.sin(angle)))

    def transform(step, carry):
        at = pl.ds(pl.multiple_of(step * 128, 128), 128)
        y = lax.dot_general(
            t_ref[at, :], x_ref[...], (((1,), (1,)), ((), ())), preferred_element_type=F32
        )
        y_ref[at, :] = (y * (1.0 / NLON)).astype(BF16)
        return carry

    lax.fori_loop(0, PARTS // 128, transform, 0)


def forward(x):
    return pl.pallas_call(
        forward_kernel,
        out_shape=(
            jax.ShapeDtypeStruct((PARTS, ROWS), BF16),
            jax.ShapeDtypeStruct((PARTS, NLON), BF16),
        ),
        in_specs=[whole()],
        out_specs=(whole(), whole()),
        compiler_params=params(),
        name="forward_fourier",
    )(x)


def theta_of(lane):
    lat = (lane & (BANDS - 1)) * BAND + (lane >> 5)
    return (lat.astype(F32) + 0.5) * (math.pi / NLAT)


def legendre_kernel(first_ref, bias_ref, table_ref, laid_ref, work_ref):
    laid_ref[...] = bias_ref[...]
    first = first_ref[0]
    lane = lax.broadcasted_iota(jnp.int32, (PAD, NLAT), 1)
    theta = theta_of(lane)
    cosine = jnp.cos(theta)
    sine = jnp.sin(theta)
    order = first + lax.broadcasted_iota(jnp.int32, (PAD, NLAT), 0)
    order = jnp.minimum(order, LMAX - 1)
    level0 = order.astype(F32)
    step0 = (lane + 1).astype(F32)
    factor = jnp.where(lane < order, jnp.log2((2.0 * step0 - 1.0) / (2.0 * step0)), 0.0)
    log_start = 0.5 * (jnp.log2(level0 + 0.5) + jnp.sum(factor, axis=1, keepdims=True))
    log_start = log_start + level0 * jnp.log2(sine)
    whole_part = jnp.floor(log_start)
    start = jnp.exp2(log_start - whole_part)
    narrow = level0[:, :128]
    square = narrow * narrow

    def eight(group, carry):
        current, previous, power = carry
        half = jnp.exp2(0.5 * power)
        for inner in range(8):
            degree = group * 8 + inner
            level = degree.astype(F32)
            inverse = lax.rsqrt(jnp.maximum(level * level - square, 1.0))
            alpha = inverse * jnp.sqrt(
                jnp.maximum(jnp.full_like(square, 4.0) * (level * level) - 1.0, 0.0)
            )
            ratio = jnp.full_like(square, 1.0) * (2.0 * level + 1.0)
            ratio = ratio / jnp.maximum(jnp.full_like(square, 1.0) * (2.0 * level - 3.0), 1.0)
            below = level - 1.0
            beta = inverse * jnp.sqrt(jnp.maximum(ratio * (below * below - square), 0.0))
            alpha = jnp.concatenate([alpha] * 3, axis=1)
            beta = jnp.concatenate([beta] * 3, axis=1)
            stepped = (alpha * cosine) * current - beta * previous
            fresh = order == degree
            previous = jnp.where(fresh, 0.0, current)
            current = jnp.where(fresh, start, stepped)
            at = pl.ds(pl.multiple_of(degree * PAD, PAD), PAD)
            value = (current * half) * half
            for tile in range(3):
                work_ref[tile, at, :] = value[:, lanes(tile)]
        size = jnp.abs(current) + jnp.abs(previous)
        live = size > 0.0
        shift = jnp.where(live, jnp.floor(jnp.log2(jnp.where(live, size, 1.0))), 0.0)
        scale = jnp.exp2(-shift)
        return (current * scale, previous * scale, power + shift)

    nought = jnp.zeros((PAD, NLAT), F32)
    lax.fori_loop(0, LMAX // 8, eight, (nought, nought, whole_part))

    def store(item, carry):
        for tile in range(3):
            table_ref[item, :, lanes(tile)] = work_ref[
                tile, pl.ds(item, LMAX, stride=PAD), :
            ].astype(BF16)
        return carry

    lax.fori_loop(0, ORDERS, store, 0)


def legendre(first, bias):
    return pl.pallas_call(
        legendre_kernel,
        out_shape=(
            jax.ShapeDtypeStruct((ORDERS, LMAX, NLAT), BF16),
            jax.ShapeDtypeStruct(bias.shape, F32),
        ),
        in_specs=[pl.BlockSpec(memory_space=pltpu.SMEM), whole()],
        out_specs=(whole(), whole()),
        scratch_shapes=[pltpu.VMEM((3, LMAX * PAD, LANES), F32)],
        compiler_params=params(),
        cost_estimate=pl.CostEstimate(
            flops=100_000_000, bytes_accessed=20_000_000, transcendentals=1_000_000
        ),
        name="legendre_table",
    )(first, bias)


def filter_kernel(r_ref, p_ref, w_ref, s_ref, rin, sout, quad):
    step = pl.program_id(0)
    group = 4 * CHANS

    @pl.when(step == 0)
    def _():
        for tile in range(3):
            rin[tile] = r_ref[:, lanes(tile)].astype(F32)
        lane = lax.broadcasted_iota(jnp.int32, (8, NLAT), 1)
        quad[...] = jnp.sin(theta_of(lane)) * (math.pi / NLAT)

    lane32 = lax.broadcasted_iota(jnp.int32, (BANDS, group), 1) >> 5

    def exchanged(blocks):
        out = []
        for to in range(4):
            block = blocks[to]
            for at in range(4):
                if at != to:
                    moved = pltpu.roll(blocks[at], (at - to) % 4 * CHANS, 1)
                    block = jnp.where(lane32 == at, moved, block)
            out.append(block)
        return out

    for part_pair in range(PAIRS):
        row = 4 * (step * PAIRS + part_pair)
        tiles = []
        for tile in range(3):
            parts = [
                rin[tile, pl.ds(row + part, BANDS, stride=2 * ORDERS), :] for part in range(4)
            ]
            tiles.append(jnp.concatenate(exchanged(parts), axis=0).T)
        data = jnp.concatenate(tiles, axis=1)
        data = (data * quad[:1, :]).astype(BF16)

        out = []
        for item in range(2):
            table = p_ref[2 * part_pair + item]
            coef = lax.dot_general(
                data[2 * CHANS * item : 2 * CHANS * (item + 1), :],
                table,
                (((1,), (1,)), ((), ())),
                preferred_element_type=F32,
            )
            real, imag = coef[:CHANS], coef[CHANS:]
            filtered = jnp.concatenate(
                [w_ref[0] * real - w_ref[1] * imag, w_ref[0] * imag + w_ref[1] * real], axis=0
            ).astype(BF16)
            out.append(jnp.dot(filtered, table, preferred_element_type=F32))
        synth = jnp.concatenate(out, axis=0)
        for tile in range(3):
            turned = synth[:, lanes(tile)].T
            blocks = exchanged([turned[BANDS * lat : BANDS * (lat + 1), :] for lat in range(4)])
            for part in range(4):
                sout[tile, pl.ds(row + part, BANDS, stride=2 * ORDERS), :] = blocks[part]

    @pl.when(step == pl.num_programs(0) - 1)
    def _():
        for tile in range(3):
            s_ref[:, lanes(tile)] = sout[tile].astype(BF16)


def spectral_filter(received, table, weights):
    same2 = lambda pair: (0, 0)
    return pl.pallas_call(
        filter_kernel,
        grid=(ORDERS // 2 // PAIRS,),
        out_shape=jax.ShapeDtypeStruct((PARTS, ROWS), BF16),
        in_specs=[
            pl.BlockSpec((PARTS, ROWS), same2),
            pl.BlockSpec((2 * PAIRS, LMAX, NLAT), lambda pair: (pair, 0, 0)),
            pl.BlockSpec((2, CHANS, LMAX), lambda pair: (0, 0, 0)),
        ],
        out_specs=pl.BlockSpec((PARTS, ROWS), same2),
        scratch_shapes=[
            pltpu.VMEM((3, PARTS, LANES), F32),
            pltpu.VMEM((3, PARTS, LANES), F32),
            pltpu.VMEM((8, NLAT), F32),
        ],
        compiler_params=params(),
        name="spectral_filter",
    )(received, table, weights)


def inverse_kernel(r_ref, t_ref, xr_ref, m_ref, spectra):
    row = lax.broadcasted_iota(jnp.int32, (PARTS, ROWS), 0)
    gained = jnp.where(row < 2, 1.0, 2.0) * r_ref[...].astype(F32)
    spectra[...] = gained.T.astype(BF16)

    def rows_of(step, carry):
        at = pl.ds(pl.multiple_of(step * BLOCK, BLOCK), BLOCK)
        smooth = jnp.dot(spectra[at, :], t_ref[...], preferred_element_type=F32)
        mixed = (xr_ref[at, :].astype(F32) + smooth).astype(BF16)
        for part in range(NLON // LONS):
            to = pl.ds(pl.multiple_of((step * 4 + part) * BLOCK, BLOCK), BLOCK)
            m_ref[to, :] = mixed[:, part * LONS : (part + 1) * LONS]
        return carry

    lax.fori_loop(0, BAND // LATS, rows_of, 0)


def inverse(returned, table, rows):
    return pl.pallas_call(
        inverse_kernel,
        out_shape=jax.ShapeDtypeStruct((MEMBERS * BLOCK, LONS), BF16),
        in_specs=[whole()] * 3,
        out_specs=whole(),
        scratch_shapes=[pltpu.VMEM((ROWS, PARTS), BF16)],
        compiler_params=params(),
        name="inverse_fourier",
    )(returned, table, rows)


def gelu(x):
    root = math.sqrt(2.0 / math.pi)
    half = 0.5 * x
    return half + half * jnp.tanh(x * (root + (root * 0.044715) * (x * x)))


def mlp_kernel(r_ref, w_ref, bias_ref, o_ref, points, act, w_out):
    step = pl.program_id(0)
    rows = w_ref.shape[0] * LANES

    @pl.when(step == 0)
    def _():
        blocks = r_ref[...].reshape(MEMBERS, BLOCK, LONS)
        for lat in range(LATS):
            points[:, lat * LONS : (lat + 1) * LONS] = blocks[
                :, lat * CHANS : (lat + 1) * CHANS, :
            ].reshape(FULL, LONS)

    w_in, bias = [], []
    for part in range(w_ref.shape[0]):
        block = w_ref[part]
        column = bias_ref[pl.ds(step * w_ref.shape[0] + part, 1), :]
        bias.append(jnp.broadcast_to(column, (LANES, LANES)).T)
        w_in.append(
            jnp.concatenate([block[LANES * tile : LANES * (tile + 1)] for tile in range(4)], axis=1)
        )
        at = pl.ds(pl.multiple_of((step * w_ref.shape[0] + part) * LANES, LANES), LANES)
        w_out[:, at] = block[FULL:]
    w_in = jnp.concatenate(w_in, axis=0)
    bias = jnp.concatenate([jnp.concatenate(bias, axis=0)] * (LONS // LANES), axis=1)
    at = pl.ds(pl.multiple_of(step * rows, rows), rows)
    for lat in range(LATS):
        cols = slice(lat * LONS, (lat + 1) * LONS)
        pre = jnp.dot(w_in, points[:, cols], preferred_element_type=F32) + bias
        act[at, cols] = gelu(pre).astype(BF16)

    @pl.when(step == pl.num_programs(0) - 1)
    def _():
        for lat in range(LATS):
            cols = slice(lat * LONS, (lat + 1) * LONS)
            branch = jnp.dot(w_out[...], act[:, cols], preferred_element_type=F32)
            out = (points[:, cols].astype(F32) + branch).astype(BF16)
            for member in range(MEMBERS):
                to = member * BLOCK + lat * CHANS
                o_ref[to : to + CHANS, :] = out[member * CHANS : (member + 1) * CHANS, :]


def mlp(received, weights, bias):
    blocks = weights.shape[0]
    take = 8
    same2 = lambda step: (0, 0)
    return pl.pallas_call(
        mlp_kernel,
        grid=(blocks // take,),
        out_shape=jax.ShapeDtypeStruct((MEMBERS * BLOCK, LONS), BF16),
        in_specs=[
            pl.BlockSpec((MEMBERS * BLOCK, LONS), same2),
            pl.BlockSpec((take, 2 * FULL, LANES), lambda step: (step, 0, 0)),
            pl.BlockSpec((blocks, LANES), same2),
        ],
        out_specs=pl.BlockSpec((MEMBERS * BLOCK, LONS), same2),
        scratch_shapes=[
            pltpu.VMEM((FULL, POINTS), BF16),
            pltpu.VMEM((HID, POINTS), BF16),
            pltpu.VMEM((FULL, HID), BF16),
        ],
        compiler_params=params(),
        name="pointwise_mlp",
    )(received, weights, bias)


def home_kernel(r_ref, o_ref):
    for member in range(MEMBERS):
        lat, part = member // 4, member % 4
        o_ref[lat * BLOCK : (lat + 1) * BLOCK, part * LONS : (part + 1) * LONS] = r_ref[
            member * BLOCK : (member + 1) * BLOCK, :
        ]


def home(received):
    return pl.pallas_call(
        home_kernel,
        out_shape=jax.ShapeDtypeStruct((ROWS, NLON), BF16),
        in_specs=[whole()],
        out_specs=whole(),
        compiler_params=params(),
        name="home_layout",
    )(received)


SENT = 32


def gather_first(proj_in, proj_out):
    column = [[xy * 32 + place for place in range(32)] for xy in range(16)]
    both = jnp.concatenate([proj_in, proj_out], axis=0)
    both = jnp.pad(both, ((0, SENT - both.shape[0]), (0, 0)))
    return lax.all_gather(both, ("spatial", "field"), axis=0, axis_index_groups=column, tiled=True)


def gather_second(column):
    split = column.reshape(32, SENT // 4, HID // FULL, FULL)
    w_in = split[:, 0].reshape(LANES, 4, LANES).transpose(1, 0, 2).reshape(FULL, LANES)
    w_out = split[:, 1].reshape(LANES, FULL).T
    block = jnp.concatenate([w_in, w_out], axis=0)
    planes = [[xy * 2 + high for xy in range(16)] for high in range(2)]
    whole_weights = lax.all_gather(block, "spatial", axis=0, axis_index_groups=planes, tiled=True)
    return whole_weights.reshape(16, 2 * FULL, LANES)


def shards(field_in, spectral_weight, proj_in, bias_in, proj_out):
    column = gather_first(proj_in, proj_out)
    bias = bias_in.reshape(16, 16, 2, 4).transpose(1, 2, 0, 3).reshape(16, LANES)
    rows = field_in.transpose(1, 0, 2).reshape(ROWS, NLON)
    spectrum, table = forward(rows)
    first = (lax.axis_index("spatial") * ORDERS).astype(jnp.int32).reshape(1)

    def swap(blocks):
        return lax.all_to_all(blocks, "spatial", split_axis=0, concat_axis=0, tiled=True)

    def filtered(step, carry):
        held, laid = carry
        polar, laid = legendre(first, laid)
        synth = spectral_filter(swap(held).reshape(PARTS, ROWS), polar, spectral_weight)
        return swap(synth.reshape(BANDS, 2 * ORDERS, ROWS)), laid

    steps = 1 + (lax.axis_index("field") >> 8)
    returned, bias = lax.fori_loop(
        0, steps, filtered, (spectrum.reshape(BANDS, 2 * ORDERS, ROWS), bias)
    )
    returned, column = lax.optimization_barrier((returned, column))
    weights = gather_second(column)
    mixed = inverse(returned.reshape(PARTS, ROWS), table, rows)
    points = lax.all_to_all(
        mixed.reshape(MEMBERS, BLOCK, LONS), "field", split_axis=0, concat_axis=0, tiled=True
    )
    result = mlp(points.reshape(MEMBERS * BLOCK, LONS), weights, bias)
    homed = lax.all_to_all(
        result.reshape(MEMBERS, BLOCK, LONS), "field", split_axis=0, concat_axis=0, tiled=True
    )
    return home(homed.reshape(MEMBERS * BLOCK, LONS)).reshape(BAND, CHANS, NLON).transpose(1, 0, 2)


def solution(mesh):
    in_specs = (
        P("field", "spatial", None),
        P(None, "field", None),
        P(("field", "spatial"), None),
        P(),
        P(("field", "spatial"), None),
    )
    out_specs = P("field", "spatial", None)
    return jax.shard_map(shards, mesh=mesh, in_specs=in_specs, out_specs=out_specs, check_vma=False)
```

```python
import functools
import math

import jax
import jax.numpy as jnp
from jax import lax
from jax.experimental import pallas as pl
from jax.experimental.pallas import tpu as pltpu
from jax.sharding import PartitionSpec as P

F32 = jnp.float32
BF16 = jnp.bfloat16

CHANS = 32
BAND = 12
BANDS = 32
ORDERS = 12
NLAT = 384
NLON = 1024
LMAX = 384
HID = 2048
FULL = 512
MEMBERS = 16
ROWS = CHANS * BAND
PARTS = 2 * BANDS * ORDERS
POINTS = 768
LONS = 256
LATS = 3
BLOCK = LATS * CHANS
LANES = 128
PAIRS = 3
PAD = 16
VMEM = 56 * 1024 * 1024


def params():
    return pltpu.CompilerParams(vmem_limit_bytes=VMEM)


def lanes(tile):
    return slice(tile * LANES, (tile + 1) * LANES)


def whole():
    return pl.BlockSpec(memory_space=pltpu.VMEM)


def forward_kernel(x_ref, y_ref, t_ref):
    unit = 2.0 * math.pi / NLON
    place = lax.broadcasted_iota(jnp.int32, (PAD, NLON), 1)
    row = lax.broadcasted_iota(jnp.int32, (PAD, NLON), 0)
    angle = unit * (((row >> 1) * place + (row & 1) * (NLON // 4)) & (NLON - 1)).astype(F32)
    turn = unit * ((place[:8] * 8) & (NLON - 1)).astype(F32)
    turn_cos = jnp.concatenate([jnp.cos(turn)] * 2, axis=0)
    turn_sin = jnp.concatenate([jnp.sin(turn)] * 2, axis=0)

    def turned(step, carry):
        cos, sin = carry
        t_ref[pl.ds(pl.multiple_of(step * PAD, PAD), PAD), :] = cos.astype(BF16)
        return (cos * turn_cos - sin * turn_sin, sin * turn_cos + cos * turn_sin)

    lax.fori_loop(0, PARTS // PAD, turned, (jnp.cos(angle), jnp.sin(angle)))

    def transform(step, carry):
        at = pl.ds(pl.multiple_of(step * 128, 128), 128)
        y = lax.dot_general(
            t_ref[at, :], x_ref[...], (((1,), (1,)), ((), ())), preferred_element_type=F32
        )
        y_ref[at, :] = (y * (1.0 / NLON)).astype(BF16)
        return carry

    lax.fori_loop(0, PARTS // 128, transform, 0)


def forward(x):
    return pl.pallas_call(
        forward_kernel,
        out_shape=(
            jax.ShapeDtypeStruct((PARTS, ROWS), BF16),
            jax.ShapeDtypeStruct((PARTS, NLON), BF16),
        ),
        in_specs=[whole()],
        out_specs=(whole(), whole()),
        compiler_params=params(),
        name="forward_fourier",
    )(x)


def theta_of(lane):
    lat = (lane & (BANDS - 1)) * BAND + (lane >> 5)
    return (lat.astype(F32) + 0.5) * (math.pi / NLAT)


def legendre_kernel(first_ref, bias_ref, table_ref, laid_ref, work_ref):
    laid_ref[...] = bias_ref[...]
    first = first_ref[0]
    lane = lax.broadcasted_iota(jnp.int32, (PAD, NLAT), 1)
    theta = theta_of(lane)
    cosine = jnp.cos(theta)
    sine = jnp.sin(theta)
    order = first + lax.broadcasted_iota(jnp.int32, (PAD, NLAT), 0)
    order = jnp.minimum(order, LMAX - 1)
    level0 = order.astype(F32)
    step0 = (lane + 1).astype(F32)
    factor = jnp.where(lane < order, jnp.log2((2.0 * step0 - 1.0) / (2.0 * step0)), 0.0)
    log_start = 0.5 * (jnp.log2(level0 + 0.5) + jnp.sum(factor, axis=1, keepdims=True))
    log_start = log_start + level0 * jnp.log2(sine)
    whole_part = jnp.floor(log_start)
    start = jnp.exp2(log_start - whole_part)
    narrow = level0[:, :128]
    square = narrow * narrow

    def eight(group, carry):
        current, previous, power = carry
        half = jnp.exp2(0.5 * power)
        for inner in range(8):
            degree = group * 8 + inner
            level = degree.astype(F32)
            inverse = lax.rsqrt(jnp.maximum(level * level - square, 1.0))
            alpha = inverse * jnp.sqrt(
                jnp.maximum(jnp.full_like(square, 4.0) * (level * level) - 1.0, 0.0)
            )
            ratio = jnp.full_like(square, 1.0) * (2.0 * level + 1.0)
            ratio = ratio / jnp.maximum(jnp.full_like(square, 1.0) * (2.0 * level - 3.0), 1.0)
            below = level - 1.0
            beta = inverse * jnp.sqrt(jnp.maximum(ratio * (below * below - square), 0.0))
            alpha = jnp.concatenate([alpha] * 3, axis=1)
            beta = jnp.concatenate([beta] * 3, axis=1)
            stepped = (alpha * cosine) * current - beta * previous
            fresh = order == degree
            previous = jnp.where(fresh, 0.0, current)
            current = jnp.where(fresh, start, stepped)
            at = pl.ds(pl.multiple_of(degree * PAD, PAD), PAD)
            value = (current * half) * half
            for tile in range(3):
                work_ref[tile, at, :] = value[:, lanes(tile)]
        size = jnp.abs(current) + jnp.abs(previous)
        live = size > 0.0
        shift = jnp.where(live, jnp.floor(jnp.log2(jnp.where(live, size, 1.0))), 0.0)
        scale = jnp.exp2(-shift)
        return (current * scale, previous * scale, power + shift)

    nought = jnp.zeros((PAD, NLAT), F32)
    lax.fori_loop(0, LMAX // 8, eight, (nought, nought, whole_part))

    def store(item, carry):
        for tile in range(3):
            table_ref[item, :, lanes(tile)] = work_ref[
                tile, pl.ds(item, LMAX, stride=PAD), :
            ].astype(BF16)
        return carry

    lax.fori_loop(0, ORDERS, store, 0)


def legendre(first, bias):
    return pl.pallas_call(
        legendre_kernel,
        out_shape=(
            jax.ShapeDtypeStruct((ORDERS, LMAX, NLAT), BF16),
            jax.ShapeDtypeStruct(bias.shape, F32),
        ),
        in_specs=[pl.BlockSpec(memory_space=pltpu.SMEM), whole()],
        out_specs=(whole(), whole()),
        scratch_shapes=[pltpu.VMEM((3, LMAX * PAD, LANES), F32)],
        compiler_params=params(),
        cost_estimate=pl.CostEstimate(
            flops=100_000_000, bytes_accessed=20_000_000, transcendentals=1_000_000
        ),
        name="legendre_table",
    )(first, bias)


def filter_kernel(r_ref, p_ref, w_ref, s_ref, rin, sout, quad):
    step = pl.program_id(0)
    group = 4 * CHANS

    @pl.when(step == 0)
    def _():
        for tile in range(3):
            rin[tile] = r_ref[:, lanes(tile)].astype(F32)
        lane = lax.broadcasted_iota(jnp.int32, (8, NLAT), 1)
        quad[...] = jnp.sin(theta_of(lane)) * (math.pi / NLAT)

    lane32 = lax.broadcasted_iota(jnp.int32, (BANDS, group), 1) >> 5

    def exchanged(blocks):
        out = []
        for to in range(4):
            block = blocks[to]
            for at in range(4):
                if at != to:
                    moved = pltpu.roll(blocks[at], (at - to) % 4 * CHANS, 1)
                    block = jnp.where(lane32 == at, moved, block)
            out.append(block)
        return out

    for part_pair in range(PAIRS):
        row = 4 * (step * PAIRS + part_pair)
        tiles = []
        for tile in range(3):
            parts = [
                rin[tile, pl.ds(row + part, BANDS, stride=2 * ORDERS), :] for part in range(4)
            ]
            tiles.append(jnp.concatenate(exchanged(parts), axis=0).T)
        data = jnp.concatenate(tiles, axis=1)
        data = (data * quad[:1, :]).astype(BF16)

        out = []
        for item in range(2):
            table = p_ref[2 * part_pair + item]
            coef = lax.dot_general(
                data[2 * CHANS * item : 2 * CHANS * (item + 1), :],
                table,
                (((1,), (1,)), ((), ())),
                preferred_element_type=F32,
            )
            real, imag = coef[:CHANS], coef[CHANS:]
            filtered = jnp.concatenate(
                [w_ref[0] * real - w_ref[1] * imag, w_ref[0] * imag + w_ref[1] * real], axis=0
            ).astype(BF16)
            out.append(jnp.dot(filtered, table, preferred_element_type=F32))
        synth = jnp.concatenate(out, axis=0)
        for tile in range(3):
            turned = synth[:, lanes(tile)].T
            blocks = exchanged([turned[BANDS * lat : BANDS * (lat + 1), :] for lat in range(4)])
            for part in range(4):
                sout[tile, pl.ds(row + part, BANDS, stride=2 * ORDERS), :] = blocks[part]

    @pl.when(step == pl.num_programs(0) - 1)
    def _():
        for tile in range(3):
            s_ref[:, lanes(tile)] = sout[tile].astype(BF16)


def spectral_filter(received, table, weights):
    same2 = lambda pair: (0, 0)
    return pl.pallas_call(
        filter_kernel,
        grid=(ORDERS // 2 // PAIRS,),
        out_shape=jax.ShapeDtypeStruct((PARTS, ROWS), BF16),
        in_specs=[
            pl.BlockSpec((PARTS, ROWS), same2),
            pl.BlockSpec((2 * PAIRS, LMAX, NLAT), lambda pair: (pair, 0, 0)),
            pl.BlockSpec((2, CHANS, LMAX), lambda pair: (0, 0, 0)),
        ],
        out_specs=pl.BlockSpec((PARTS, ROWS), same2),
        scratch_shapes=[
            pltpu.VMEM((3, PARTS, LANES), F32),
            pltpu.VMEM((3, PARTS, LANES), F32),
            pltpu.VMEM((8, NLAT), F32),
        ],
        compiler_params=params(),
        name="spectral_filter",
    )(received, table, weights)


def inverse_kernel(r_ref, t_ref, xr_ref, m_ref, spectra):
    row = lax.broadcasted_iota(jnp.int32, (PARTS, ROWS), 0)
    gained = jnp.where(row < 2, 1.0, 2.0) * r_ref[...].astype(F32)
    spectra[...] = gained.T.astype(BF16)

    def rows_of(step, carry):
        at = pl.ds(pl.multiple_of(step * BLOCK, BLOCK), BLOCK)
        smooth = jnp.dot(spectra[at, :], t_ref[...], preferred_element_type=F32)
        mixed = (xr_ref[at, :].astype(F32) + smooth).astype(BF16)
        for part in range(NLON // LONS):
            to = pl.ds(pl.multiple_of((step * 4 + part) * BLOCK, BLOCK), BLOCK)
            m_ref[to, :] = mixed[:, part * LONS : (part + 1) * LONS]
        return carry

    lax.fori_loop(0, BAND // LATS, rows_of, 0)


def inverse(returned, table, rows):
    return pl.pallas_call(
        inverse_kernel,
        out_shape=jax.ShapeDtypeStruct((MEMBERS * BLOCK, LONS), BF16),
        in_specs=[whole()] * 3,
        out_specs=whole(),
        scratch_shapes=[pltpu.VMEM((ROWS, PARTS), BF16)],
        compiler_params=params(),
        name="inverse_fourier",
    )(returned, table, rows)


def gelu(x):
    root = math.sqrt(2.0 / math.pi)
    half = 0.5 * x
    return half + half * jnp.tanh(x * (root + (root * 0.044715) * (x * x)))


def mlp_kernel(r_ref, w_ref, bias_ref, o_ref, points, act, w_out):
    step = pl.program_id(0)
    rows = w_ref.shape[0] * LANES

    @pl.when(step == 0)
    def _():
        blocks = r_ref[...].reshape(MEMBERS, BLOCK, LONS)
        for lat in range(LATS):
            points[:, lat * LONS : (lat + 1) * LONS] = blocks[
                :, lat * CHANS : (lat + 1) * CHANS, :
            ].reshape(FULL, LONS)

    w_in, bias = [], []
    for part in range(w_ref.shape[0]):
        block = w_ref[part]
        column = bias_ref[pl.ds(step * w_ref.shape[0] + part, 1), :]
        bias.append(jnp.broadcast_to(column, (LANES, LANES)).T)
        w_in.append(
            jnp.concatenate([block[LANES * tile : LANES * (tile + 1)] for tile in range(4)], axis=1)
        )
        at = pl.ds(pl.multiple_of((step * w_ref.shape[0] + part) * LANES, LANES), LANES)
        w_out[:, at] = block[FULL:]
    w_in = jnp.concatenate(w_in, axis=0)
    bias = jnp.concatenate([jnp.concatenate(bias, axis=0)] * (LONS // LANES), axis=1)
    at = pl.ds(pl.multiple_of(step * rows, rows), rows)
    for lat in range(LATS):
        cols = slice(lat * LONS, (lat + 1) * LONS)
        pre = jnp.dot(w_in, points[:, cols], preferred_element_type=F32) + bias
        act[at, cols] = gelu(pre).astype(BF16)

    @pl.when(step == pl.num_programs(0) - 1)
    def _():
        for lat in range(LATS):
            cols = slice(lat * LONS, (lat + 1) * LONS)
            branch = jnp.dot(w_out[...], act[:, cols], preferred_element_type=F32)
            out = (points[:, cols].astype(F32) + branch).astype(BF16)
            for member in range(MEMBERS):
                to = member * BLOCK + lat * CHANS
                o_ref[to : to + CHANS, :] = out[member * CHANS : (member + 1) * CHANS, :]


def mlp(received, weights, bias):
    blocks = weights.shape[0]
    take = 8
    same2 = lambda step: (0, 0)
    return pl.pallas_call(
        mlp_kernel,
        grid=(blocks // take,),
        out_shape=jax.ShapeDtypeStruct((MEMBERS * BLOCK, LONS), BF16),
        in_specs=[
            pl.BlockSpec((MEMBERS * BLOCK, LONS), same2),
            pl.BlockSpec((take, 2 * FULL, LANES), lambda step: (step, 0, 0)),
            pl.BlockSpec((blocks, LANES), same2),
        ],
        out_specs=pl.BlockSpec((MEMBERS * BLOCK, LONS), same2),
        scratch_shapes=[
            pltpu.VMEM((FULL, POINTS), BF16),
            pltpu.VMEM((HID, POINTS), BF16),
            pltpu.VMEM((FULL, HID), BF16),
        ],
        compiler_params=params(),
        name="pointwise_mlp",
    )(received, weights, bias)


def home_kernel(r_ref, o_ref):
    for member in range(MEMBERS):
        lat, part = member // 4, member % 4
        o_ref[lat * BLOCK : (lat + 1) * BLOCK, part * LONS : (part + 1) * LONS] = r_ref[
            member * BLOCK : (member + 1) * BLOCK, :
        ]


def home(received):
    return pl.pallas_call(
        home_kernel,
        out_shape=jax.ShapeDtypeStruct((ROWS, NLON), BF16),
        in_specs=[whole()],
        out_specs=whole(),
        compiler_params=params(),
        name="home_layout",
    )(received)


def gather_first(proj_in, proj_out):
    column = [[xy * 32 + place for place in range(32)] for xy in range(16)]
    both = jnp.concatenate([proj_in, proj_out], axis=0)
    return lax.all_to_all(
        jnp.broadcast_to(both[None], (32,) + both.shape),
        ("spatial", "field"),
        split_axis=0,
        concat_axis=0,
        axis_index_groups=column,
        tiled=True,
    )


def gather_second(column):
    split = column.reshape(32, 2, HID // FULL, FULL)
    w_in = split[:, 0].reshape(LANES, 4, LANES).transpose(1, 0, 2).reshape(FULL, LANES)
    w_out = split[:, 1].reshape(LANES, FULL).T
    block = jnp.concatenate([w_in, w_out], axis=0)
    planes = [[xy * 2 + high for xy in range(16)] for high in range(2)]
    whole_weights = lax.all_gather(block, "spatial", axis=0, axis_index_groups=planes, tiled=True)
    return whole_weights.reshape(16, 2 * FULL, LANES)


def shards(field_in, spectral_weight, proj_in, bias_in, proj_out):
    column = gather_first(proj_in, proj_out)
    bias = bias_in.reshape(16, 16, 2, 4).transpose(1, 2, 0, 3).reshape(16, LANES)
    rows = field_in.transpose(1, 0, 2).reshape(ROWS, NLON)
    spectrum, table = forward(rows)
    spectrum, column = lax.optimization_barrier((spectrum, column))
    weights = gather_second(column)
    pencil = lax.all_to_all(
        spectrum.reshape(BANDS, 2 * ORDERS, ROWS), "spatial", split_axis=0, concat_axis=0, tiled=True
    )
    first = (lax.axis_index("spatial") * ORDERS).astype(jnp.int32).reshape(1)
    polar, bias = legendre(first, bias)
    synth = spectral_filter(pencil.reshape(PARTS, ROWS), polar, spectral_weight)
    returned = lax.all_to_all(
        synth.reshape(BANDS, 2 * ORDERS, ROWS), "spatial", split_axis=0, concat_axis=0, tiled=True
    )
    mixed = inverse(returned.reshape(PARTS, ROWS), table, rows)
    points = lax.all_to_all(
        mixed.reshape(MEMBERS, BLOCK, LONS), "field", split_axis=0, concat_axis=0, tiled=True
    )
    result = mlp(points.reshape(MEMBERS * BLOCK, LONS), weights, bias)
    homed = lax.all_to_all(
        result.reshape(MEMBERS, BLOCK, LONS), "field", split_axis=0, concat_axis=0, tiled=True
    )
    return home(homed.reshape(MEMBERS * BLOCK, LONS)).reshape(BAND, CHANS, NLON).transpose(1, 0, 2)


def solution(mesh):
    in_specs = (
        P("field", "spatial", None),
        P(None, "field", None),
        P(("field", "spatial"), None),
        P(),
        P(("field", "spatial"), None),
    )
    out_specs = P("field", "spatial", None)
    return jax.shard_map(shards, mesh=mesh, in_specs=in_specs, out_specs=out_specs, check_vma=False)
```

```python
import functools
import math

import jax
import jax.numpy as jnp
from jax import lax
from jax.experimental import pallas as pl
from jax.experimental.pallas import tpu as pltpu
from jax.sharding import PartitionSpec as P

F32 = jnp.float32
BF16 = jnp.bfloat16

CHANS = 32
BAND = 12
BANDS = 32
ORDERS = 12
NLAT = 384
NLON = 1024
LMAX = 384
HID = 2048
FULL = 512
MEMBERS = 16
ROWS = CHANS * BAND
PARTS = 2 * BANDS * ORDERS
POINTS = 768
LONS = 256
LATS = 3
BLOCK = LATS * CHANS
LANES = 128
PAIRS = 3
PAD = 16
VMEM = 56 * 1024 * 1024


def params():
    return pltpu.CompilerParams(vmem_limit_bytes=VMEM)


def lanes(tile):
    return slice(tile * LANES, (tile + 1) * LANES)


def whole():
    return pl.BlockSpec(memory_space=pltpu.VMEM)


def forward_kernel(x_ref, y_ref, t_ref):
    unit = 2.0 * math.pi / NLON
    place = lax.broadcasted_iota(jnp.int32, (PAD, NLON), 1)
    row = lax.broadcasted_iota(jnp.int32, (PAD, NLON), 0)
    angle = unit * (((row >> 1) * place + (row & 1) * (NLON // 4)) & (NLON - 1)).astype(F32)
    turn = unit * ((place[:8] * 8) & (NLON - 1)).astype(F32)
    turn_cos = jnp.concatenate([jnp.cos(turn)] * 2, axis=0)
    turn_sin = jnp.concatenate([jnp.sin(turn)] * 2, axis=0)

    def turned(step, carry):
        cos, sin = carry
        t_ref[pl.ds(pl.multiple_of(step * PAD, PAD), PAD), :] = cos.astype(BF16)
        return (cos * turn_cos - sin * turn_sin, sin * turn_cos + cos * turn_sin)

    lax.fori_loop(0, PARTS // PAD, turned, (jnp.cos(angle), jnp.sin(angle)))

    def transform(step, carry):
        at = pl.ds(pl.multiple_of(step * 128, 128), 128)
        y = lax.dot_general(
            t_ref[at, :], x_ref[...], (((1,), (1,)), ((), ())), preferred_element_type=F32
        )
        y_ref[at, :] = (y * (1.0 / NLON)).astype(BF16)
        return carry

    lax.fori_loop(0, PARTS // 128, transform, 0)


def forward(x):
    return pl.pallas_call(
        forward_kernel,
        out_shape=(
            jax.ShapeDtypeStruct((PARTS, ROWS), BF16),
            jax.ShapeDtypeStruct((PARTS, NLON), BF16),
        ),
        in_specs=[whole()],
        out_specs=(whole(), whole()),
        compiler_params=params(),
        name="forward_fourier",
    )(x)


def theta_of(lane):
    lat = (lane & (BANDS - 1)) * BAND + (lane >> 5)
    return (lat.astype(F32) + 0.5) * (math.pi / NLAT)


def legendre_kernel(first_ref, bias_ref, table_ref, laid_ref, work_ref):
    laid_ref[...] = bias_ref[...]
    first = first_ref[0]
    lane = lax.broadcasted_iota(jnp.int32, (PAD, NLAT), 1)
    theta = theta_of(lane)
    cosine = jnp.cos(theta)
    sine = jnp.sin(theta)
    order = first + lax.broadcasted_iota(jnp.int32, (PAD, NLAT), 0)
    order = jnp.minimum(order, LMAX - 1)
    level0 = order.astype(F32)
    step0 = (lane + 1).astype(F32)
    factor = jnp.where(lane < order, jnp.log2((2.0 * step0 - 1.0) / (2.0 * step0)), 0.0)
    log_start = 0.5 * (jnp.log2(level0 + 0.5) + jnp.sum(factor, axis=1, keepdims=True))
    log_start = log_start + level0 * jnp.log2(sine)
    whole_part = jnp.floor(log_start)
    start = jnp.exp2(log_start - whole_part)
    narrow = level0[:, :128]
    square = narrow * narrow

    def eight(group, carry):
        current, previous, power = carry
        half = jnp.exp2(0.5 * power)
        for inner in range(8):
            degree = group * 8 + inner
            level = degree.astype(F32)
            inverse = lax.rsqrt(jnp.maximum(level * level - square, 1.0))
            alpha = inverse * jnp.sqrt(
                jnp.maximum(jnp.full_like(square, 4.0) * (level * level) - 1.0, 0.0)
            )
            ratio = jnp.full_like(square, 1.0) * (2.0 * level + 1.0)
            ratio = ratio / jnp.maximum(jnp.full_like(square, 1.0) * (2.0 * level - 3.0), 1.0)
            below = level - 1.0
            beta = inverse * jnp.sqrt(jnp.maximum(ratio * (below * below - square), 0.0))
            alpha = jnp.concatenate([alpha] * 3, axis=1)
            beta = jnp.concatenate([beta] * 3, axis=1)
            stepped = (alpha * cosine) * current - beta * previous
            fresh = order == degree
            previous = jnp.where(fresh, 0.0, current)
            current = jnp.where(fresh, start, stepped)
            at = pl.ds(pl.multiple_of(degree * PAD, PAD), PAD)
            value = (current * half) * half
            for tile in range(3):
                work_ref[tile, at, :] = value[:, lanes(tile)]
        size = jnp.abs(current) + jnp.abs(previous)
        live = size > 0.0
        shift = jnp.where(live, jnp.floor(jnp.log2(jnp.where(live, size, 1.0))), 0.0)
        scale = jnp.exp2(-shift)
        return (current * scale, previous * scale, power + shift)

    nought = jnp.zeros((PAD, NLAT), F32)
    lax.fori_loop(0, LMAX // 8, eight, (nought, nought, whole_part))

    def store(item, carry):
        for tile in range(3):
            table_ref[item, :, lanes(tile)] = work_ref[
                tile, pl.ds(item, LMAX, stride=PAD), :
            ].astype(BF16)
        return carry

    lax.fori_loop(0, ORDERS, store, 0)


def legendre(first, bias):
    return pl.pallas_call(
        legendre_kernel,
        out_shape=(
            jax.ShapeDtypeStruct((ORDERS, LMAX, NLAT), BF16),
            jax.ShapeDtypeStruct(bias.shape, F32),
        ),
        in_specs=[pl.BlockSpec(memory_space=pltpu.SMEM), whole()],
        out_specs=(whole(), whole()),
        scratch_shapes=[pltpu.VMEM((3, LMAX * PAD, LANES), F32)],
        compiler_params=params(),
        cost_estimate=pl.CostEstimate(
            flops=100_000_000, bytes_accessed=20_000_000, transcendentals=1_000_000
        ),
        name="legendre_table",
    )(first, bias)


def filter_kernel(r_ref, p_ref, w_ref, s_ref, rin, sout, quad):
    step = pl.program_id(0)
    group = 4 * CHANS

    @pl.when(step == 0)
    def _():
        for tile in range(3):
            rin[tile] = r_ref[:, lanes(tile)].astype(F32)
        lane = lax.broadcasted_iota(jnp.int32, (8, NLAT), 1)
        quad[...] = jnp.sin(theta_of(lane)) * (math.pi / NLAT)

    lane32 = lax.broadcasted_iota(jnp.int32, (BANDS, group), 1) >> 5

    def exchanged(blocks):
        out = []
        for to in range(4):
            block = blocks[to]
            for at in range(4):
                if at != to:
                    moved = pltpu.roll(blocks[at], (at - to) % 4 * CHANS, 1)
                    block = jnp.where(lane32 == at, moved, block)
            out.append(block)
        return out

    for part_pair in range(PAIRS):
        row = 4 * (step * PAIRS + part_pair)
        tiles = []
        for tile in range(3):
            parts = [
                rin[tile, pl.ds(row + part, BANDS, stride=2 * ORDERS), :] for part in range(4)
            ]
            tiles.append(jnp.concatenate(exchanged(parts), axis=0).T)
        data = jnp.concatenate(tiles, axis=1)
        data = (data * quad[:1, :]).astype(BF16)

        out = []
        for item in range(2):
            table = p_ref[2 * part_pair + item]
            coef = lax.dot_general(
                data[2 * CHANS * item : 2 * CHANS * (item + 1), :],
                table,
                (((1,), (1,)), ((), ())),
                preferred_element_type=F32,
            )
            real, imag = coef[:CHANS], coef[CHANS:]
            filtered = jnp.concatenate(
                [w_ref[0] * real - w_ref[1] * imag, w_ref[0] * imag + w_ref[1] * real], axis=0
            ).astype(BF16)
            out.append(jnp.dot(filtered, table, preferred_element_type=F32))
        synth = jnp.concatenate(out, axis=0)
        for tile in range(3):
            turned = synth[:, lanes(tile)].T
            blocks = exchanged([turned[BANDS * lat : BANDS * (lat + 1), :] for lat in range(4)])
            for part in range(4):
                sout[tile, pl.ds(row + part, BANDS, stride=2 * ORDERS), :] = blocks[part]

    @pl.when(step == pl.num_programs(0) - 1)
    def _():
        for tile in range(3):
            s_ref[:, lanes(tile)] = sout[tile].astype(BF16)


def spectral_filter(received, table, weights):
    same2 = lambda pair: (0, 0)
    return pl.pallas_call(
        filter_kernel,
        grid=(ORDERS // 2 // PAIRS,),
        out_shape=jax.ShapeDtypeStruct((PARTS, ROWS), BF16),
        in_specs=[
            pl.BlockSpec((PARTS, ROWS), same2),
            pl.BlockSpec((2 * PAIRS, LMAX, NLAT), lambda pair: (pair, 0, 0)),
            pl.BlockSpec((2, CHANS, LMAX), lambda pair: (0, 0, 0)),
        ],
        out_specs=pl.BlockSpec((PARTS, ROWS), same2),
        scratch_shapes=[
            pltpu.VMEM((3, PARTS, LANES), F32),
            pltpu.VMEM((3, PARTS, LANES), F32),
            pltpu.VMEM((8, NLAT), F32),
        ],
        compiler_params=params(),
        name="spectral_filter",
    )(received, table, weights)


def inverse_kernel(r_ref, t_ref, xr_ref, m_ref, spectra):
    row = lax.broadcasted_iota(jnp.int32, (PARTS, ROWS), 0)
    gained = jnp.where(row < 2, 1.0, 2.0) * r_ref[...].astype(F32)
    spectra[...] = gained.T.astype(BF16)

    def rows_of(step, carry):
        at = pl.ds(pl.multiple_of(step * BLOCK, BLOCK), BLOCK)
        smooth = jnp.dot(spectra[at, :], t_ref[...], preferred_element_type=F32)
        mixed = (xr_ref[at, :].astype(F32) + smooth).astype(BF16)
        for part in range(NLON // LONS):
            to = pl.ds(pl.multiple_of((step * 4 + part) * BLOCK, BLOCK), BLOCK)
            m_ref[to, :] = mixed[:, part * LONS : (part + 1) * LONS]
        return carry

    lax.fori_loop(0, BAND // LATS, rows_of, 0)


def inverse(returned, table, rows):
    return pl.pallas_call(
        inverse_kernel,
        out_shape=jax.ShapeDtypeStruct((MEMBERS * BLOCK, LONS), BF16),
        in_specs=[whole()] * 3,
        out_specs=whole(),
        scratch_shapes=[pltpu.VMEM((ROWS, PARTS), BF16)],
        compiler_params=params(),
        name="inverse_fourier",
    )(returned, table, rows)


def gelu(x):
    root = math.sqrt(2.0 / math.pi)
    half = 0.5 * x
    return half + half * jnp.tanh(x * (root + (root * 0.044715) * (x * x)))


def mlp_kernel(r_ref, w_ref, bias_ref, o_ref, points, act, w_out):
    step = pl.program_id(0)
    rows = w_ref.shape[0] * LANES

    @pl.when(step == 0)
    def _():
        blocks = r_ref[...].reshape(MEMBERS, BLOCK, LONS)
        for lat in range(LATS):
            points[:, lat * LONS : (lat + 1) * LONS] = blocks[
                :, lat * CHANS : (lat + 1) * CHANS, :
            ].reshape(FULL, LONS)

    w_in, bias = [], []
    for part in range(w_ref.shape[0]):
        block = w_ref[part]
        column = bias_ref[pl.ds(step * w_ref.shape[0] + part, 1), :]
        bias.append(jnp.broadcast_to(column, (LANES, LANES)).T)
        w_in.append(
            jnp.concatenate([block[LANES * tile : LANES * (tile + 1)] for tile in range(4)], axis=1)
        )
        at = pl.ds(pl.multiple_of((step * w_ref.shape[0] + part) * LANES, LANES), LANES)
        w_out[:, at] = block[FULL:]
    w_in = jnp.concatenate(w_in, axis=0)
    bias = jnp.concatenate([jnp.concatenate(bias, axis=0)] * (LONS // LANES), axis=1)
    at = pl.ds(pl.multiple_of(step * rows, rows), rows)
    for lat in range(LATS):
        cols = slice(lat * LONS, (lat + 1) * LONS)
        pre = jnp.dot(w_in, points[:, cols], preferred_element_type=F32) + bias
        act[at, cols] = gelu(pre).astype(BF16)

    @pl.when(step == pl.num_programs(0) - 1)
    def _():
        for lat in range(LATS):
            cols = slice(lat * LONS, (lat + 1) * LONS)
            branch = jnp.dot(w_out[...], act[:, cols], preferred_element_type=F32)
            out = (points[:, cols].astype(F32) + branch).astype(BF16)
            for member in range(MEMBERS):
                to = member * BLOCK + lat * CHANS
                o_ref[to : to + CHANS, :] = out[member * CHANS : (member + 1) * CHANS, :]


def mlp(received, weights, bias):
    blocks = weights.shape[0]
    take = 8
    same2 = lambda step: (0, 0)
    return pl.pallas_call(
        mlp_kernel,
        grid=(blocks // take,),
        out_shape=jax.ShapeDtypeStruct((MEMBERS * BLOCK, LONS), BF16),
        in_specs=[
            pl.BlockSpec((MEMBERS * BLOCK, LONS), same2),
            pl.BlockSpec((take, 2 * FULL, LANES), lambda step: (step, 0, 0)),
            pl.BlockSpec((blocks, LANES), same2),
        ],
        out_specs=pl.BlockSpec((MEMBERS * BLOCK, LONS), same2),
        scratch_shapes=[
            pltpu.VMEM((FULL, POINTS), BF16),
            pltpu.VMEM((HID, POINTS), BF16),
            pltpu.VMEM((FULL, HID), BF16),
        ],
        compiler_params=params(),
        name="pointwise_mlp",
    )(received, weights, bias)


def home_kernel(r_ref, o_ref):
    for member in range(MEMBERS):
        lat, part = member // 4, member % 4
        o_ref[lat * BLOCK : (lat + 1) * BLOCK, part * LONS : (part + 1) * LONS] = r_ref[
            member * BLOCK : (member + 1) * BLOCK, :
        ]


def home(received):
    return pl.pallas_call(
        home_kernel,
        out_shape=jax.ShapeDtypeStruct((ROWS, NLON), BF16),
        in_specs=[whole()],
        out_specs=whole(),
        compiler_params=params(),
        name="home_layout",
    )(received)


def gather_first(proj_in, proj_out):
    held = jnp.concatenate([proj_in, proj_out], axis=0)
    near = [
        [xy * 32 + (4 * four + at) * 2 + core for at in range(4)]
        for xy in range(16)
        for four in range(4)
        for core in range(2)
    ]
    far = [
        [xy * 32 + (4 * four + at) * 2 + core for four in range(4)]
        for xy in range(16)
        for at in range(4)
        for core in range(2)
    ]
    for groups in (near, far):
        rows = held.shape[0]
        held = lax.all_to_all(
            jnp.broadcast_to(held[None], (4,) + held.shape),
            ("spatial", "field"),
            split_axis=0,
            concat_axis=0,
            axis_index_groups=groups,
            tiled=True,
        ).reshape(4 * rows, FULL)
    cores = [[2 * chip, 2 * chip + 1] for chip in range(8)]
    return lax.all_gather(held, "field", axis=0, axis_index_groups=cores, tiled=True)


def gather_second(column):
    split = column.reshape(32, 2, HID // FULL, FULL)
    w_in = split[:, 0].reshape(LANES, 4, LANES).transpose(1, 0, 2).reshape(FULL, LANES)
    w_out = split[:, 1].reshape(LANES, FULL).T
    block = jnp.concatenate([w_in, w_out], axis=0)
    planes = [[xy * 2 + high for xy in range(16)] for high in range(2)]
    whole_weights = lax.all_gather(block, "spatial", axis=0, axis_index_groups=planes, tiled=True)
    return whole_weights.reshape(16, 2 * FULL, LANES)


def shards(field_in, spectral_weight, proj_in, bias_in, proj_out):
    column = gather_first(proj_in, proj_out)
    bias = bias_in.reshape(8, 2, 16, 2, 4).transpose(2, 1, 3, 0, 4).reshape(16, LANES)
    rows = field_in.transpose(1, 0, 2).reshape(ROWS, NLON)
    spectrum, table = forward(rows)
    spectrum, column = lax.optimization_barrier((spectrum, column))
    weights = gather_second(column)
    pencil = lax.all_to_all(
        spectrum.reshape(BANDS, 2 * ORDERS, ROWS), "spatial", split_axis=0, concat_axis=0, tiled=True
    )
    first = (lax.axis_index("spatial") * ORDERS).astype(jnp.int32).reshape(1)
    polar, bias = legendre(first, bias)
    synth = spectral_filter(pencil.reshape(PARTS, ROWS), polar, spectral_weight)
    returned = lax.all_to_all(
        synth.reshape(BANDS, 2 * ORDERS, ROWS), "spatial", split_axis=0, concat_axis=0, tiled=True
    )
    mixed = inverse(returned.reshape(PARTS, ROWS), table, rows)
    points = lax.all_to_all(
        mixed.reshape(MEMBERS, BLOCK, LONS), "field", split_axis=0, concat_axis=0, tiled=True
    )
    result = mlp(points.reshape(MEMBERS * BLOCK, LONS), weights, bias)
    homed = lax.all_to_all(
        result.reshape(MEMBERS, BLOCK, LONS), "field", split_axis=0, concat_axis=0, tiled=True
    )
    return home(homed.reshape(MEMBERS * BLOCK, LONS)).reshape(BAND, CHANS, NLON).transpose(1, 0, 2)


def solution(mesh):
    in_specs = (
        P("field", "spatial", None),
        P(None, "field", None),
        P(("field", "spatial"), None),
        P(),
        P(("field", "spatial"), None),
    )
    out_specs = P("field", "spatial", None)
    return jax.shard_map(shards, mesh=mesh, in_specs=in_specs, out_specs=out_specs, check_vma=False)
```

```python
import functools
import math

import jax
import jax.numpy as jnp
from jax import lax
from jax.experimental import pallas as pl
from jax.experimental.pallas import tpu as pltpu
from jax.sharding import PartitionSpec as P

F32 = jnp.float32
BF16 = jnp.bfloat16

CHANS = 32
BAND = 12
BANDS = 32
ORDERS = 12
NLAT = 384
NLON = 1024
LMAX = 384
HID = 2048
FULL = 512
MEMBERS = 16
ROWS = CHANS * BAND
PARTS = 2 * BANDS * ORDERS
POINTS = 768
LONS = 256
LATS = 3
BLOCK = LATS * CHANS
LANES = 128
PAIRS = 3
PAD = 16
VMEM = 56 * 1024 * 1024


def params():
    return pltpu.CompilerParams(vmem_limit_bytes=VMEM)


def lanes(tile):
    return slice(tile * LANES, (tile + 1) * LANES)


def whole():
    return pl.BlockSpec(memory_space=pltpu.VMEM)


def forward_kernel(x_ref, y_ref, t_ref):
    unit = 2.0 * math.pi / NLON
    place = lax.broadcasted_iota(jnp.int32, (PAD, NLON), 1)
    row = lax.broadcasted_iota(jnp.int32, (PAD, NLON), 0)
    angle = unit * (((row >> 1) * place + (row & 1) * (NLON // 4)) & (NLON - 1)).astype(F32)
    turn = unit * ((place[:8] * 8) & (NLON - 1)).astype(F32)
    turn_cos = jnp.concatenate([jnp.cos(turn)] * 2, axis=0)
    turn_sin = jnp.concatenate([jnp.sin(turn)] * 2, axis=0)

    def turned(step, carry):
        cos, sin = carry
        t_ref[pl.ds(pl.multiple_of(step * PAD, PAD), PAD), :] = cos.astype(BF16)
        return (cos * turn_cos - sin * turn_sin, sin * turn_cos + cos * turn_sin)

    lax.fori_loop(0, PARTS // PAD, turned, (jnp.cos(angle), jnp.sin(angle)))

    def transform(step, carry):
        at = pl.ds(pl.multiple_of(step * 128, 128), 128)
        y = lax.dot_general(
            t_ref[at, :], x_ref[...], (((1,), (1,)), ((), ())), preferred_element_type=F32
        )
        y_ref[at, :] = (y * (1.0 / NLON)).astype(BF16)
        return carry

    lax.fori_loop(0, PARTS // 128, transform, 0)


def forward(x):
    return pl.pallas_call(
        forward_kernel,
        out_shape=(
            jax.ShapeDtypeStruct((PARTS, ROWS), BF16),
            jax.ShapeDtypeStruct((PARTS, NLON), BF16),
        ),
        in_specs=[whole()],
        out_specs=(whole(), whole()),
        compiler_params=params(),
        name="forward_fourier",
    )(x)


def theta_of(lane):
    lat = (lane & (BANDS - 1)) * BAND + (lane >> 5)
    return (lat.astype(F32) + 0.5) * (math.pi / NLAT)


def legendre_kernel(first_ref, bias_ref, table_ref, laid_ref, work_ref):
    laid_ref[...] = bias_ref[...]
    first = first_ref[0]
    lane = lax.broadcasted_iota(jnp.int32, (PAD, NLAT), 1)
    theta = theta_of(lane)
    cosine = jnp.cos(theta)
    sine = jnp.sin(theta)
    order = first + lax.broadcasted_iota(jnp.int32, (PAD, NLAT), 0)
    order = jnp.minimum(order, LMAX - 1)
    level0 = order.astype(F32)
    step0 = (lane + 1).astype(F32)
    factor = jnp.where(lane < order, jnp.log2((2.0 * step0 - 1.0) / (2.0 * step0)), 0.0)
    log_start = 0.5 * (jnp.log2(level0 + 0.5) + jnp.sum(factor, axis=1, keepdims=True))
    log_start = log_start + level0 * jnp.log2(sine)
    whole_part = jnp.floor(log_start)
    start = jnp.exp2(log_start - whole_part)
    narrow = level0[:, :128]
    square = narrow * narrow

    def eight(group, carry):
        current, previous, power = carry
        half = jnp.exp2(0.5 * power)
        for inner in range(8):
            degree = group * 8 + inner
            level = degree.astype(F32)
            inverse = lax.rsqrt(jnp.maximum(level * level - square, 1.0))
            alpha = inverse * jnp.sqrt(
                jnp.maximum(jnp.full_like(square, 4.0) * (level * level) - 1.0, 0.0)
            )
            ratio = jnp.full_like(square, 1.0) * (2.0 * level + 1.0)
            ratio = ratio / jnp.maximum(jnp.full_like(square, 1.0) * (2.0 * level - 3.0), 1.0)
            below = level - 1.0
            beta = inverse * jnp.sqrt(jnp.maximum(ratio * (below * below - square), 0.0))
            alpha = jnp.concatenate([alpha] * 3, axis=1)
            beta = jnp.concatenate([beta] * 3, axis=1)
            stepped = (alpha * cosine) * current - beta * previous
            fresh = order == degree
            previous = jnp.where(fresh, 0.0, current)
            current = jnp.where(fresh, start, stepped)
            at = pl.ds(pl.multiple_of(degree * PAD, PAD), PAD)
            value = (current * half) * half
            for tile in range(3):
                work_ref[tile, at, :] = value[:, lanes(tile)]
        size = jnp.abs(current) + jnp.abs(previous)
        live = size > 0.0
        shift = jnp.where(live, jnp.floor(jnp.log2(jnp.where(live, size, 1.0))), 0.0)
        scale = jnp.exp2(-shift)
        return (current * scale, previous * scale, power + shift)

    nought = jnp.zeros((PAD, NLAT), F32)
    lax.fori_loop(0, LMAX // 8, eight, (nought, nought, whole_part))

    def store(item, carry):
        for tile in range(3):
            table_ref[item, :, lanes(tile)] = work_ref[
                tile, pl.ds(item, LMAX, stride=PAD), :
            ].astype(BF16)
        return carry

    lax.fori_loop(0, ORDERS, store, 0)


def legendre(first, bias):
    return pl.pallas_call(
        legendre_kernel,
        out_shape=(
            jax.ShapeDtypeStruct((ORDERS, LMAX, NLAT), BF16),
            jax.ShapeDtypeStruct(bias.shape, F32),
        ),
        in_specs=[pl.BlockSpec(memory_space=pltpu.SMEM), whole()],
        out_specs=(whole(), whole()),
        scratch_shapes=[pltpu.VMEM((3, LMAX * PAD, LANES), F32)],
        compiler_params=params(),
        cost_estimate=pl.CostEstimate(
            flops=100_000_000, bytes_accessed=20_000_000, transcendentals=1_000_000
        ),
        name="legendre_table",
    )(first, bias)


def filter_kernel(r_ref, p_ref, w_ref, s_ref, rin, sout, quad):
    step = pl.program_id(0)
    group = 4 * CHANS

    @pl.when(step == 0)
    def _():
        for tile in range(3):
            rin[tile] = r_ref[:, lanes(tile)].astype(F32)
        lane = lax.broadcasted_iota(jnp.int32, (8, NLAT), 1)
        quad[...] = jnp.sin(theta_of(lane)) * (math.pi / NLAT)

    lane32 = lax.broadcasted_iota(jnp.int32, (BANDS, group), 1) >> 5

    def exchanged(blocks):
        out = []
        for to in range(4):
            block = blocks[to]
            for at in range(4):
                if at != to:
                    moved = pltpu.roll(blocks[at], (at - to) % 4 * CHANS, 1)
                    block = jnp.where(lane32 == at, moved, block)
            out.append(block)
        return out

    for part_pair in range(PAIRS):
        row = 4 * (step * PAIRS + part_pair)
        tiles = []
        for tile in range(3):
            parts = [
                rin[tile, pl.ds(row + part, BANDS, stride=2 * ORDERS), :] for part in range(4)
            ]
            tiles.append(jnp.concatenate(exchanged(parts), axis=0).T)
        data = jnp.concatenate(tiles, axis=1)
        data = (data * quad[:1, :]).astype(BF16)

        out = []
        for item in range(2):
            table = p_ref[2 * part_pair + item]
            coef = lax.dot_general(
                data[2 * CHANS * item : 2 * CHANS * (item + 1), :],
                table,
                (((1,), (1,)), ((), ())),
                preferred_element_type=F32,
            )
            real, imag = coef[:CHANS], coef[CHANS:]
            filtered = jnp.concatenate(
                [w_ref[0] * real - w_ref[1] * imag, w_ref[0] * imag + w_ref[1] * real], axis=0
            ).astype(BF16)
            out.append(jnp.dot(filtered, table, preferred_element_type=F32))
        synth = jnp.concatenate(out, axis=0)
        for tile in range(3):
            turned = synth[:, lanes(tile)].T
            blocks = exchanged([turned[BANDS * lat : BANDS * (lat + 1), :] for lat in range(4)])
            for part in range(4):
                sout[tile, pl.ds(row + part, BANDS, stride=2 * ORDERS), :] = blocks[part]

    @pl.when(step == pl.num_programs(0) - 1)
    def _():
        for tile in range(3):
            s_ref[:, lanes(tile)] = sout[tile].astype(BF16)


def spectral_filter(received, table, weights):
    same2 = lambda pair: (0, 0)
    return pl.pallas_call(
        filter_kernel,
        grid=(ORDERS // 2 // PAIRS,),
        out_shape=jax.ShapeDtypeStruct((PARTS, ROWS), BF16),
        in_specs=[
            pl.BlockSpec((PARTS, ROWS), same2),
            pl.BlockSpec((2 * PAIRS, LMAX, NLAT), lambda pair: (pair, 0, 0)),
            pl.BlockSpec((2, CHANS, LMAX), lambda pair: (0, 0, 0)),
        ],
        out_specs=pl.BlockSpec((PARTS, ROWS), same2),
        scratch_shapes=[
            pltpu.VMEM((3, PARTS, LANES), F32),
            pltpu.VMEM((3, PARTS, LANES), F32),
            pltpu.VMEM((8, NLAT), F32),
        ],
        compiler_params=params(),
        name="spectral_filter",
    )(received, table, weights)


def inverse_kernel(r_ref, t_ref, xr_ref, m_ref, spectra):
    row = lax.broadcasted_iota(jnp.int32, (PARTS, ROWS), 0)
    gained = jnp.where(row < 2, 1.0, 2.0) * r_ref[...].astype(F32)
    spectra[...] = gained.T.astype(BF16)

    def rows_of(step, carry):
        at = pl.ds(pl.multiple_of(step * BLOCK, BLOCK), BLOCK)
        smooth = jnp.dot(spectra[at, :], t_ref[...], preferred_element_type=F32)
        mixed = (xr_ref[at, :].astype(F32) + smooth).astype(BF16)
        for part in range(NLON // LONS):
            to = pl.ds(pl.multiple_of((step * 4 + part) * BLOCK, BLOCK), BLOCK)
            m_ref[to, :] = mixed[:, part * LONS : (part + 1) * LONS]
        return carry

    lax.fori_loop(0, BAND // LATS, rows_of, 0)


def inverse(returned, table, rows):
    return pl.pallas_call(
        inverse_kernel,
        out_shape=jax.ShapeDtypeStruct((MEMBERS * BLOCK, LONS), BF16),
        in_specs=[whole()] * 3,
        out_specs=whole(),
        scratch_shapes=[pltpu.VMEM((ROWS, PARTS), BF16)],
        compiler_params=params(),
        name="inverse_fourier",
    )(returned, table, rows)


def gelu(x):
    root = math.sqrt(2.0 / math.pi)
    half = 0.5 * x
    return half + half * jnp.tanh(x * (root + (root * 0.044715) * (x * x)))


def mlp_kernel(r_ref, w_ref, bias_ref, o_ref, points, act, w_out):
    step = pl.program_id(0)
    rows = w_ref.shape[0] * LANES

    @pl.when(step == 0)
    def _():
        blocks = r_ref[...].reshape(MEMBERS, BLOCK, LONS)
        for lat in range(LATS):
            points[:, lat * LONS : (lat + 1) * LONS] = blocks[
                :, lat * CHANS : (lat + 1) * CHANS, :
            ].reshape(FULL, LONS)

    w_in, bias = [], []
    for part in range(w_ref.shape[0]):
        block = w_ref[part]
        column = bias_ref[pl.ds(step * w_ref.shape[0] + part, 1), :]
        bias.append(jnp.broadcast_to(column, (LANES, LANES)).T)
        w_in.append(
            jnp.concatenate([block[LANES * tile : LANES * (tile + 1)] for tile in range(4)], axis=1)
        )
        at = pl.ds(pl.multiple_of((step * w_ref.shape[0] + part) * LANES, LANES), LANES)
        w_out[:, at] = block[FULL:]
    w_in = jnp.concatenate(w_in, axis=0)
    bias = jnp.concatenate([jnp.concatenate(bias, axis=0)] * (LONS // LANES), axis=1)
    at = pl.ds(pl.multiple_of(step * rows, rows), rows)
    for lat in range(LATS):
        cols = slice(lat * LONS, (lat + 1) * LONS)
        pre = jnp.dot(w_in, points[:, cols], preferred_element_type=F32) + bias
        act[at, cols] = gelu(pre).astype(BF16)

    @pl.when(step == pl.num_programs(0) - 1)
    def _():
        for lat in range(LATS):
            cols = slice(lat * LONS, (lat + 1) * LONS)
            branch = jnp.dot(w_out[...], act[:, cols], preferred_element_type=F32)
            out = (points[:, cols].astype(F32) + branch).astype(BF16)
            for member in range(MEMBERS):
                to = member * BLOCK + lat * CHANS
                o_ref[to : to + CHANS, :] = out[member * CHANS : (member + 1) * CHANS, :]


def mlp(received, weights, bias):
    blocks = weights.shape[0]
    take = 8
    same2 = lambda step: (0, 0)
    return pl.pallas_call(
        mlp_kernel,
        grid=(blocks // take,),
        out_shape=jax.ShapeDtypeStruct((MEMBERS * BLOCK, LONS), BF16),
        in_specs=[
            pl.BlockSpec((MEMBERS * BLOCK, LONS), same2),
            pl.BlockSpec((take, 2 * FULL, LANES), lambda step: (step, 0, 0)),
            pl.BlockSpec((blocks, LANES), same2),
        ],
        out_specs=pl.BlockSpec((MEMBERS * BLOCK, LONS), same2),
        scratch_shapes=[
            pltpu.VMEM((FULL, POINTS), BF16),
            pltpu.VMEM((HID, POINTS), BF16),
            pltpu.VMEM((FULL, HID), BF16),
        ],
        compiler_params=params(),
        name="pointwise_mlp",
    )(received, weights, bias)


def home_kernel(r_ref, o_ref):
    for member in range(MEMBERS):
        lat, part = member // 4, member % 4
        o_ref[lat * BLOCK : (lat + 1) * BLOCK, part * LONS : (part + 1) * LONS] = r_ref[
            member * BLOCK : (member + 1) * BLOCK, :
        ]


def home(received):
    return pl.pallas_call(
        home_kernel,
        out_shape=jax.ShapeDtypeStruct((ROWS, NLON), BF16),
        in_specs=[whole()],
        out_specs=whole(),
        compiler_params=params(),
        name="home_layout",
    )(received)


SENT = 32


def gather_first(proj_in, proj_out):
    column = [[xy * 32 + place for place in range(32)] for xy in range(16)]
    both = jnp.concatenate([proj_in, proj_out], axis=0)
    both = jnp.pad(both, ((0, SENT - both.shape[0]), (0, 0)))
    return lax.all_gather(both, ("spatial", "field"), axis=0, axis_index_groups=column, tiled=True)


def gather_second(column):
    split = column.reshape(32, SENT // 4, HID // FULL, FULL)
    w_in = split[:, 0].reshape(LANES, 4, LANES).transpose(1, 0, 2).reshape(FULL, LANES)
    w_out = split[:, 1].reshape(LANES, FULL).T
    block = jnp.concatenate([w_in, w_out], axis=0)
    planes = [[xy * 2 + high for xy in range(16)] for high in range(2)]
    whole_weights = lax.all_gather(block, "spatial", axis=0, axis_index_groups=planes, tiled=True)
    return whole_weights.reshape(16, 2 * FULL, LANES)


def shards(field_in, spectral_weight, proj_in, bias_in, proj_out):
    column = gather_first(proj_in, proj_out)
    bias = bias_in.reshape(16, 16, 2, 4).transpose(1, 2, 0, 3).reshape(16, LANES)
    rows = field_in.transpose(1, 0, 2).reshape(ROWS, NLON)
    spectrum, table = forward(rows)
    first = (lax.axis_index("spatial") * ORDERS).astype(jnp.int32).reshape(1)
    polar, bias = legendre(first, bias)

    def swap(blocks):
        return lax.all_to_all(blocks, "spatial", split_axis=0, concat_axis=0, tiled=True)

    def filtered(step, held):
        synth = spectral_filter(swap(held).reshape(PARTS, ROWS), polar, spectral_weight)
        return swap(synth.reshape(BANDS, 2 * ORDERS, ROWS))

    steps = 1 + (lax.axis_index("field") >> 8)
    returned = lax.fori_loop(0, steps, filtered, spectrum.reshape(BANDS, 2 * ORDERS, ROWS))
    returned, column = lax.optimization_barrier((returned, column))
    weights = gather_second(column)
    mixed = inverse(returned.reshape(PARTS, ROWS), table, rows)
    points = lax.all_to_all(
        mixed.reshape(MEMBERS, BLOCK, LONS), "field", split_axis=0, concat_axis=0, tiled=True
    )
    result = mlp(points.reshape(MEMBERS * BLOCK, LONS), weights, bias)
    homed = lax.all_to_all(
        result.reshape(MEMBERS, BLOCK, LONS), "field", split_axis=0, concat_axis=0, tiled=True
    )
    return home(homed.reshape(MEMBERS * BLOCK, LONS)).reshape(BAND, CHANS, NLON).transpose(1, 0, 2)


def solution(mesh):
    in_specs = (
        P("field", "spatial", None),
        P(None, "field", None),
        P(("field", "spatial"), None),
        P(),
        P(("field", "spatial"), None),
    )
    out_specs = P("field", "spatial", None)
    return jax.shard_map(shards, mesh=mesh, in_specs=in_specs, out_specs=out_specs, check_vma=False)
```

```python
import functools
import math

import jax
import jax.numpy as jnp
from jax import lax
from jax.experimental import pallas as pl
from jax.experimental.pallas import tpu as pltpu
from jax.sharding import PartitionSpec as P

F32 = jnp.float32
BF16 = jnp.bfloat16

CHANS = 32
BAND = 12
BANDS = 32
ORDERS = 12
NLAT = 384
NLON = 1024
LMAX = 384
HID = 2048
FULL = 512
MEMBERS = 16
ROWS = CHANS * BAND
PARTS = 2 * BANDS * ORDERS
POINTS = 768
LONS = 256
LATS = 3
BLOCK = LATS * CHANS
LANES = 128
PAIRS = 3
PAD = 16
VMEM = 56 * 1024 * 1024


def params():
    return pltpu.CompilerParams(vmem_limit_bytes=VMEM)


def lanes(tile):
    return slice(tile * LANES, (tile + 1) * LANES)


def whole():
    return pl.BlockSpec(memory_space=pltpu.VMEM)


def forward_kernel(x_ref, y_ref, t_ref):
    unit = 2.0 * math.pi / NLON
    place = lax.broadcasted_iota(jnp.int32, (PAD, NLON), 1)
    row = lax.broadcasted_iota(jnp.int32, (PAD, NLON), 0)
    angle = unit * (((row >> 1) * place + (row & 1) * (NLON // 4)) & (NLON - 1)).astype(F32)
    turn = unit * ((place[:8] * 8) & (NLON - 1)).astype(F32)
    turn_cos = jnp.concatenate([jnp.cos(turn)] * 2, axis=0)
    turn_sin = jnp.concatenate([jnp.sin(turn)] * 2, axis=0)

    def turned(step, carry):
        cos, sin = carry
        t_ref[pl.ds(pl.multiple_of(step * PAD, PAD), PAD), :] = cos.astype(BF16)
        return (cos * turn_cos - sin * turn_sin, sin * turn_cos + cos * turn_sin)

    lax.fori_loop(0, PARTS // PAD, turned, (jnp.cos(angle), jnp.sin(angle)))

    def transform(step, carry):
        at = pl.ds(pl.multiple_of(step * 128, 128), 128)
        y = lax.dot_general(
            t_ref[at, :], x_ref[...], (((1,), (1,)), ((), ())), preferred_element_type=F32
        )
        y_ref[at, :] = (y * (1.0 / NLON)).astype(BF16)
        return carry

    lax.fori_loop(0, PARTS // 128, transform, 0)


def forward(x):
    return pl.pallas_call(
        forward_kernel,
        out_shape=(
            jax.ShapeDtypeStruct((PARTS, ROWS), BF16),
            jax.ShapeDtypeStruct((PARTS, NLON), BF16),
        ),
        in_specs=[whole()],
        out_specs=(whole(), whole()),
        compiler_params=params(),
        name="forward_fourier",
    )(x)


def theta_of(lane):
    lat = (lane & (BANDS - 1)) * BAND + (lane >> 5)
    return (lat.astype(F32) + 0.5) * (math.pi / NLAT)


def legendre_kernel(first_ref, bias_ref, table_ref, laid_ref, work_ref):
    laid_ref[...] = bias_ref[...]
    first = first_ref[0]
    lane = lax.broadcasted_iota(jnp.int32, (PAD, NLAT), 1)
    theta = theta_of(lane)
    cosine = jnp.cos(theta)
    sine = jnp.sin(theta)
    order = first + lax.broadcasted_iota(jnp.int32, (PAD, NLAT), 0)
    order = jnp.minimum(order, LMAX - 1)
    level0 = order.astype(F32)
    step0 = (lane + 1).astype(F32)
    factor = jnp.where(lane < order, jnp.log2((2.0 * step0 - 1.0) / (2.0 * step0)), 0.0)
    log_start = 0.5 * (jnp.log2(level0 + 0.5) + jnp.sum(factor, axis=1, keepdims=True))
    log_start = log_start + level0 * jnp.log2(sine)
    whole_part = jnp.floor(log_start)
    start = jnp.exp2(log_start - whole_part)
    narrow = level0[:, :128]
    square = narrow * narrow

    def eight(group, carry):
        current, previous, power = carry
        half = jnp.exp2(0.5 * power)
        for inner in range(8):
            degree = group * 8 + inner
            level = degree.astype(F32)
            inverse = lax.rsqrt(jnp.maximum(level * level - square, 1.0))
            alpha = inverse * jnp.sqrt(
                jnp.maximum(jnp.full_like(square, 4.0) * (level * level) - 1.0, 0.0)
            )
            ratio = jnp.full_like(square, 1.0) * (2.0 * level + 1.0)
            ratio = ratio / jnp.maximum(jnp.full_like(square, 1.0) * (2.0 * level - 3.0), 1.0)
            below = level - 1.0
            beta = inverse * jnp.sqrt(jnp.maximum(ratio * (below * below - square), 0.0))
            alpha = jnp.concatenate([alpha] * 3, axis=1)
            beta = jnp.concatenate([beta] * 3, axis=1)
            stepped = (alpha * cosine) * current - beta * previous
            fresh = order == degree
            previous = jnp.where(fresh, 0.0, current)
            current = jnp.where(fresh, start, stepped)
            at = pl.ds(pl.multiple_of(degree * PAD, PAD), PAD)
            value = (current * half) * half
            for tile in range(3):
                work_ref[tile, at, :] = value[:, lanes(tile)]
        size = jnp.abs(current) + jnp.abs(previous)
        live = size > 0.0
        shift = jnp.where(live, jnp.floor(jnp.log2(jnp.where(live, size, 1.0))), 0.0)
        scale = jnp.exp2(-shift)
        return (current * scale, previous * scale, power + shift)

    nought = jnp.zeros((PAD, NLAT), F32)
    lax.fori_loop(0, LMAX // 8, eight, (nought, nought, whole_part))

    def store(item, carry):
        for tile in range(3):
            table_ref[item, :, lanes(tile)] = work_ref[
                tile, pl.ds(item, LMAX, stride=PAD), :
            ].astype(BF16)
        return carry

    lax.fori_loop(0, ORDERS, store, 0)


def legendre(first, bias):
    return pl.pallas_call(
        legendre_kernel,
        out_shape=(
            jax.ShapeDtypeStruct((ORDERS, LMAX, NLAT), BF16),
            jax.ShapeDtypeStruct(bias.shape, F32),
        ),
        in_specs=[pl.BlockSpec(memory_space=pltpu.SMEM), whole()],
        out_specs=(whole(), whole()),
        scratch_shapes=[pltpu.VMEM((3, LMAX * PAD, LANES), F32)],
        compiler_params=params(),
        cost_estimate=pl.CostEstimate(
            flops=100_000_000, bytes_accessed=20_000_000, transcendentals=1_000_000
        ),
        name="legendre_table",
    )(first, bias)


def filter_kernel(r_ref, p_ref, w_ref, s_ref, rin, sout, quad):
    step = pl.program_id(0)
    group = 4 * CHANS

    @pl.when(step == 0)
    def _():
        for tile in range(3):
            rin[tile] = r_ref[:, lanes(tile)].astype(F32)
        lane = lax.broadcasted_iota(jnp.int32, (8, NLAT), 1)
        quad[...] = jnp.sin(theta_of(lane)) * (math.pi / NLAT)

    lane32 = lax.broadcasted_iota(jnp.int32, (BANDS, group), 1) >> 5

    def exchanged(blocks):
        out = []
        for to in range(4):
            block = blocks[to]
            for at in range(4):
                if at != to:
                    moved = pltpu.roll(blocks[at], (at - to) % 4 * CHANS, 1)
                    block = jnp.where(lane32 == at, moved, block)
            out.append(block)
        return out

    for part_pair in range(PAIRS):
        row = 4 * (step * PAIRS + part_pair)
        tiles = []
        for tile in range(3):
            parts = [
                rin[tile, pl.ds(row + part, BANDS, stride=2 * ORDERS), :] for part in range(4)
            ]
            tiles.append(jnp.concatenate(exchanged(parts), axis=0).T)
        data = jnp.concatenate(tiles, axis=1)
        data = (data * quad[:1, :]).astype(BF16)

        out = []
        for item in range(2):
            table = p_ref[2 * part_pair + item]
            coef = lax.dot_general(
                data[2 * CHANS * item : 2 * CHANS * (item + 1), :],
                table,
                (((1,), (1,)), ((), ())),
                preferred_element_type=F32,
            )
            real, imag = coef[:CHANS], coef[CHANS:]
            filtered = jnp.concatenate(
                [w_ref[0] * real - w_ref[1] * imag, w_ref[0] * imag + w_ref[1] * real], axis=0
            ).astype(BF16)
            out.append(jnp.dot(filtered, table, preferred_element_type=F32))
        synth = jnp.concatenate(out, axis=0)
        for tile in range(3):
            turned = synth[:, lanes(tile)].T
            blocks = exchanged([turned[BANDS * lat : BANDS * (lat + 1), :] for lat in range(4)])
            for part in range(4):
                sout[tile, pl.ds(row + part, BANDS, stride=2 * ORDERS), :] = blocks[part]

    @pl.when(step == pl.num_programs(0) - 1)
    def _():
        for tile in range(3):
            s_ref[:, lanes(tile)] = sout[tile].astype(BF16)


def spectral_filter(received, table, weights):
    same2 = lambda pair: (0, 0)
    return pl.pallas_call(
        filter_kernel,
        grid=(ORDERS // 2 // PAIRS,),
        out_shape=jax.ShapeDtypeStruct((PARTS, ROWS), BF16),
        in_specs=[
            pl.BlockSpec((PARTS, ROWS), same2),
            pl.BlockSpec((2 * PAIRS, LMAX, NLAT), lambda pair: (pair, 0, 0)),
            pl.BlockSpec((2, CHANS, LMAX), lambda pair: (0, 0, 0)),
        ],
        out_specs=pl.BlockSpec((PARTS, ROWS), same2),
        scratch_shapes=[
            pltpu.VMEM((3, PARTS, LANES), F32),
            pltpu.VMEM((3, PARTS, LANES), F32),
            pltpu.VMEM((8, NLAT), F32),
        ],
        compiler_params=params(),
        name="spectral_filter",
    )(received, table, weights)


def inverse_kernel(r_ref, t_ref, xr_ref, m_ref, spectra):
    row = lax.broadcasted_iota(jnp.int32, (PARTS, ROWS), 0)
    gained = jnp.where(row < 2, 1.0, 2.0) * r_ref[...].astype(F32)
    spectra[...] = gained.T.astype(BF16)

    def rows_of(step, carry):
        at = pl.ds(pl.multiple_of(step * BLOCK, BLOCK), BLOCK)
        smooth = jnp.dot(spectra[at, :], t_ref[...], preferred_element_type=F32)
        mixed = (xr_ref[at, :].astype(F32) + smooth).astype(BF16)
        for part in range(NLON // LONS):
            to = pl.ds(pl.multiple_of((step * 4 + part) * BLOCK, BLOCK), BLOCK)
            m_ref[to, :] = mixed[:, part * LONS : (part + 1) * LONS]
        return carry

    lax.fori_loop(0, BAND // LATS, rows_of, 0)


def inverse(returned, table, rows):
    return pl.pallas_call(
        inverse_kernel,
        out_shape=jax.ShapeDtypeStruct((MEMBERS * BLOCK, LONS), BF16),
        in_specs=[whole()] * 3,
        out_specs=whole(),
        scratch_shapes=[pltpu.VMEM((ROWS, PARTS), BF16)],
        compiler_params=params(),
        name="inverse_fourier",
    )(returned, table, rows)


def gelu(x):
    root = math.sqrt(2.0 / math.pi)
    half = 0.5 * x
    return half + half * jnp.tanh(x * (root + (root * 0.044715) * (x * x)))


def mlp_kernel(r_ref, w_ref, bias_ref, o_ref, points, act, w_out):
    step = pl.program_id(0)
    rows = w_ref.shape[0] * LANES

    @pl.when(step == 0)
    def _():
        blocks = r_ref[...].reshape(MEMBERS, BLOCK, LONS)
        for lat in range(LATS):
            points[:, lat * LONS : (lat + 1) * LONS] = blocks[
                :, lat * CHANS : (lat + 1) * CHANS, :
            ].reshape(FULL, LONS)

    w_in, bias = [], []
    for part in range(w_ref.shape[0]):
        block = w_ref[part]
        column = bias_ref[pl.ds(step * w_ref.shape[0] + part, 1), :]
        bias.append(jnp.broadcast_to(column, (LANES, LANES)).T)
        w_in.append(
            jnp.concatenate([block[LANES * tile : LANES * (tile + 1)] for tile in range(4)], axis=1)
        )
        at = pl.ds(pl.multiple_of((step * w_ref.shape[0] + part) * LANES, LANES), LANES)
        w_out[:, at] = block[FULL:]
    w_in = jnp.concatenate(w_in, axis=0)
    bias = jnp.concatenate([jnp.concatenate(bias, axis=0)] * (LONS // LANES), axis=1)
    at = pl.ds(pl.multiple_of(step * rows, rows), rows)
    for lat in range(LATS):
        cols = slice(lat * LONS, (lat + 1) * LONS)
        pre = jnp.dot(w_in, points[:, cols], preferred_element_type=F32) + bias
        act[at, cols] = gelu(pre).astype(BF16)

    @pl.when(step == pl.num_programs(0) - 1)
    def _():
        for lat in range(LATS):
            cols = slice(lat * LONS, (lat + 1) * LONS)
            branch = jnp.dot(w_out[...], act[:, cols], preferred_element_type=F32)
            out = (points[:, cols].astype(F32) + branch).astype(BF16)
            for member in range(MEMBERS):
                to = member * BLOCK + lat * CHANS
                o_ref[to : to + CHANS, :] = out[member * CHANS : (member + 1) * CHANS, :]


def mlp(received, weights, bias):
    blocks = weights.shape[0]
    take = 8
    same2 = lambda step: (0, 0)
    return pl.pallas_call(
        mlp_kernel,
        grid=(blocks // take,),
        out_shape=jax.ShapeDtypeStruct((MEMBERS * BLOCK, LONS), BF16),
        in_specs=[
            pl.BlockSpec((MEMBERS * BLOCK, LONS), same2),
            pl.BlockSpec((take, 2 * FULL, LANES), lambda step: (step, 0, 0)),
            pl.BlockSpec((blocks, LANES), same2),
        ],
        out_specs=pl.BlockSpec((MEMBERS * BLOCK, LONS), same2),
        scratch_shapes=[
            pltpu.VMEM((FULL, POINTS), BF16),
            pltpu.VMEM((HID, POINTS), BF16),
            pltpu.VMEM((FULL, HID), BF16),
        ],
        compiler_params=params(),
        name="pointwise_mlp",
    )(received, weights, bias)


def home_kernel(r_ref, o_ref):
    for member in range(MEMBERS):
        lat, part = member // 4, member % 4
        o_ref[lat * BLOCK : (lat + 1) * BLOCK, part * LONS : (part + 1) * LONS] = r_ref[
            member * BLOCK : (member + 1) * BLOCK, :
        ]


def home(received):
    return pl.pallas_call(
        home_kernel,
        out_shape=jax.ShapeDtypeStruct((ROWS, NLON), BF16),
        in_specs=[whole()],
        out_specs=whole(),
        compiler_params=params(),
        name="home_layout",
    )(received)


RINGS = (
    [x * 4 + (y if x % 2 == 0 else 3 - y) for x in range(4) for y in range(4)],
    [(x if y % 2 == 0 else 3 - x) * 4 + y for y in range(4) for x in range(4)],
)
SENT = 32


def gather_first(proj_in, proj_out):
    column = [[xy * 32 + place for place in range(32)] for xy in range(16)]
    both = jnp.concatenate([proj_in, proj_out], axis=0)
    both = jnp.pad(both, ((0, SENT - both.shape[0]), (0, 0)))
    return lax.all_gather(both, ("spatial", "field"), axis=0, axis_index_groups=column, tiled=True)


def gather_second(column):
    split = column.reshape(32, SENT // 4, HID // FULL, FULL)
    w_in = split[:, 0].reshape(LANES, 4, LANES).transpose(1, 0, 2).reshape(FULL, LANES)
    w_out = split[:, 1].reshape(LANES, FULL).T
    block = jnp.concatenate([w_in, w_out], axis=0)
    planes = [
        [(xy * 2 + high) * 16 + low * 2 + core for xy in RINGS[core]]
        for high in range(2)
        for low in range(8)
        for core in range(2)
    ]
    whole_weights = lax.all_gather(
        block, ("spatial", "field"), axis=0, axis_index_groups=planes, tiled=True
    )
    return whole_weights.reshape(16, 2 * FULL, LANES)


def shards(field_in, spectral_weight, proj_in, bias_in, proj_out):
    column = gather_first(proj_in, proj_out)
    bias = bias_in.reshape(16, 16, 2, 4).transpose(1, 2, 0, 3).reshape(16, LANES)
    turns = [jnp.concatenate([bias[xy : xy + 1] for xy in ring]) for ring in RINGS]
    bias = jnp.where((lax.axis_index("field") & 1) == 0, turns[0], turns[1])
    rows = field_in.transpose(1, 0, 2).reshape(ROWS, NLON)
    spectrum, table = forward(rows)
    first = (lax.axis_index("spatial") * ORDERS).astype(jnp.int32).reshape(1)

    def swap(blocks):
        return lax.all_to_all(blocks, "spatial", split_axis=0, concat_axis=0, tiled=True)

    def filtered(step, carry):
        held, laid = carry
        polar, laid = legendre(first, laid)
        synth = spectral_filter(swap(held).reshape(PARTS, ROWS), polar, spectral_weight)
        return swap(synth.reshape(BANDS, 2 * ORDERS, ROWS)), laid

    steps = 1 + (lax.axis_index("field") >> 8)
    returned, bias = lax.fori_loop(
        0, steps, filtered, (spectrum.reshape(BANDS, 2 * ORDERS, ROWS), bias)
    )
    returned, column = lax.optimization_barrier((returned, column))
    weights = gather_second(column)
    mixed = inverse(returned.reshape(PARTS, ROWS), table, rows)
    points = lax.all_to_all(
        mixed.reshape(MEMBERS, BLOCK, LONS), "field", split_axis=0, concat_axis=0, tiled=True
    )
    result = mlp(points.reshape(MEMBERS * BLOCK, LONS), weights, bias)
    homed = lax.all_to_all(
        result.reshape(MEMBERS, BLOCK, LONS), "field", split_axis=0, concat_axis=0, tiled=True
    )
    return home(homed.reshape(MEMBERS * BLOCK, LONS)).reshape(BAND, CHANS, NLON).transpose(1, 0, 2)


def solution(mesh):
    in_specs = (
        P("field", "spatial", None),
        P(None, "field", None),
        P(("field", "spatial"), None),
        P(),
        P(("field", "spatial"), None),
    )
    out_specs = P("field", "spatial", None)
    return jax.shard_map(shards, mesh=mesh, in_specs=in_specs, out_specs=out_specs, check_vma=False)
```

```python
import functools
import math

import jax
import jax.numpy as jnp
from jax import lax
from jax.experimental import pallas as pl
from jax.experimental.pallas import tpu as pltpu
from jax.sharding import PartitionSpec as P

F32 = jnp.float32
BF16 = jnp.bfloat16

CHANS = 32
BAND = 12
BANDS = 32
ORDERS = 12
NLAT = 384
NLON = 1024
LMAX = 384
HID = 2048
FULL = 512
MEMBERS = 16
ROWS = CHANS * BAND
PARTS = 2 * BANDS * ORDERS
POINTS = 768
LONS = 256
LATS = 3
BLOCK = LATS * CHANS
LANES = 128
PAIRS = 3
PAD = 16
VMEM = 56 * 1024 * 1024


def params():
    return pltpu.CompilerParams(vmem_limit_bytes=VMEM)


def lanes(tile):
    return slice(tile * LANES, (tile + 1) * LANES)


def whole():
    return pl.BlockSpec(memory_space=pltpu.VMEM)


def forward_kernel(x_ref, y_ref, t_ref):
    unit = 2.0 * math.pi / NLON
    place = lax.broadcasted_iota(jnp.int32, (PAD, NLON), 1)
    row = lax.broadcasted_iota(jnp.int32, (PAD, NLON), 0)
    angle = unit * (((row >> 1) * place + (row & 1) * (NLON // 4)) & (NLON - 1)).astype(F32)
    turn = unit * ((place[:8] * 8) & (NLON - 1)).astype(F32)
    turn_cos = jnp.concatenate([jnp.cos(turn)] * 2, axis=0)
    turn_sin = jnp.concatenate([jnp.sin(turn)] * 2, axis=0)

    def turned(step, carry):
        cos, sin = carry
        t_ref[pl.ds(pl.multiple_of(step * PAD, PAD), PAD), :] = cos.astype(BF16)
        return (cos * turn_cos - sin * turn_sin, sin * turn_cos + cos * turn_sin)

    lax.fori_loop(0, PARTS // PAD, turned, (jnp.cos(angle), jnp.sin(angle)))

    def transform(step, carry):
        at = pl.ds(pl.multiple_of(step * 128, 128), 128)
        y = lax.dot_general(
            t_ref[at, :], x_ref[...], (((1,), (1,)), ((), ())), preferred_element_type=F32
        )
        y_ref[at, :] = (y * (1.0 / NLON)).astype(BF16)
        return carry

    lax.fori_loop(0, PARTS // 128, transform, 0)


def forward(x):
    return pl.pallas_call(
        forward_kernel,
        out_shape=(
            jax.ShapeDtypeStruct((PARTS, ROWS), BF16),
            jax.ShapeDtypeStruct((PARTS, NLON), BF16),
        ),
        in_specs=[whole()],
        out_specs=(whole(), whole()),
        compiler_params=params(),
        name="forward_fourier",
    )(x)


def theta_of(lane):
    lat = (lane & (BANDS - 1)) * BAND + (lane >> 5)
    return (lat.astype(F32) + 0.5) * (math.pi / NLAT)


def legendre_kernel(first_ref, bias_ref, table_ref, laid_ref, work_ref):
    laid_ref[...] = bias_ref[...]
    first = first_ref[0]
    lane = lax.broadcasted_iota(jnp.int32, (PAD, NLAT), 1)
    theta = theta_of(lane)
    cosine = jnp.cos(theta)
    sine = jnp.sin(theta)
    order = first + lax.broadcasted_iota(jnp.int32, (PAD, NLAT), 0)
    order = jnp.minimum(order, LMAX - 1)
    level0 = order.astype(F32)
    step0 = (lane + 1).astype(F32)
    factor = jnp.where(lane < order, jnp.log2((2.0 * step0 - 1.0) / (2.0 * step0)), 0.0)
    log_start = 0.5 * (jnp.log2(level0 + 0.5) + jnp.sum(factor, axis=1, keepdims=True))
    log_start = log_start + level0 * jnp.log2(sine)
    whole_part = jnp.floor(log_start)
    start = jnp.exp2(log_start - whole_part)
    narrow = level0[:, :128]
    square = narrow * narrow

    def eight(group, carry):
        current, previous, power = carry
        half = jnp.exp2(0.5 * power)
        for inner in range(8):
            degree = group * 8 + inner
            level = degree.astype(F32)
            inverse = lax.rsqrt(jnp.maximum(level * level - square, 1.0))
            alpha = inverse * jnp.sqrt(
                jnp.maximum(jnp.full_like(square, 4.0) * (level * level) - 1.0, 0.0)
            )
            ratio = jnp.full_like(square, 1.0) * (2.0 * level + 1.0)
            ratio = ratio / jnp.maximum(jnp.full_like(square, 1.0) * (2.0 * level - 3.0), 1.0)
            below = level - 1.0
            beta = inverse * jnp.sqrt(jnp.maximum(ratio * (below * below - square), 0.0))
            alpha = jnp.concatenate([alpha] * 3, axis=1)
            beta = jnp.concatenate([beta] * 3, axis=1)
            stepped = (alpha * cosine) * current - beta * previous
            fresh = order == degree
            previous = jnp.where(fresh, 0.0, current)
            current = jnp.where(fresh, start, stepped)
            at = pl.ds(pl.multiple_of(degree * PAD, PAD), PAD)
            value = (current * half) * half
            for tile in range(3):
                work_ref[tile, at, :] = value[:, lanes(tile)]
        size = jnp.abs(current) + jnp.abs(previous)
        live = size > 0.0
        shift = jnp.where(live, jnp.floor(jnp.log2(jnp.where(live, size, 1.0))), 0.0)
        scale = jnp.exp2(-shift)
        return (current * scale, previous * scale, power + shift)

    nought = jnp.zeros((PAD, NLAT), F32)
    lax.fori_loop(0, LMAX // 8, eight, (nought, nought, whole_part))

    def store(item, carry):
        for tile in range(3):
            table_ref[item, :, lanes(tile)] = work_ref[
                tile, pl.ds(item, LMAX, stride=PAD), :
            ].astype(BF16)
        return carry

    lax.fori_loop(0, ORDERS, store, 0)


def legendre(first, bias):
    return pl.pallas_call(
        legendre_kernel,
        out_shape=(
            jax.ShapeDtypeStruct((ORDERS, LMAX, NLAT), BF16),
            jax.ShapeDtypeStruct(bias.shape, F32),
        ),
        in_specs=[pl.BlockSpec(memory_space=pltpu.SMEM), whole()],
        out_specs=(whole(), whole()),
        scratch_shapes=[pltpu.VMEM((3, LMAX * PAD, LANES), F32)],
        compiler_params=params(),
        cost_estimate=pl.CostEstimate(
            flops=100_000_000, bytes_accessed=20_000_000, transcendentals=1_000_000
        ),
        name="legendre_table",
    )(first, bias)


def filter_kernel(r_ref, p_ref, w_ref, s_ref, rin, sout, quad):
    step = pl.program_id(0)
    group = 4 * CHANS

    @pl.when(step == 0)
    def _():
        for tile in range(3):
            rin[tile] = r_ref[:, lanes(tile)].astype(F32)
        lane = lax.broadcasted_iota(jnp.int32, (8, NLAT), 1)
        quad[...] = jnp.sin(theta_of(lane)) * (math.pi / NLAT)

    lane32 = lax.broadcasted_iota(jnp.int32, (BANDS, group), 1) >> 5

    def exchanged(blocks):
        out = []
        for to in range(4):
            block = blocks[to]
            for at in range(4):
                if at != to:
                    moved = pltpu.roll(blocks[at], (at - to) % 4 * CHANS, 1)
                    block = jnp.where(lane32 == at, moved, block)
            out.append(block)
        return out

    for part_pair in range(PAIRS):
        row = 4 * (step * PAIRS + part_pair)
        tiles = []
        for tile in range(3):
            parts = [
                rin[tile, pl.ds(row + part, BANDS, stride=2 * ORDERS), :] for part in range(4)
            ]
            tiles.append(jnp.concatenate(exchanged(parts), axis=0).T)
        data = jnp.concatenate(tiles, axis=1)
        data = (data * quad[:1, :]).astype(BF16)

        out = []
        for item in range(2):
            table = p_ref[2 * part_pair + item]
            coef = lax.dot_general(
                data[2 * CHANS * item : 2 * CHANS * (item + 1), :],
                table,
                (((1,), (1,)), ((), ())),
                preferred_element_type=F32,
            )
            real, imag = coef[:CHANS], coef[CHANS:]
            filtered = jnp.concatenate(
                [w_ref[0] * real - w_ref[1] * imag, w_ref[0] * imag + w_ref[1] * real], axis=0
            ).astype(BF16)
            out.append(jnp.dot(filtered, table, preferred_element_type=F32))
        synth = jnp.concatenate(out, axis=0)
        for tile in range(3):
            turned = synth[:, lanes(tile)].T
            blocks = exchanged([turned[BANDS * lat : BANDS * (lat + 1), :] for lat in range(4)])
            for part in range(4):
                sout[tile, pl.ds(row + part, BANDS, stride=2 * ORDERS), :] = blocks[part]

    @pl.when(step == pl.num_programs(0) - 1)
    def _():
        for tile in range(3):
            s_ref[:, lanes(tile)] = sout[tile].astype(BF16)


def spectral_filter(received, table, weights):
    same2 = lambda pair: (0, 0)
    return pl.pallas_call(
        filter_kernel,
        grid=(ORDERS // 2 // PAIRS,),
        out_shape=jax.ShapeDtypeStruct((PARTS, ROWS), BF16),
        in_specs=[
            pl.BlockSpec((PARTS, ROWS), same2),
            pl.BlockSpec((2 * PAIRS, LMAX, NLAT), lambda pair: (pair, 0, 0)),
            pl.BlockSpec((2, CHANS, LMAX), lambda pair: (0, 0, 0)),
        ],
        out_specs=pl.BlockSpec((PARTS, ROWS), same2),
        scratch_shapes=[
            pltpu.VMEM((3, PARTS, LANES), F32),
            pltpu.VMEM((3, PARTS, LANES), F32),
            pltpu.VMEM((8, NLAT), F32),
        ],
        compiler_params=params(),
        name="spectral_filter",
    )(received, table, weights)


def inverse_kernel(r_ref, t_ref, xr_ref, m_ref, spectra):
    row = lax.broadcasted_iota(jnp.int32, (PARTS, ROWS), 0)
    gained = jnp.where(row < 2, 1.0, 2.0) * r_ref[...].astype(F32)
    spectra[...] = gained.T.astype(BF16)

    def rows_of(step, carry):
        at = pl.ds(pl.multiple_of(step * BLOCK, BLOCK), BLOCK)
        smooth = jnp.dot(spectra[at, :], t_ref[...], preferred_element_type=F32)
        mixed = (xr_ref[at, :].astype(F32) + smooth).astype(BF16)
        for part in range(NLON // LONS):
            to = pl.ds(pl.multiple_of((step * 4 + part) * BLOCK, BLOCK), BLOCK)
            m_ref[to, :] = mixed[:, part * LONS : (part + 1) * LONS]
        return carry

    lax.fori_loop(0, BAND // LATS, rows_of, 0)


def inverse(returned, table, rows):
    return pl.pallas_call(
        inverse_kernel,
        out_shape=jax.ShapeDtypeStruct((MEMBERS * BLOCK, LONS), BF16),
        in_specs=[whole()] * 3,
        out_specs=whole(),
        scratch_shapes=[pltpu.VMEM((ROWS, PARTS), BF16)],
        compiler_params=params(),
        name="inverse_fourier",
    )(returned, table, rows)


def gelu(x):
    root = math.sqrt(2.0 / math.pi)
    half = 0.5 * x
    return half + half * jnp.tanh(x * (root + (root * 0.044715) * (x * x)))


def mlp_kernel(r_ref, w_ref, bias_ref, o_ref, points, act, w_out):
    step = pl.program_id(0)
    rows = w_ref.shape[0] * LANES

    @pl.when(step == 0)
    def _():
        blocks = r_ref[...].reshape(MEMBERS, BLOCK, LONS)
        for lat in range(LATS):
            points[:, lat * LONS : (lat + 1) * LONS] = blocks[
                :, lat * CHANS : (lat + 1) * CHANS, :
            ].reshape(FULL, LONS)

    w_in, bias = [], []
    for part in range(w_ref.shape[0]):
        block = w_ref[part]
        column = bias_ref[pl.ds(step * w_ref.shape[0] + part, 1), :]
        bias.append(jnp.broadcast_to(column, (LANES, LANES)).T)
        w_in.append(
            jnp.concatenate([block[LANES * tile : LANES * (tile + 1)] for tile in range(4)], axis=1)
        )
        at = pl.ds(pl.multiple_of((step * w_ref.shape[0] + part) * LANES, LANES), LANES)
        w_out[:, at] = block[FULL:]
    w_in = jnp.concatenate(w_in, axis=0)
    bias = jnp.concatenate([jnp.concatenate(bias, axis=0)] * (LONS // LANES), axis=1)
    at = pl.ds(pl.multiple_of(step * rows, rows), rows)
    for lat in range(LATS):
        cols = slice(lat * LONS, (lat + 1) * LONS)
        pre = jnp.dot(w_in, points[:, cols], preferred_element_type=F32) + bias
        act[at, cols] = gelu(pre).astype(BF16)

    @pl.when(step == pl.num_programs(0) - 1)
    def _():
        for lat in range(LATS):
            cols = slice(lat * LONS, (lat + 1) * LONS)
            branch = jnp.dot(w_out[...], act[:, cols], preferred_element_type=F32)
            out = (points[:, cols].astype(F32) + branch).astype(BF16)
            for member in range(MEMBERS):
                to = member * BLOCK + lat * CHANS
                o_ref[to : to + CHANS, :] = out[member * CHANS : (member + 1) * CHANS, :]


def mlp(received, weights, bias):
    blocks = weights.shape[0]
    take = 8
    same2 = lambda step: (0, 0)
    return pl.pallas_call(
        mlp_kernel,
        grid=(blocks // take,),
        out_shape=jax.ShapeDtypeStruct((MEMBERS * BLOCK, LONS), BF16),
        in_specs=[
            pl.BlockSpec((MEMBERS * BLOCK, LONS), same2),
            pl.BlockSpec((take, 2 * FULL, LANES), lambda step: (step, 0, 0)),
            pl.BlockSpec((blocks, LANES), same2),
        ],
        out_specs=pl.BlockSpec((MEMBERS * BLOCK, LONS), same2),
        scratch_shapes=[
            pltpu.VMEM((FULL, POINTS), BF16),
            pltpu.VMEM((HID, POINTS), BF16),
            pltpu.VMEM((FULL, HID), BF16),
        ],
        compiler_params=params(),
        name="pointwise_mlp",
    )(received, weights, bias)


def home_kernel(r_ref, o_ref):
    for member in range(MEMBERS):
        lat, part = member // 4, member % 4
        o_ref[lat * BLOCK : (lat + 1) * BLOCK, part * LONS : (part + 1) * LONS] = r_ref[
            member * BLOCK : (member + 1) * BLOCK, :
        ]


def home(received):
    return pl.pallas_call(
        home_kernel,
        out_shape=jax.ShapeDtypeStruct((ROWS, NLON), BF16),
        in_specs=[whole()],
        out_specs=whole(),
        compiler_params=params(),
        name="home_layout",
    )(received)


def gather_first(proj_in, proj_out):
    column = [[xy * 32 + place for place in range(32)] for xy in range(16)]
    both = jnp.concatenate([proj_in, proj_out], axis=0)
    return lax.all_to_all(
        jnp.broadcast_to(both[None], (32,) + both.shape),
        ("spatial", "field"),
        split_axis=0,
        concat_axis=0,
        axis_index_groups=column,
        tiled=True,
    )


def gather_second(column):
    split = column.reshape(32, 2, HID // FULL, FULL)
    w_in = split[:, 0].reshape(LANES, 4, LANES).transpose(1, 0, 2).reshape(FULL, LANES)
    w_out = split[:, 1].reshape(LANES, FULL).T
    block = jnp.concatenate([w_in, w_out], axis=0)
    planes = [[xy * 2 + high for xy in range(16)] for high in range(2)]
    whole_weights = lax.all_gather(block, "spatial", axis=0, axis_index_groups=planes, tiled=True)
    return whole_weights.reshape(16, 2 * FULL, LANES)


def shards(field_in, spectral_weight, proj_in, bias_in, proj_out):
    column = gather_first(proj_in, proj_out)
    bias = bias_in.reshape(16, 16, 2, 4).transpose(1, 2, 0, 3).reshape(16, LANES)
    rows = field_in.transpose(1, 0, 2).reshape(ROWS, NLON)
    spectrum, table = forward(rows)
    first = (lax.axis_index("spatial") * ORDERS).astype(jnp.int32).reshape(1)
    polar, bias = legendre(first, bias)
    spectrum, column, polar = lax.optimization_barrier((spectrum, column, polar))
    weights = gather_second(column)
    pencil = lax.all_to_all(
        spectrum.reshape(BANDS, 2 * ORDERS, ROWS), "spatial", split_axis=0, concat_axis=0, tiled=True
    )
    synth = spectral_filter(pencil.reshape(PARTS, ROWS), polar, spectral_weight)
    returned = lax.all_to_all(
        synth.reshape(BANDS, 2 * ORDERS, ROWS), "spatial", split_axis=0, concat_axis=0, tiled=True
    )
    mixed = inverse(returned.reshape(PARTS, ROWS), table, rows)
    points = lax.all_to_all(
        mixed.reshape(MEMBERS, BLOCK, LONS), "field", split_axis=0, concat_axis=0, tiled=True
    )
    result = mlp(points.reshape(MEMBERS * BLOCK, LONS), weights, bias)
    homed = lax.all_to_all(
        result.reshape(MEMBERS, BLOCK, LONS), "field", split_axis=0, concat_axis=0, tiled=True
    )
    return home(homed.reshape(MEMBERS * BLOCK, LONS)).reshape(BAND, CHANS, NLON).transpose(1, 0, 2)


def solution(mesh):
    in_specs = (
        P("field", "spatial", None),
        P(None, "field", None),
        P(("field", "spatial"), None),
        P(),
        P(("field", "spatial"), None),
    )
    out_specs = P("field", "spatial", None)
    return jax.shard_map(shards, mesh=mesh, in_specs=in_specs, out_specs=out_specs, check_vma=False)
```

```python
import functools
import math

import jax
import jax.numpy as jnp
from jax import lax
from jax.experimental import pallas as pl
from jax.experimental.pallas import tpu as pltpu
from jax.sharding import PartitionSpec as P

F32 = jnp.float32
BF16 = jnp.bfloat16

CHANS = 32
BAND = 12
BANDS = 32
ORDERS = 12
NLAT = 384
NLON = 1024
LMAX = 384
HID = 2048
FULL = 512
MEMBERS = 16
ROWS = CHANS * BAND
PARTS = 2 * BANDS * ORDERS
POINTS = 768
LONS = 256
LATS = 3
BLOCK = LATS * CHANS
LANES = 128
PAIRS = 3
PAD = 16
VMEM = 56 * 1024 * 1024


def params():
    return pltpu.CompilerParams(vmem_limit_bytes=VMEM)


def lanes(tile):
    return slice(tile * LANES, (tile + 1) * LANES)


def whole():
    return pl.BlockSpec(memory_space=pltpu.VMEM)


def forward_kernel(x_ref, y_ref, t_ref):
    unit = 2.0 * math.pi / NLON
    place = lax.broadcasted_iota(jnp.int32, (PAD, NLON), 1)
    row = lax.broadcasted_iota(jnp.int32, (PAD, NLON), 0)
    angle = unit * (((row >> 1) * place + (row & 1) * (NLON // 4)) & (NLON - 1)).astype(F32)
    turn = unit * ((place[:8] * 8) & (NLON - 1)).astype(F32)
    turn_cos = jnp.concatenate([jnp.cos(turn)] * 2, axis=0)
    turn_sin = jnp.concatenate([jnp.sin(turn)] * 2, axis=0)

    def turned(step, carry):
        cos, sin = carry
        t_ref[pl.ds(pl.multiple_of(step * PAD, PAD), PAD), :] = cos.astype(BF16)
        return (cos * turn_cos - sin * turn_sin, sin * turn_cos + cos * turn_sin)

    lax.fori_loop(0, PARTS // PAD, turned, (jnp.cos(angle), jnp.sin(angle)))

    def transform(step, carry):
        at = pl.ds(pl.multiple_of(step * 128, 128), 128)
        y = lax.dot_general(
            t_ref[at, :], x_ref[...], (((1,), (1,)), ((), ())), preferred_element_type=F32
        )
        y_ref[at, :] = (y * (1.0 / NLON)).astype(BF16)
        return carry

    lax.fori_loop(0, PARTS // 128, transform, 0)


def forward(x):
    return pl.pallas_call(
        forward_kernel,
        out_shape=(
            jax.ShapeDtypeStruct((PARTS, ROWS), BF16),
            jax.ShapeDtypeStruct((PARTS, NLON), BF16),
        ),
        in_specs=[whole()],
        out_specs=(whole(), whole()),
        compiler_params=params(),
        name="forward_fourier",
    )(x)


def theta_of(lane):
    lat = (lane & (BANDS - 1)) * BAND + (lane >> 5)
    return (lat.astype(F32) + 0.5) * (math.pi / NLAT)


def legendre_kernel(first_ref, bias_ref, table_ref, laid_ref, work_ref):
    laid_ref[...] = bias_ref[...]
    first = first_ref[0]
    lane = lax.broadcasted_iota(jnp.int32, (PAD, NLAT), 1)
    theta = theta_of(lane)
    cosine = jnp.cos(theta)
    sine = jnp.sin(theta)
    order = first + lax.broadcasted_iota(jnp.int32, (PAD, NLAT), 0)
    order = jnp.minimum(order, LMAX - 1)
    level0 = order.astype(F32)
    step0 = (lane + 1).astype(F32)
    factor = jnp.where(lane < order, jnp.log2((2.0 * step0 - 1.0) / (2.0 * step0)), 0.0)
    log_start = 0.5 * (jnp.log2(level0 + 0.5) + jnp.sum(factor, axis=1, keepdims=True))
    log_start = log_start + level0 * jnp.log2(sine)
    whole_part = jnp.floor(log_start)
    start = jnp.exp2(log_start - whole_part)
    narrow = level0[:, :128]
    square = narrow * narrow

    def eight(group, carry):
        current, previous, power = carry
        half = jnp.exp2(0.5 * power)
        for inner in range(8):
            degree = group * 8 + inner
            level = degree.astype(F32)
            inverse = lax.rsqrt(jnp.maximum(level * level - square, 1.0))
            alpha = inverse * jnp.sqrt(
                jnp.maximum(jnp.full_like(square, 4.0) * (level * level) - 1.0, 0.0)
            )
            ratio = jnp.full_like(square, 1.0) * (2.0 * level + 1.0)
            ratio = ratio / jnp.maximum(jnp.full_like(square, 1.0) * (2.0 * level - 3.0), 1.0)
            below = level - 1.0
            beta = inverse * jnp.sqrt(jnp.maximum(ratio * (below * below - square), 0.0))
            alpha = jnp.concatenate([alpha] * 3, axis=1)
            beta = jnp.concatenate([beta] * 3, axis=1)
            stepped = (alpha * cosine) * current - beta * previous
            fresh = order == degree
            previous = jnp.where(fresh, 0.0, current)
            current = jnp.where(fresh, start, stepped)
            at = pl.ds(pl.multiple_of(degree * PAD, PAD), PAD)
            value = (current * half) * half
            for tile in range(3):
                work_ref[tile, at, :] = value[:, lanes(tile)]
        size = jnp.abs(current) + jnp.abs(previous)
        live = size > 0.0
        shift = jnp.where(live, jnp.floor(jnp.log2(jnp.where(live, size, 1.0))), 0.0)
        scale = jnp.exp2(-shift)
        return (current * scale, previous * scale, power + shift)

    nought = jnp.zeros((PAD, NLAT), F32)
    lax.fori_loop(0, LMAX // 8, eight, (nought, nought, whole_part))

    def store(item, carry):
        for tile in range(3):
            table_ref[item, :, lanes(tile)] = work_ref[
                tile, pl.ds(item, LMAX, stride=PAD), :
            ].astype(BF16)
        return carry

    lax.fori_loop(0, ORDERS, store, 0)


def legendre(first, bias):
    return pl.pallas_call(
        legendre_kernel,
        out_shape=(
            jax.ShapeDtypeStruct((ORDERS, LMAX, NLAT), BF16),
            jax.ShapeDtypeStruct(bias.shape, F32),
        ),
        in_specs=[pl.BlockSpec(memory_space=pltpu.SMEM), whole()],
        out_specs=(whole(), whole()),
        scratch_shapes=[pltpu.VMEM((3, LMAX * PAD, LANES), F32)],
        compiler_params=params(),
        cost_estimate=pl.CostEstimate(
            flops=100_000_000, bytes_accessed=20_000_000, transcendentals=1_000_000
        ),
        name="legendre_table",
    )(first, bias)


def filter_kernel(r_ref, p_ref, w_ref, s_ref, rin, sout, quad):
    step = pl.program_id(0)
    group = 4 * CHANS

    @pl.when(step == 0)
    def _():
        for tile in range(3):
            rin[tile] = r_ref[:, lanes(tile)].astype(F32)
        lane = lax.broadcasted_iota(jnp.int32, (8, NLAT), 1)
        quad[...] = jnp.sin(theta_of(lane)) * (math.pi / NLAT)

    lane32 = lax.broadcasted_iota(jnp.int32, (BANDS, group), 1) >> 5

    def exchanged(blocks):
        out = []
        for to in range(4):
            block = blocks[to]
            for at in range(4):
                if at != to:
                    moved = pltpu.roll(blocks[at], (at - to) % 4 * CHANS, 1)
                    block = jnp.where(lane32 == at, moved, block)
            out.append(block)
        return out

    for part_pair in range(PAIRS):
        row = 4 * (step * PAIRS + part_pair)
        tiles = []
        for tile in range(3):
            parts = [
                rin[tile, pl.ds(row + part, BANDS, stride=2 * ORDERS), :] for part in range(4)
            ]
            tiles.append(jnp.concatenate(exchanged(parts), axis=0).T)
        data = jnp.concatenate(tiles, axis=1)
        data = (data * quad[:1, :]).astype(BF16)

        out = []
        for item in range(2):
            table = p_ref[2 * part_pair + item]
            coef = lax.dot_general(
                data[2 * CHANS * item : 2 * CHANS * (item + 1), :],
                table,
                (((1,), (1,)), ((), ())),
                preferred_element_type=F32,
            )
            real, imag = coef[:CHANS], coef[CHANS:]
            filtered = jnp.concatenate(
                [w_ref[0] * real - w_ref[1] * imag, w_ref[0] * imag + w_ref[1] * real], axis=0
            ).astype(BF16)
            out.append(jnp.dot(filtered, table, preferred_element_type=F32))
        synth = jnp.concatenate(out, axis=0)
        for tile in range(3):
            turned = synth[:, lanes(tile)].T
            blocks = exchanged([turned[BANDS * lat : BANDS * (lat + 1), :] for lat in range(4)])
            for part in range(4):
                sout[tile, pl.ds(row + part, BANDS, stride=2 * ORDERS), :] = blocks[part]

    @pl.when(step == pl.num_programs(0) - 1)
    def _():
        for tile in range(3):
            s_ref[:, lanes(tile)] = sout[tile].astype(BF16)


def spectral_filter(received, table, weights):
    same2 = lambda pair: (0, 0)
    return pl.pallas_call(
        filter_kernel,
        grid=(ORDERS // 2 // PAIRS,),
        out_shape=jax.ShapeDtypeStruct((PARTS, ROWS), BF16),
        in_specs=[
            pl.BlockSpec((PARTS, ROWS), same2),
            pl.BlockSpec((2 * PAIRS, LMAX, NLAT), lambda pair: (pair, 0, 0)),
            pl.BlockSpec((2, CHANS, LMAX), lambda pair: (0, 0, 0)),
        ],
        out_specs=pl.BlockSpec((PARTS, ROWS), same2),
        scratch_shapes=[
            pltpu.VMEM((3, PARTS, LANES), F32),
            pltpu.VMEM((3, PARTS, LANES), F32),
            pltpu.VMEM((8, NLAT), F32),
        ],
        compiler_params=params(),
        name="spectral_filter",
    )(received, table, weights)


def inverse_kernel(r_ref, t_ref, xr_ref, m_ref, spectra):
    row = lax.broadcasted_iota(jnp.int32, (PARTS, ROWS), 0)
    gained = jnp.where(row < 2, 1.0, 2.0) * r_ref[...].astype(F32)
    spectra[...] = gained.T.astype(BF16)

    def rows_of(step, carry):
        at = pl.ds(pl.multiple_of(step * BLOCK, BLOCK), BLOCK)
        smooth = jnp.dot(spectra[at, :], t_ref[...], preferred_element_type=F32)
        mixed = (xr_ref[at, :].astype(F32) + smooth).astype(BF16)
        for part in range(NLON // LONS):
            to = pl.ds(pl.multiple_of((step * 4 + part) * BLOCK, BLOCK), BLOCK)
            m_ref[to, :] = mixed[:, part * LONS : (part + 1) * LONS]
        return carry

    lax.fori_loop(0, BAND // LATS, rows_of, 0)


def inverse(returned, table, rows):
    return pl.pallas_call(
        inverse_kernel,
        out_shape=jax.ShapeDtypeStruct((MEMBERS * BLOCK, LONS), BF16),
        in_specs=[whole()] * 3,
        out_specs=whole(),
        scratch_shapes=[pltpu.VMEM((ROWS, PARTS), BF16)],
        compiler_params=params(),
        name="inverse_fourier",
    )(returned, table, rows)


def gelu(x):
    root = math.sqrt(2.0 / math.pi)
    half = 0.5 * x
    return half + half * jnp.tanh(x * (root + (root * 0.044715) * (x * x)))


def mlp_kernel(r_ref, w_ref, bias_ref, o_ref, points, act, w_out):
    step = pl.program_id(0)
    rows = w_ref.shape[0] * LANES

    @pl.when(step == 0)
    def _():
        blocks = r_ref[...].reshape(MEMBERS, BLOCK, LONS)
        for lat in range(LATS):
            points[:, lat * LONS : (lat + 1) * LONS] = blocks[
                :, lat * CHANS : (lat + 1) * CHANS, :
            ].reshape(FULL, LONS)

    w_in, bias = [], []
    for part in range(w_ref.shape[0]):
        block = w_ref[part]
        column = bias_ref[pl.ds(step * w_ref.shape[0] + part, 1), :]
        bias.append(jnp.broadcast_to(column, (LANES, LANES)).T)
        w_in.append(
            jnp.concatenate([block[LANES * tile : LANES * (tile + 1)] for tile in range(4)], axis=1)
        )
        at = pl.ds(pl.multiple_of((step * w_ref.shape[0] + part) * LANES, LANES), LANES)
        w_out[:, at] = block[FULL:]
    w_in = jnp.concatenate(w_in, axis=0)
    bias = jnp.concatenate([jnp.concatenate(bias, axis=0)] * (LONS // LANES), axis=1)
    at = pl.ds(pl.multiple_of(step * rows, rows), rows)
    for lat in range(LATS):
        cols = slice(lat * LONS, (lat + 1) * LONS)
        pre = jnp.dot(w_in, points[:, cols], preferred_element_type=F32) + bias
        act[at, cols] = gelu(pre).astype(BF16)

    @pl.when(step == pl.num_programs(0) - 1)
    def _():
        for lat in range(LATS):
            cols = slice(lat * LONS, (lat + 1) * LONS)
            branch = jnp.dot(w_out[...], act[:, cols], preferred_element_type=F32)
            out = (points[:, cols].astype(F32) + branch).astype(BF16)
            for member in range(MEMBERS):
                to = member * BLOCK + lat * CHANS
                o_ref[to : to + CHANS, :] = out[member * CHANS : (member + 1) * CHANS, :]


def mlp(received, weights, bias):
    blocks = weights.shape[0]
    take = 8
    same2 = lambda step: (0, 0)
    return pl.pallas_call(
        mlp_kernel,
        grid=(blocks // take,),
        out_shape=jax.ShapeDtypeStruct((MEMBERS * BLOCK, LONS), BF16),
        in_specs=[
            pl.BlockSpec((MEMBERS * BLOCK, LONS), same2),
            pl.BlockSpec((take, 2 * FULL, LANES), lambda step: (step, 0, 0)),
            pl.BlockSpec((blocks, LANES), same2),
        ],
        out_specs=pl.BlockSpec((MEMBERS * BLOCK, LONS), same2),
        scratch_shapes=[
            pltpu.VMEM((FULL, POINTS), BF16),
            pltpu.VMEM((HID, POINTS), BF16),
            pltpu.VMEM((FULL, HID), BF16),
        ],
        compiler_params=params(),
        name="pointwise_mlp",
    )(received, weights, bias)


def home_kernel(r_ref, o_ref):
    for member in range(MEMBERS):
        lat, part = member // 4, member % 4
        o_ref[lat * BLOCK : (lat + 1) * BLOCK, part * LONS : (part + 1) * LONS] = r_ref[
            member * BLOCK : (member + 1) * BLOCK, :
        ]


def home(received):
    return pl.pallas_call(
        home_kernel,
        out_shape=jax.ShapeDtypeStruct((ROWS, NLON), BF16),
        in_specs=[whole()],
        out_specs=whole(),
        compiler_params=params(),
        name="home_layout",
    )(received)


def gather_first(proj_in, proj_out):
    column = [[xy * 32 + place for place in range(32)] for xy in range(16)]
    both = jnp.concatenate([proj_in, proj_out], axis=0)
    return lax.all_gather(both, ("spatial", "field"), axis=0, axis_index_groups=column, tiled=True)


def gather_second(column):
    split = column.reshape(32, 2, HID // FULL, FULL)
    w_in = split[:, 0].reshape(LANES, 4, LANES).transpose(1, 0, 2).reshape(FULL, LANES)
    w_out = split[:, 1].reshape(LANES, FULL).T
    block = jnp.concatenate([w_in, w_out], axis=0)
    planes = [[xy * 2 + high for xy in range(16)] for high in range(2)]
    whole_weights = lax.all_gather(block, "spatial", axis=0, axis_index_groups=planes, tiled=True)
    return whole_weights.reshape(16, 2 * FULL, LANES)


def shards(field_in, spectral_weight, proj_in, bias_in, proj_out):
    column = gather_first(proj_in, proj_out)
    bias = bias_in.reshape(16, 16, 2, 4).transpose(1, 2, 0, 3).reshape(16, LANES)
    rows = field_in.transpose(1, 0, 2).reshape(ROWS, NLON)
    spectrum, table = forward(rows)
    spectrum, column = lax.optimization_barrier((spectrum, column))
    weights = gather_second(column)
    pencil = lax.all_to_all(
        spectrum.reshape(BANDS, 2 * ORDERS, ROWS), "spatial", split_axis=0, concat_axis=0, tiled=True
    )
    first = (lax.axis_index("spatial") * ORDERS).astype(jnp.int32).reshape(1)
    polar, bias = legendre(first, bias)
    synth = spectral_filter(pencil.reshape(PARTS, ROWS), polar, spectral_weight)
    returned = lax.all_to_all(
        synth.reshape(BANDS, 2 * ORDERS, ROWS), "spatial", split_axis=0, concat_axis=0, tiled=True
    )
    mixed = inverse(returned.reshape(PARTS, ROWS), table, rows)
    points = lax.all_to_all(
        mixed.reshape(MEMBERS, BLOCK, LONS), "field", split_axis=0, concat_axis=0, tiled=True
    )
    result = mlp(points.reshape(MEMBERS * BLOCK, LONS), weights, bias)
    homed = lax.all_to_all(
        result.reshape(MEMBERS, BLOCK, LONS), "field", split_axis=0, concat_axis=0, tiled=True
    )
    return home(homed.reshape(MEMBERS * BLOCK, LONS)).reshape(BAND, CHANS, NLON).transpose(1, 0, 2)


def solution(mesh):
    in_specs = (
        P("field", "spatial", None),
        P(None, "field", None),
        P(("field", "spatial"), None),
        P(),
        P(("field", "spatial"), None),
    )
    out_specs = P("field", "spatial", None)
    return jax.shard_map(shards, mesh=mesh, in_specs=in_specs, out_specs=out_specs, check_vma=False)
```
